32 devices in a mesh: batch: 4 (over y, x), strip: 8 (over z, core).
Axes of the slice: x: 2, y: 2, z: 4, core: 2. Of those that a mesh axis runs over, the one named last changes fastest.
Arguments:
- camera_features: bfloat16 [4, 16896, 256], P('batch', 'strip'), may hold values from -6 to 6
- lidar_bev: bfloat16 [4, 48, 180, 256], P('batch', 'strip'), may hold values from -6 to 6
- pool_index: int32 [4, 16896, 118], P('batch', 'strip'), may hold values from 0 to 8639, as said below
- box_peaks: int32 [4, 3, 150], P('batch'), may hold values from 0 to 179, as said below
- box_count: int32 [4], P('batch'), may hold values from 1 to 150
- w_depth: float32 [256, 198], replicated, may hold values from -1 to 1
- m_depth: float32 [256, 198], replicated, may hold values from -7.6293945e-05 to 7.6293945e-05
- v_depth: float32 [256, 198], replicated, may hold values from 9.864268e-13 to 1.5782828e-11
- w_join: float32 [3, 3, 336, 256], P(None, None, None, 'strip'), may hold values from -0.109375 to 0.109375
- m_join: float32 [3, 3, 336, 256], P(None, None, None, 'strip'), may hold values from -1.9073486e-05 to 1.9073486e-05
- v_join: float32 [3, 3, 336, 256], P(None, None, None, 'strip'), may hold values from 6.458747e-14 to 1.0333995e-12
- w_res: float32 [3, 3, 256, 256], P(None, None, None, 'strip'), may hold values from -0.125 to 0.125
- m_res: float32 [3, 3, 256, 256], P(None, None, None, 'strip'), may hold values from -2.2888184e-05 to 2.2888184e-05
- v_res: float32 [3, 3, 256, 256], P(None, None, None, 'strip'), may hold values from 8.477105e-14 to 1.3563368e-12
- w_head: float32 [256, 10], replicated, may hold values from -0.375 to 0.375
- m_head: float32 [256, 10], replicated, may hold values from -0.00030517578 to 0.00030517578
- v_head: float32 [256, 10], replicated, may hold values from 1.953125e-11 to 3.125e-10
- norm_params: float32 [4, 256], replicated, may hold values from 0.25 to 1.75
- m_norm: float32 [4, 256], replicated, may hold values from -0.00048828125 to 0.00048828125
- v_norm: float32 [4, 256], replicated, may hold values from 4.8828126e-11 to 7.8125e-10
- head_bias: float32 [10], replicated, may hold values from -2.5 to -1.5
- m_bias: float32 [10], replicated, may hold values from -0.0048828125 to 0.0048828125
- v_bias: float32 [10], replicated, may hold values from 5e-09 to 8e-08
Outputs:
- loss: float32 [1], replicated
- grad_norms: float32 [6], replicated
- new_w_depth: float32 [256, 198], replicated
- new_m_depth: float32 [256, 198], replicated
- new_v_depth: float32 [256, 198], replicated
- new_w_join: float32 [3, 3, 336, 256], P(None, None, None, 'strip')
- new_m_join: float32 [3, 3, 336, 256], P(None, None, None, 'strip')
- new_v_join: float32 [3, 3, 336, 256], P(None, None, None, 'strip')
- new_w_res: float32 [3, 3, 256, 256], P(None, None, None, 'strip')
- new_m_res: float32 [3, 3, 256, 256], P(None, None, None, 'strip')
- new_v_res: float32 [3, 3, 256, 256], P(None, None, None, 'strip')
- new_w_head: float32 [256, 10], replicated
- new_m_head: float32 [256, 10], replicated
- new_v_head: float32 [256, 10], replicated
- new_norm: float32 [4, 256], replicated
- new_m_norm: float32 [4, 256], replicated
- new_v_norm: float32 [4, 256], replicated
- new_bias: float32 [10], replicated
- new_m_bias: float32 [10], replicated
- new_v_bias: float32 [10], replicated
The draws below stay inside these ranges and needn't reach their ends.
Inputs may be any that keep to these rules, and one draw needn't show every extreme that they name: `pool_index`: cell = row * 180 + column of one sample's grid; rows near the middle of the grid are named more often. `box_peaks`: per slot: row below 48, column below 180, class below 10.
All inputs are finite; a program needn't handle non-finite values.
Results may differ from the reference program's by a relative error of at most 0.015.
Values may be sent and summed in bfloat16 or wider, within the bound.
No kernel may reach another device: no remote copies, remote signals or barrier semaphores. Data moves between devices by JAX's collectives and lax.ppermute only.
A program may use at most 192 MiB of HBM per device.

```python
import math
import jax
import jax.numpy as jnp
from jax import lax

W = 180
LIDAR = 256
CAM = 80
CAMF = 256
DEPTH = 118
HID = 256
NCLS = 10
BOXES = 150
STEP = 5
SAMPLES = 4
ROWS = 48
PIX = 16896


def draw_pool_index(key, part):
    key_ahead, key_behind, key_column = jax.random.split(key, 3)
    shape = (SAMPLES, PIX, DEPTH)
    middle = ROWS // 2
    ahead = jax.random.randint(key_ahead, shape, 0, middle)
    behind = jax.random.randint(key_behind, shape, 0, middle + 1)
    column = jax.random.randint(key_column, shape, 0, W)
    return ((middle + ahead - behind) * W + column).astype(jnp.int32)


def draw_box_peaks(key, part):
    key_row, key_column, key_class = jax.random.split(key, 3)
    shape = (SAMPLES, BOXES)
    row_ids = jax.random.randint(key_row, shape, 0, ROWS)
    col_ids = jax.random.randint(key_column, shape, 0, W)
    class_ids = jax.random.randint(key_class, shape, 0, NCLS)
    return jnp.stack([row_ids, col_ids, class_ids], axis=1).astype(jnp.int32)


def plant(values, rng, low, largest):
    longest = values.shape.index(max(values.shape))
    spots = []
    for shift in (0, 1):
        where = [jax.random.randint(jax.random.fold_in(rng, axis), (), 0, length) for axis, length in enumerate(values.shape)]
        where[longest] = (where[longest] + shift) % values.shape[longest]
        spots.append(tuple(where))
    return values.at[spots[0]].set(low).at[spots[1]].set(largest)


def block_levels(own_key, shape, shards, smallest, top_value):
    level = 1.0
    for dim, blocks in shards:
        draws = jax.random.uniform(jax.random.fold_in(jax.random.fold_in(own_key, 6), dim), (blocks,), jnp.float32, smallest / len(shards), top_value / len(shards))
        level = level * jnp.repeat(jnp.exp(draws), shape[dim] // blocks).reshape((-1,) + (1,) * (len(shape) - 1 - dim))
    return level


def centred(own_key, shape, scale, reach, shards=(), kind=jnp.bfloat16):
    values = jax.random.normal(own_key, shape, jnp.float32) * scale
    if len(shards) > 0:
        values = block_levels(own_key, shape, shards, -0.22, 0.18) * values
    return jnp.clip(values, min=-reach, max=reach).astype(kind)


def setup_inputs(seed: int = 0) -> dict:
    splits = jax.random.split(jax.random.key(seed), 24)
    camera_features = centred(splits[0], (SAMPLES, PIX, CAMF), 1.0, 6.0, ((0, 4), (1, 8)))
    lidar_bev = centred(splits[1], (SAMPLES, ROWS, W, LIDAR), 1.0, 6.0, ((0, 4), (1, 8)))
    pool_index = draw_pool_index(jax.random.fold_in(splits[23], 71), 0)
    box_peaks = draw_box_peaks(jax.random.fold_in(splits[23], 71), 0)
    box_count = plant(jax.random.randint(splits[4], (SAMPLES,), 1, BOXES + 1), jax.random.fold_in(splits[4], 1), 1, BOXES).astype(jnp.int32)
    w_depth = centred(splits[5], (CAMF, DEPTH + CAM), (CAMF / 9) ** -0.5, 1.0, (), jnp.float32)
    m_depth = centred(splits[6], (CAMF, DEPTH + CAM), (0.00111 / (CAMF * (DEPTH + CAM)) ** 0.5), 7.62939453125e-05, (), jnp.float32)
    v_depth = jnp.clip(jnp.exp(jax.random.uniform(splits[7], (CAMF, DEPTH + CAM), jnp.float32, math.log(9.86426760586634e-13), math.log(1.5782828169386143e-11))), 9.86426760586634e-13, 1.5782828169386143e-11)
    w_join = centred(splits[8], (3, 3, LIDAR + CAM, HID), (9 * (LIDAR + CAM)) ** -0.5, 0.109375, ((3, 8),), jnp.float32)
    m_join = centred(splits[9], (3, 3, LIDAR + CAM, HID), (0.00111 / (9 * (LIDAR + CAM) * HID) ** 0.5), 1.9073486328125e-05, ((3, 8),), jnp.float32)
    v_join = jnp.clip(jnp.exp(math.log(1.0333994944489167e-12) - 2.7725887 * jax.random.uniform(splits[10], (3, 3, LIDAR + CAM, HID), jnp.float32) ** block_levels(splits[10], (3, 3, LIDAR + CAM, HID), ((3, 8),), -0.2, 0.2)), 6.458746840305729e-14, 1.0333994944489167e-12)
    w_res = centred(splits[11], (3, 3, HID, HID), (9 * HID) ** -0.5, 0.125, ((3, 8),), jnp.float32)
    m_res = centred(splits[12], (3, 3, HID, HID), (0.00111 / (9 * HID * HID) ** 0.5), 2.288818359375e-05, ((3, 8),), jnp.float32)
    v_res = jnp.clip(jnp.exp(math.log(1.3563368093591488e-12) - 2.7725887 * jax.random.uniform(splits[13], (3, 3, HID, HID), jnp.float32) ** block_levels(splits[13], (3, 3, HID, HID), ((3, 8),), -0.2, 0.2)), 8.47710505849468e-14, 1.3563368093591488e-12)
    w_head = centred(splits[14], (HID, NCLS), HID ** -0.5, 0.375, (), jnp.float32)
    m_head = centred(splits[15], (HID, NCLS), (0.00111 / (HID * NCLS) ** 0.5), 0.00030517578, (), jnp.float32)
    v_head = jnp.clip(jnp.exp(jax.random.uniform(splits[16], (HID, NCLS), jnp.float32, math.log(1.9531249881299395e-11), math.log(3.124999981007903e-10))), 1.9531249881299395e-11, 3.124999981007903e-10)
    norm_params = jnp.clip(1.0 + 0.15 * jax.random.normal(splits[17], (4, HID), jnp.float32), 0.25, 1.75)
    m_norm = centred(splits[18], (4, HID), (0.00111 / (4 * HID) ** 0.5), 0.00048828125, (), jnp.float32)
    v_norm = jnp.clip(jnp.exp(jax.random.uniform(splits[19], (4, HID), jnp.float32, math.log(4.8828125570610226e-11), math.log(7.812500091297636e-10))), 4.8828125570610226e-11, 7.812500091297636e-10)
    head_bias = jnp.clip(jax.random.uniform(splits[20], (NCLS,), jnp.float32, -2.5, -1.5), -2.5, -1.5)
    m_bias = centred(splits[21], (NCLS,), (0.00111 / NCLS ** 0.5), 0.0048828125, (), jnp.float32)
    v_bias = jnp.clip(jnp.exp(jax.random.uniform(splits[22], (NCLS,), jnp.float32, math.log(4.999999969612645e-09), math.log(7.999999951380232e-08))), 4.999999969612645e-09, 7.999999951380232e-08)
    return dict(camera_features=camera_features, lidar_bev=lidar_bev, pool_index=pool_index, box_peaks=box_peaks, box_count=box_count, w_depth=w_depth, m_depth=m_depth, v_depth=v_depth, w_join=w_join, m_join=m_join, v_join=v_join, w_res=w_res, m_res=m_res, v_res=v_res, w_head=w_head, m_head=m_head, v_head=v_head, norm_params=norm_params, m_norm=m_norm, v_norm=v_norm, head_bias=head_bias, m_bias=m_bias, v_bias=v_bias)


@jax.custom_vjp
def low(v):
    return lax.optimization_barrier(v.astype(jnp.bfloat16)).astype(jnp.float32)

@jax.custom_vjp
def low_back(v):
    return v

def low_keep(v):
    return (low(v), None)

def low_pass(kept, grad):
    return (grad,)

def back_keep(v):
    return (v, None)

def back_low(kept, grad):
    return (low(grad),)
low.defvjp(low_keep, low_pass)
low_back.defvjp(back_keep, back_low)
HIGHEST = lax.Precision.HIGHEST
EPS_NORM = 1e-05
SPREAD_TWICE = 8.0
SMALL_RATE = 0.25
CLIP_NORM = 0.01

def targets(box_peaks, box_count, first_row, row_total, col_total, classes):
    row_ids = first_row + jnp.arange(row_total, dtype=jnp.int32)
    col_ids = jnp.arange(col_total, dtype=jnp.int32)
    slots = box_peaks.shape[2]
    alive = jnp.arange(slots, dtype=jnp.int32)[None, :] < box_count[:, None]
    row_gap = row_ids[None, :, None] - box_peaks[:, 0][:, None, :]
    col_gap = col_ids[None, :, None] - box_peaks[:, 1][:, None, :]
    distance = (row_gap * row_gap)[:, :, None, :] + (col_gap * col_gap)[:, None, :, :]
    member = (box_peaks[:, 2][:, :, None] == jnp.arange(classes, dtype=jnp.int32)) & alive[:, :, None]
    gaussian = jnp.exp(-distance.astype(jnp.float32) / SPREAD_TWICE)
    heatmap = lax.optimization_barrier(jnp.max(jnp.where(member[:, None, None], gaussian[..., None], jnp.float32(0.0)), axis=3))
    struck = jnp.any(member[:, None, None] & (distance == 0)[..., None], axis=3)
    return (heatmap, struck.astype(jnp.float32))

def batch_norm(values, gain, shift):
    center = lax.optimization_barrier(jnp.mean(values, axis=(0, 1, 2)))
    spread = lax.optimization_barrier(jnp.mean((values - center) ** 2, axis=(0, 1, 2)))
    return (values - center) * lax.rsqrt(spread + EPS_NORM) * gain + shift

def convolve(inputs, kernel):
    return lax.conv_general_dilated(inputs, kernel, (1, 1), ((1, 1), (1, 1)), dimension_numbers=('NHWC', 'HWIO', 'NHWC'), precision=HIGHEST)

def adamw(weight, gradient, first, second, rate, step_value):
    first = 0.9 * first + 0.1 * gradient
    second = 0.999 * second + 0.001 * gradient * gradient
    fix_one = 1.0 - jnp.power(jnp.float32(0.9), step_value)
    fix_two = 1.0 - jnp.power(jnp.float32(0.999), step_value)
    update = first / fix_one / (jnp.sqrt(second / fix_two) + 1e-08) + 0.01 * weight
    return (weight - rate * update, first, second)

def reference(camera_features, lidar_bev, pool_index, box_peaks, box_count, w_depth, m_depth, v_depth, w_join, m_join, v_join, w_res, m_res, v_res, w_head, m_head, v_head, norm_params, m_norm, v_norm, head_bias, m_bias, v_bias):
    features = camera_features.astype(jnp.float32)
    lidar = lidar_bev.astype(jnp.float32)

    def one_target(pair):
        peaks, count = pair
        heat_one, struck_one = targets(peaks[None], count[None], 0, ROWS, W, NCLS)
        return (heat_one[0], struck_one[0])
    heatmap, struck = lax.map(one_target, (box_peaks, box_count))
    positives = jnp.sum(struck)

    def forward(w_depth, w_join, w_res, w_head, norm_params, head_bias):

        def lift(pair):
            feature, index = pair
            logits = low_back(jnp.dot(feature, low(w_depth), precision=HIGHEST))
            depth = jax.nn.softmax(logits[:, :DEPTH], axis=-1)
            context = logits[:, DEPTH:]
            values = depth[:, :, None] * context[:, None, :]
            return jax.ops.segment_sum(values.reshape(-1, CAM), index.reshape(-1), num_segments=ROWS * W)
        pooled = lax.map(jax.checkpoint(lift), (features, pool_index))
        camera = low(low_back(pooled)).reshape(SAMPLES, ROWS, W, CAM)
        joined = jnp.concatenate([camera, lidar], axis=-1)
        join_out = low_back(convolve(joined, low(w_join)))
        act_one = low(jax.nn.silu(batch_norm(join_out, norm_params[0], norm_params[1])))
        res_out = low_back(convolve(act_one, low(w_res)))
        summed = batch_norm(res_out, norm_params[2], norm_params[3]) + act_one
        hidden = low(jax.nn.silu(summed))
        logits = low_back(jnp.einsum('srwc,ck->srwk', hidden, low(w_head), precision=HIGHEST) + head_bias)
        prob = jax.nn.sigmoid(logits)
        pos_term = struck * (1.0 - prob) ** 2 * jax.nn.softplus(-logits)
        neg_term = (1.0 - heatmap) ** 4 * prob ** 2 * jax.nn.softplus(logits)
        return jnp.sum(pos_term + neg_term) / positives
    params = (w_depth, w_join, w_res, w_head, norm_params, head_bias)
    loss, pull = jax.vjp(forward, *params)
    grads = pull(jnp.ones_like(loss))
    norms = [jnp.sqrt(jnp.sum(gradient * gradient)) for gradient in grads]
    clipped = [gradient * (CLIP_NORM / jnp.maximum(norm_value, CLIP_NORM)) for gradient, norm_value in zip(grads, norms)]
    step_value = jnp.float32(STEP)
    rates = (0.5 * CAMF ** (-0.5), 0.5 * (9 * (LIDAR + CAM)) ** (-0.5), 0.5 * (9 * HID) ** (-0.5), 0.5 * HID ** (-0.5), SMALL_RATE, SMALL_RATE)
    firsts = (m_depth, m_join, m_res, m_head, m_norm, m_bias)
    seconds = (v_depth, v_join, v_res, v_head, v_norm, v_bias)
    result = [jnp.reshape(loss, (1,)), jnp.log(jnp.stack(norms))]
    for weight, gradient, first, second, rate in zip(params, clipped, firsts, seconds, rates):
        result.extend(adamw(weight, gradient, first, second, rate, step_value))
    return tuple(result)
```

```python
import functools

import jax
import jax.numpy as jnp
from jax import lax
from jax.experimental import pallas as pl
from jax.experimental.pallas import tpu as pltpu
from jax.sharding import PartitionSpec as P

STEP = 5


EPS_NORM = 1e-05
SPREAD_TWICE = 8.0
SMALL_RATE = 0.25
CLIP_NORM = 0.01


def extended(shard, sides, width):
    for axis, dim in sides:
        peers, length = (lax.axis_size(axis), shard.shape[dim])
        up = [(i, (i + 1) % peers) for i in range(peers - 1)]
        down = [(j, i) for i, j in up]
        last = lax.slice_in_dim(shard, length - width, length, axis=dim)
        leading = lax.slice_in_dim(shard, 0, width, axis=dim)
        before = lax.ppermute(last, axis, up)
        after = lax.ppermute(leading, axis, down)
        shard = jnp.concatenate([before, shard, after], axis=dim)
    return shard


def targets(box_peaks, box_count, first_row, row_total, col_total, classes):
    row_ids = first_row + jnp.arange(row_total, dtype=jnp.int32)
    col_ids = jnp.arange(col_total, dtype=jnp.int32)
    slots = box_peaks.shape[2]
    alive = jnp.arange(slots, dtype=jnp.int32)[None, :] < box_count[:, None]
    row_gap = row_ids[None, :, None] - box_peaks[:, 0][:, None, :]
    col_gap = col_ids[None, :, None] - box_peaks[:, 1][:, None, :]
    distance = (row_gap * row_gap)[:, :, None, :] + (col_gap * col_gap)[:, None, :, :]
    member = (box_peaks[:, 2][:, :, None] == jnp.arange(classes, dtype=jnp.int32)) & alive[
        :, :, None
    ]
    gaussian = jnp.exp(-distance.astype(jnp.float32) / SPREAD_TWICE)
    heatmap = jnp.max(
        jnp.where(member[:, None, None], gaussian[..., None], jnp.float32(0.0)), axis=3
    )
    struck = jnp.any(member[:, None, None] & (distance == 0)[..., None], axis=3)
    return (heatmap, struck.astype(jnp.float32))


def rims(tensor):
    padded = extended(tensor, (("strip", 1),), 1)
    return jnp.pad(padded, ((0, 0), (0, 0), (1, 1), (0, 0)))


def rims_back(tensor):
    padded = extended(tensor, (("strip", 1),), 1)
    return jnp.pad(padded, ((0, 0), (0, 0), (1, 1), (0, 0)))


def conv_taps(padded, kernel, row_total, col_total):
    total = jnp.zeros((padded.shape[0], row_total, col_total, kernel.shape[3]), jnp.float32)
    for upward in range(3):
        for across in range(3):
            window = padded[:, upward : upward + row_total, across : across + col_total]
            total = total + jnp.einsum(
                "brwc,ch->brwh", window, kernel[upward, across], preferred_element_type=jnp.float32
            )
    return total


def kernel_taps(padded, grad_out):
    row_total, col_total = (grad_out.shape[1], grad_out.shape[2])
    pieces = []
    for upward in range(3):
        for across in range(3):
            window = padded[:, upward : upward + row_total, across : across + col_total]
            pieces.append(
                jnp.einsum("brwc,brwh->ch", window, grad_out, preferred_element_type=jnp.float32)
            )
    return jnp.stack(pieces).reshape((3, 3) + pieces[0].shape)


def flipped(kernel):
    return jnp.transpose(kernel, (0, 1, 3, 2))[::-1, ::-1]


LANES = 128
BF = jnp.bfloat16
F32 = jnp.float32


def plan(pixels, strips, strip_cells):
    per_strip = -(-strip_cells // LANES)
    high = strips * per_strip
    block = 176 if high <= 128 else 48
    return dict(
        per_strip=per_strip,
        high=high,
        high_pad=-(-high // 16) * 16,
        offset=high // 2,
        block=block,
        stride=block + 4,
        group=block // 4,
        strip_cells=strip_cells,
    )


def split_cells(index, plan):
    cell = index.astype(F32)
    strip = jnp.floor((cell + 0.5) * (1.0 / plan["strip_cells"]))
    rest = cell - strip * plan["strip_cells"]
    part = jnp.floor((rest + 0.5) * (1.0 / LANES))
    return strip * plan["per_strip"] + part - plan["offset"], rest - part * LANES


def softmax_lanes(logits, bins):
    lane = lax.broadcasted_iota(jnp.int32, logits.shape, 1)
    logits = jnp.where(lane < bins, logits, -jnp.inf)
    powers = jnp.exp(logits - jnp.max(logits, axis=1, keepdims=True))
    return powers / jnp.sum(powers, axis=1, keepdims=True)


def spread(ref, pixel):
    return jnp.broadcast_to(ref[pl.ds(pixel, 1), :], (16, LANES)).astype(BF)


def one_hot(row, value, rows, offset=0):
    base = (lax.broadcasted_iota(jnp.int32, (rows, LANES), 0) - offset).astype(F32).astype(BF)
    none = jnp.zeros((16, LANES), BF)
    return [
        jnp.where(base[k : k + 16] == row, value, none) for k in range(0, rows, 16)
    ]


def pool_kernel(feat_ref, index_ref, bins_ref, context_ref, pooled_ref, dense_ref, high_ref, low_ref, depth_ref, held, total, *, plan):
    bins = index_ref.shape[1]
    block, stride, high, high_pad = (plan[k] for k in ("block", "stride", "high", "high_pad"))
    step = pl.program_id(0)

    @pl.when(step == 0)
    def _():
        high_ref[...] = jnp.zeros_like(high_ref)
        low_ref[...] = jnp.zeros_like(low_ref)
        total[...] = jnp.zeros_like(total)

    feat = feat_ref[...]
    depth_ref[...] = softmax_lanes(jnp.dot(feat, bins_ref[...], preferred_element_type=F32), bins)
    context = lax.dot_general(context_ref[...], feat, (((1,), (1,)), ((), ())), preferred_element_type=F32).astype(BF)
    high_id, low_id = split_cells(index_ref[...], plan)
    high_ref[:, :bins] = high_id
    low_ref[:, :bins] = low_id
    one = jnp.ones((16, LANES), BF)

    def scatter(group, carry):
        for k in range(0, plan["group"], 2):
            first = group * plan["group"] + k
            left, right = [], []
            for j in range(2):
                left += one_hot(spread(high_ref, first + j), spread(depth_ref, first + j), high_pad, plan["offset"])
                right += one_hot(spread(low_ref, first + j), one, LANES)
            tile = lax.dot_general(jnp.concatenate(left, 0), jnp.concatenate(right, 0), (((1,), (1,)), ((), ())), preferred_element_type=F32)
            for j in range(2):
                held[pl.ds(first + j, high, stride=stride), :] = tile[j * high_pad : j * high_pad + high, j * LANES : (j + 1) * LANES]
        return carry

    lax.fori_loop(0, block // plan["group"], scatter, 0)

    def gather(k, carry):
        parts = []
        for j in range(2):
            part = held[pl.ds((k * 2 + j) * stride, block), :].astype(BF)
            dense_ref[k * 2 + j] = part
            parts.append(part)
        out = jnp.dot(context, jnp.concatenate(parts, 1), preferred_element_type=F32)
        for j in range(2):
            total[k * 2 + j] += out[:, j * LANES : (j + 1) * LANES]
        return carry

    lax.fori_loop(0, high // 2, gather, 0, unroll=2)

    @pl.when(step == pl.num_programs(0) - 1)
    def _():
        pooled_ref[...] = total[...].astype(BF)


def pool(features, index, bins_low, context_low, plan):
    pixels, width = features.shape
    bins = index.shape[1]
    channels = context_low.shape[0]
    block, high = plan["block"], plan["high"]
    return pl.pallas_call(
        functools.partial(pool_kernel, plan=plan),
        grid=(pixels // block,),
        in_specs=[
            pl.BlockSpec((block, width), lambda i: (i, 0)),
            pl.BlockSpec((block, bins), lambda i: (i, 0)),
            pl.BlockSpec(bins_low.shape, lambda i: (0, 0)),
            pl.BlockSpec(context_low.shape, lambda i: (0, 0)),
        ],
        out_specs=[
            pl.BlockSpec((high, channels, LANES), lambda i: (0, 0, 0)),
            pl.BlockSpec((high, block, LANES), lambda i: (0, i, 0)),
        ],
        out_shape=[
            jax.ShapeDtypeStruct((high, channels, LANES), BF),
            jax.ShapeDtypeStruct((high, pixels, LANES), BF),
        ],
        scratch_shapes=[pltpu.VMEM((block, LANES), F32)] * 3
        + [
            pltpu.VMEM((plan["high_pad"] * plan["stride"], LANES), F32),
            pltpu.VMEM((high, channels, LANES), F32),
        ],
        compiler_params=pltpu.CompilerParams(vmem_limit_bytes=60 << 20),
        name="pool",
    )(features, index, bins_low, context_low)


def unpool_kernel(feat_ref, index_ref, both_ref, dense_ref, grid_ref, grad_ref, high_ref, low_ref, pick_ref, held, *, plan):
    bins = index_ref.shape[1]
    channels = grid_ref.shape[2]
    block, stride, high, high_pad = (plan[k] for k in ("block", "stride", "high", "high_pad"))
    step = pl.program_id(0)

    @pl.when(step == 0)
    def _():
        high_ref[...] = jnp.zeros_like(high_ref)
        low_ref[...] = jnp.zeros_like(low_ref)
        held[...] = jnp.zeros_like(held)
        grad_ref[...] = jnp.zeros_like(grad_ref)

    feat = feat_ref[...]
    logits = jnp.dot(feat, both_ref[...], preferred_element_type=F32)
    depth = softmax_lanes(logits[:, :LANES], bins)
    context = logits[:, LANES : LANES + channels].astype(BF)
    high_id, low_id = split_cells(index_ref[...], plan)
    high_ref[:, :bins] = high_id
    low_ref[:, :bins] = low_id

    def project(k, carry):
        grid = grid_ref[pl.ds(k * 2, 2)].reshape(2 * LANES, channels)
        out = lax.dot_general(context, grid, (((1,), (1,)), ((), ())), preferred_element_type=F32)
        for j in range(2):
            held[pl.ds((k * 2 + j) * stride, block), :] = out[:, j * LANES : (j + 1) * LANES]
        parts = [dense_ref[k * 2 + j] for j in range(2)]
        return carry + jnp.dot(jnp.concatenate(parts, 1), grid, preferred_element_type=F32)

    grad_context = lax.fori_loop(0, high // 2, project, jnp.zeros((block, channels), F32), unroll=2)
    one = jnp.ones((16, LANES), BF)
    rows = (lax.broadcasted_iota(jnp.int32, (high, LANES), 0) - plan["offset"]).astype(F32)

    def collect(group, carry):
        for k in range(0, plan["group"], 2):
            first = group * plan["group"] + k
            left, right = [], []
            for j in range(2):
                left.append(held[pl.ds(first + j, high_pad, stride=stride), :].astype(BF))
                right.append(jnp.concatenate(one_hot(spread(low_ref, first + j), one, LANES), 0))
            tile = jnp.dot(jnp.concatenate(left, 0), jnp.concatenate(right, 1), preferred_element_type=F32)
            for j in range(2):
                part = tile[j * high_pad : j * high_pad + high, j * LANES : (j + 1) * LANES]
                kept = jnp.where(rows == high_ref[pl.ds(first + j, 1), :], part, 0.0)
                pick_ref[pl.ds(first + j, 1), :] = jnp.sum(kept, axis=0, keepdims=True)
        return carry

    lax.fori_loop(0, block // plan["group"], collect, 0)
    grad_prob = pick_ref[...]
    grad_depth = depth * (grad_prob - jnp.sum(grad_prob * depth, axis=1, keepdims=True))
    grad_low = jnp.concatenate(
        [grad_depth, grad_context, jnp.zeros((block, LANES - channels), F32)], axis=1
    ).astype(BF)
    grad_ref[...] += lax.dot_general(feat, grad_low, (((0,), (0,)), ((), ())), preferred_element_type=F32)


def unpool(features, index, both_low, dense, grid, plan):
    pixels, width = features.shape
    bins = index.shape[1]
    channels = grid.shape[2]
    block, high = plan["block"], plan["high"]
    return pl.pallas_call(
        functools.partial(unpool_kernel, plan=plan),
        grid=(pixels // block,),
        in_specs=[
            pl.BlockSpec((block, width), lambda i: (i, 0)),
            pl.BlockSpec((block, bins), lambda i: (i, 0)),
            pl.BlockSpec(both_low.shape, lambda i: (0, 0)),
            pl.BlockSpec((high, block, LANES), lambda i: (0, i, 0)),
            pl.BlockSpec(grid.shape, lambda i: (0, 0, 0)),
        ],
        out_specs=pl.BlockSpec((width, 2 * LANES), lambda i: (0, 0)),
        out_shape=jax.ShapeDtypeStruct((width, 2 * LANES), F32),
        scratch_shapes=[pltpu.VMEM((block, LANES), F32)] * 3
        + [pltpu.VMEM((plan["high_pad"] * plan["stride"], LANES), F32)],
        compiler_params=pltpu.CompilerParams(vmem_limit_bytes=60 << 20),
        name="unpool",
    )(features, index, both_low, dense, grid)


def everywhere(tensor):
    axes = ("batch", "strip")
    copies = jnp.broadcast_to(tensor[None], (lax.axis_size(axes),) + tensor.shape)
    return lax.all_to_all(copies, axes, 0, 0)


def summed_everywhere(tensor):
    return jnp.sum(everywhere(tensor), axis=0)


def moments(values, extra_term):
    cells = values.shape[0] * values.shape[1] * values.shape[2]
    center = jnp.sum(values, axis=(0, 1, 2)) / cells
    spread_sum = jnp.sum((values - center) ** 2, axis=(0, 1, 2))
    extra_row = jnp.full(center.shape, extra_term)
    shared = everywhere(jnp.stack([center, spread_sum, extra_row]))
    centers = shared[:, 0]
    total = jnp.mean(centers, axis=0)
    spread_mean = jnp.mean(shared[:, 1] / cells + (centers - total) ** 2, axis=0)
    return (total, lax.rsqrt(spread_mean + EPS_NORM), jnp.sum(shared[:, 2, 0]))


def norm_backward(grad_norm, normed, gain, scale_inv, cell_total):
    grad_shift, grad_gain = summed_everywhere(
        jnp.stack(
            [jnp.sum(grad_norm, axis=(0, 1, 2)), jnp.sum(grad_norm * normed, axis=(0, 1, 2))]
        )
    )
    grad_in = (
        gain * scale_inv * (grad_norm - grad_shift / cell_total - normed * grad_gain / cell_total)
    )
    return (grad_in, grad_gain, grad_shift)


def silu_slope(value):
    sig = jax.nn.sigmoid(value)
    return sig * (1.0 + value * (1.0 - sig))


def adamw(weight, gradient, first, second, rate, step_value):
    first = 0.9 * first + 0.1 * gradient
    second = 0.999 * second + 0.001 * gradient * gradient
    fix_one = 1.0 - jnp.power(jnp.float32(0.9), step_value)
    fix_two = 1.0 - jnp.power(jnp.float32(0.999), step_value)
    update = first / fix_one / (jnp.sqrt(second / fix_two) + 1e-08) + 0.01 * weight
    return (weight - rate * update, first, second)


def squares(tensor):
    return jnp.sum(tensor * tensor)


def shards(
    camera_features,
    lidar_bev,
    pool_index,
    box_peaks,
    box_count,
    w_depth,
    m_depth,
    v_depth,
    w_join,
    m_join,
    v_join,
    w_res,
    m_res,
    v_res,
    w_head,
    m_head,
    v_head,
    norm_params,
    m_norm,
    v_norm,
    head_bias,
    m_bias,
    v_bias,
):
    samples, row_local, col_total, lidar_width = lidar_bev.shape
    strips = lax.axis_size("strip")
    row_total = row_local * strips
    cell_total = float(samples * lax.axis_size("batch") * row_total * col_total)
    depth_bins = pool_index.shape[2]
    classes = w_head.shape[1]
    owned = w_join.shape[3]
    cam_width = w_depth.shape[1] - depth_bins
    first_row = lax.axis_index("strip") * row_local
    join_full, res_full = (
        lax.all_gather(w_join.astype(jnp.bfloat16), "strip", axis=3, tiled=True),
        lax.all_gather(w_res.astype(jnp.bfloat16), "strip", axis=3, tiled=True),
    )
    depth_low = w_depth.astype(jnp.bfloat16)
    head_low = w_head.astype(jnp.bfloat16)
    strip_cells = row_local * col_total
    layout = plan(camera_features.shape[1], strips, strip_cells)
    bins_low = jnp.pad(depth_low[:, :depth_bins], ((0, 0), (0, LANES - depth_bins)))
    context_low = depth_low[:, depth_bins:]
    term, dense = pool(camera_features[0], pool_index[0], bins_low, context_low.T, layout)
    pooled = lax.psum_scatter(term, "strip", scatter_dimension=0, tiled=True)
    pooled = jnp.transpose(pooled, (0, 2, 1)).reshape(-1, cam_width)[:strip_cells]
    pooled = pooled.reshape(samples, row_local, col_total, cam_width)
    joined = jnp.concatenate([pooled, lidar_bev], axis=-1)
    heatmap, struck = targets(box_peaks, box_count, first_row, row_local, col_total, classes)
    joined_pad = rims(joined)
    join_out = conv_taps(joined_pad, join_full, row_local, col_total)
    center_one, scale_one, positives = moments(join_out, jnp.sum(struck))
    normed_one = (join_out - center_one) * scale_one
    pre_one = normed_one * norm_params[0] + norm_params[1]
    act_one = jax.nn.silu(pre_one).astype(jnp.bfloat16)
    act_pad = rims(act_one)
    res_out = conv_taps(act_pad, res_full, row_local, col_total)
    center_two, scale_two, unused_term = moments(res_out, jnp.float32(0.0))
    normed_two = (res_out - center_two) * scale_two
    summed = normed_two * norm_params[2] + norm_params[3] + act_one.astype(jnp.float32)
    hidden = jax.nn.silu(summed).astype(jnp.bfloat16)
    logits = (
        jnp.einsum("brwh,hk->brwk", hidden, head_low, preferred_element_type=jnp.float32)
        + head_bias
    )
    prob = jax.nn.sigmoid(logits)
    soft_neg = jax.nn.softplus(-logits)
    soft_pos = jax.nn.softplus(logits)
    weighting = (1.0 - heatmap) ** 4
    local_loss = jnp.sum(struck * (1.0 - prob) ** 2 * soft_neg + weighting * prob**2 * soft_pos)
    grad_pos = -2.0 * prob * (1.0 - prob) ** 2 * soft_neg - (1.0 - prob) ** 3
    grad_neg = 2.0 * prob**2 * (1.0 - prob) * soft_pos + prob**3
    grad_logits = ((struck * grad_pos + weighting * grad_neg) / positives).astype(jnp.bfloat16)
    grad_head = jnp.einsum("brwh,brwk->hk", hidden, grad_logits, preferred_element_type=jnp.float32)
    grad_bias = jnp.sum(grad_logits.astype(jnp.float32), axis=(0, 1, 2))
    grad_hidden = jnp.einsum(
        "brwk,hk->brwh", grad_logits, head_low, preferred_element_type=jnp.float32
    )
    grad_summed = grad_hidden * silu_slope(summed)
    grad_res_out, gain_two, shift_two = norm_backward(
        grad_summed, normed_two, norm_params[2], scale_two, cell_total
    )
    grad_res_low = grad_res_out.astype(jnp.bfloat16)
    grad_res = kernel_taps(act_pad, grad_res_low)
    grad_act = (
        conv_taps(rims_back(grad_res_low), flipped(res_full), row_local, col_total) + grad_summed
    )
    grad_pre = grad_act * silu_slope(pre_one)
    grad_join_out, gain_one, shift_one = norm_backward(
        grad_pre, normed_one, norm_params[0], scale_one, cell_total
    )
    grad_join_low = grad_join_out.astype(jnp.bfloat16)
    grad_join = kernel_taps(joined_pad, grad_join_low)
    grad_camera = conv_taps(
        rims_back(grad_join_low), flipped(join_full[:, :, :cam_width, :]), row_local, col_total
    ).astype(jnp.bfloat16)
    cells = layout["per_strip"] * LANES
    grad_cells = jnp.pad(
        grad_camera.reshape(strip_cells, cam_width), ((0, cells - strip_cells), (0, 0))
    ).reshape(layout["per_strip"], LANES, cam_width)
    camera_grid = lax.all_gather(grad_cells, "strip", axis=0, tiled=True)
    both_low = jnp.concatenate(
        [bins_low, jnp.pad(context_low, ((0, 0), (0, LANES - cam_width)))], axis=1
    )
    grad_both = unpool(camera_features[0], pool_index[0], both_low, dense, camera_grid, layout)
    grad_depth = jnp.concatenate(
        [grad_both[:, :depth_bins], grad_both[:, LANES : LANES + cam_width]], axis=1
    )
    total_join, total_res = (
        lax.psum(lax.psum_scatter(part, "strip", scatter_dimension=3, tiled=True), "batch")
        for part in (grad_join, grad_res)
    )
    axes = ("batch", "strip")
    devices = lax.axis_size(axes)
    depth_share = lax.all_to_all(
        grad_depth.reshape(devices, -1, grad_depth.shape[1]), axes, 0, 0
    )
    total_depth = everywhere(jnp.sum(depth_share, axis=0)).reshape(grad_depth.shape)
    shares = lax.axis_size("batch")
    small = jnp.concatenate(
        [
            grad_head.reshape(-1),
            grad_bias,
            jnp.stack([local_loss, squares(total_join) / shares, squares(total_res) / shares]),
        ]
    )
    small = summed_everywhere(small)
    total_head = small[: grad_head.size].reshape(grad_head.shape)
    total_bias = small[grad_head.size : grad_head.size + classes]
    loss_sum = small[-3]
    norm_join = jnp.sqrt(small[-2])
    norm_res = jnp.sqrt(small[-1])
    grad_norm = jnp.stack([gain_one, shift_one, gain_two, shift_two])
    norms = [
        jnp.sqrt(squares(total_depth)),
        norm_join,
        norm_res,
        jnp.sqrt(squares(total_head)),
        jnp.sqrt(squares(grad_norm)),
        jnp.sqrt(squares(total_bias)),
    ]
    grads = [total_depth, total_join, total_res, total_head, grad_norm, total_bias]
    clipped = [
        gradient * (CLIP_NORM / jnp.maximum(norm_value, CLIP_NORM))
        for gradient, norm_value in zip(grads, norms)
    ]
    step_value = jnp.float32(STEP)
    rates = [
        0.5 * w_depth.shape[0] ** (-0.5),
        0.5 * (9 * w_join.shape[2]) ** (-0.5),
        0.5 * (9 * w_res.shape[2]) ** (-0.5),
        0.5 * w_head.shape[0] ** (-0.5),
        SMALL_RATE,
        SMALL_RATE,
    ]
    weights = [w_depth, w_join, w_res, w_head, norm_params, head_bias]
    firsts = [m_depth, m_join, m_res, m_head, m_norm, m_bias]
    seconds = [v_depth, v_join, v_res, v_head, v_norm, v_bias]
    result = [jnp.reshape(loss_sum / positives, (1,)), jnp.log(jnp.stack(norms))]
    for weight, gradient, first, second, rate in zip(weights, clipped, firsts, seconds, rates):
        result.extend(adamw(weight, gradient, first, second, rate, step_value))
    return tuple(result)


def solution(mesh):
    in_specs = (
        P("batch", "strip", None),
        P("batch", "strip", None, None),
        P("batch", "strip", None),
        P("batch", None, None),
        P("batch"),
        P(),
        P(),
        P(),
        P(None, None, None, "strip"),
        P(None, None, None, "strip"),
        P(None, None, None, "strip"),
        P(None, None, None, "strip"),
        P(None, None, None, "strip"),
        P(None, None, None, "strip"),
        P(),
        P(),
        P(),
        P(),
        P(),
        P(),
        P(),
        P(),
        P(),
    )
    out_specs = (
        P(),
        P(),
        P(),
        P(),
        P(),
        P(None, None, None, "strip"),
        P(None, None, None, "strip"),
        P(None, None, None, "strip"),
        P(None, None, None, "strip"),
        P(None, None, None, "strip"),
        P(None, None, None, "strip"),
        P(),
        P(),
        P(),
        P(),
        P(),
        P(),
        P(),
        P(),
        P(),
    )
    return jax.shard_map(shards, mesh=mesh, in_specs=in_specs, out_specs=out_specs, check_vma=False)
```

```python
import functools

import jax
import jax.numpy as jnp
from jax import lax
from jax.experimental import pallas as pl
from jax.experimental.pallas import tpu as pltpu
from jax.sharding import PartitionSpec as P

STEP = 5


EPS_NORM = 1e-05
SPREAD_TWICE = 8.0
SMALL_RATE = 0.25
CLIP_NORM = 0.01
FAR = 1e9


def halo(shard):
    peers = lax.axis_size("strip")
    up = [(i, i + 1) for i in range(peers - 1)]
    before = lax.ppermute(shard[-1:], "strip", up)
    after = lax.ppermute(shard[:1], "strip", [(j, i) for i, j in up])
    return [before, shard, after]


def target_kernel(peaks_ref, count_ref, first_ref, gap_ref):
    gap_ref[...] = jnp.full(gap_ref.shape, FAR, jnp.float32)
    shape = gap_ref.shape[1:]
    row_ids = lax.broadcasted_iota(jnp.int32, shape, 0) + first_ref[0]
    col_ids = lax.broadcasted_iota(jnp.int32, shape, 1)

    def visit(slot, carry):
        row_gap = row_ids - peaks_ref[0, slot]
        col_gap = col_ids - peaks_ref[1, slot]
        distance = (row_gap * row_gap + col_gap * col_gap).astype(jnp.float32)
        kind = peaks_ref[2, slot]
        gap_ref[kind] = jnp.minimum(gap_ref[kind], distance)
        return carry

    lax.fori_loop(0, count_ref[0], visit, 0)


def nearest_gaps(box_peaks, box_count, first_row, row_total, col_total, classes):
    return pl.pallas_call(
        target_kernel,
        in_specs=[pl.BlockSpec(memory_space=pltpu.SMEM)] * 3,
        out_specs=pl.BlockSpec(memory_space=pltpu.VMEM),
        out_shape=jax.ShapeDtypeStruct((classes, row_total, col_total), jnp.float32),
        cost_estimate=pl.CostEstimate(flops=4000000, bytes_accessed=1000000, transcendentals=0),
        name="targets",
    )(box_peaks, box_count, first_row[None])


LANES = 128
BF = jnp.bfloat16
F32 = jnp.float32


def plan(pixels, strips, strip_cells):
    per_strip = -(-strip_cells // LANES)
    high = strips * per_strip
    block = 352 if pixels % 352 == 0 and high <= 128 else 48
    return dict(
        per_strip=per_strip,
        high=high,
        offset=high // 2,
        block=block,
        stride=block + 4,
        group=block,
        strip_cells=strip_cells,
    )


def split_cells(index, plan):
    cell = index.astype(F32)
    strip = jnp.floor((cell + 0.5) * (1.0 / plan["strip_cells"]))
    rest = cell - strip * plan["strip_cells"]
    part = jnp.floor((rest + 0.5) * (1.0 / LANES))
    return strip * plan["per_strip"] + part - plan["offset"], rest - part * LANES


def softmax_lanes(logits, bins):
    lane = lax.broadcasted_iota(jnp.int32, logits.shape, 1)
    logits = jnp.where(lane < bins, logits, -jnp.inf)
    powers = jnp.exp(logits - jnp.max(logits, axis=1, keepdims=True))
    return powers / jnp.sum(powers, axis=1, keepdims=True)


def spread(ref, pixel, rows=16):
    return jnp.broadcast_to(ref[pl.ds(pixel, 1), :], (rows, LANES))


def one_hot(row, value, rows, offset=0):
    base = (lax.broadcasted_iota(jnp.int32, (rows, LANES), 0) - offset).astype(F32).astype(BF)
    none = jnp.zeros((16, LANES), BF)
    return [
        jnp.where(base[k : k + 16] == row, value, none) for k in range(0, rows, 16)
    ]


def high_pair(high_ref, depth_ref, first, plan):
    whole = plan["high"] // 16 * 16
    parts = []
    for j in range(2):
        row = spread(high_ref, first + j).astype(BF)
        value = spread(depth_ref, first + j).astype(BF)
        parts += one_hot(row, value, whole, plan["offset"])
    if whole < plan["high"]:
        both = [
            jnp.concatenate([spread(ref, first, 8), spread(ref, first + 1, 8)], 0).astype(BF)
            for ref in (high_ref, depth_ref)
        ]
        base = lax.broadcasted_iota(jnp.int32, (16, LANES), 0)
        base = jnp.where(base < 8, base, base - 8) + (whole - plan["offset"])
        none = jnp.zeros((16, LANES), BF)
        parts.append(jnp.where(base.astype(F32).astype(BF) == both[0], both[1], none))
    return jnp.concatenate(parts, 0)


def pool_kernel(place_ref, feat_ref, index_ref, weight_ref, own_ref, other_ref, dense_ref, both_ref, high_ref, low_ref, depth_ref, held, total, *, plan):
    bins = index_ref.shape[1]
    block, stride, high = (plan[k] for k in ("block", "stride", "high"))
    step = pl.program_id(0)

    @pl.when(step == 0)
    def _():
        high_ref[...] = jnp.zeros_like(high_ref)
        low_ref[...] = jnp.zeros_like(low_ref)
        total[...] = jnp.zeros_like(total)
        channels = total.shape[1]
        both_ref[...] = jnp.zeros_like(both_ref)
        both_ref[:bins] = weight_ref[:bins].astype(BF)
        both_ref[LANES : LANES + channels] = weight_ref[bins : bins + channels].astype(BF)

    feat = feat_ref[...]
    logits = lax.dot_general(feat, both_ref[:LANES], (((1,), (1,)), ((), ())), preferred_element_type=F32)
    depth_ref[...] = softmax_lanes(logits, bins)
    channels = total.shape[1]
    context_low = both_ref[LANES : LANES + channels]
    context = lax.dot_general(context_low, feat, (((1,), (1,)), ((), ())), preferred_element_type=F32).astype(BF)
    high_id, low_id = split_cells(index_ref[...], plan)
    high_ref[:, :bins] = high_id
    low_ref[:, :bins] = low_id
    one = jnp.ones((16, LANES), BF)

    def scatter(group, carry):
        for k in range(0, plan["group"], 2):
            first = group * plan["group"] + k
            left = high_pair(high_ref, depth_ref, first, plan)
            right = []
            for j in range(2):
                low = spread(low_ref, first + j).astype(BF)
                right.append(jnp.concatenate(one_hot(low, one, LANES), 0))
            tile = lax.dot_general(
                left, jnp.concatenate(right, 0), (((1,), (1,)), ((), ())), preferred_element_type=F32
            )
            whole = high // 16 * 16
            for j in range(2):
                part = tile[:, j * LANES : (j + 1) * LANES]
                held[pl.ds(first + j, whole, stride=stride), :] = part[j * whole : (j + 1) * whole]
                if whole < high:
                    held[pl.ds(first + j + whole * stride, 8, stride=stride), :] = part[
                        2 * whole + 8 * j : 2 * whole + 8 * j + 8
                    ]
        return carry

    lax.fori_loop(0, block // plan["group"], scatter, 0)

    def gather(k, carry):
        parts = []
        for j in range(2):
            part = held[pl.ds((k * 2 + j) * stride, block), :].astype(BF)
            dense_ref[k * 2 + j] = part
            parts.append(part)
        out = jnp.dot(context, jnp.concatenate(parts, 1), preferred_element_type=F32)
        for j in range(2):
            total[k * 2 + j] += out[:, j * LANES : (j + 1) * LANES]
        return carry

    lax.fori_loop(0, high // 2, gather, 0, unroll=36)

    @pl.when(step == pl.num_programs(0) - 1)
    def _():
        count = plan["per_strip"]
        chips = own_ref.shape[0]
        for shift in range(chips):
            chip = lax.rem(place_ref[0] + shift, chips)
            for ref, core in ((own_ref, place_ref[1]), (other_ref, 1 - place_ref[1])):
                first = (2 * chip + core) * count
                ref[shift] = total[pl.ds(first, count)].astype(BF)


def pool(place, features, index, weight, plan):
    pixels, width = features.shape
    bins = index.shape[1]
    channels = weight.shape[0] - bins
    block, high = plan["block"], plan["high"]
    halves = (high // plan["per_strip"] // 2, plan["per_strip"], channels, LANES)
    return pl.pallas_call(
        functools.partial(pool_kernel, plan=plan),
        grid=(pixels // block,),
        in_specs=[
            pl.BlockSpec(memory_space=pltpu.SMEM),
            pl.BlockSpec((block, width), lambda i: (i, 0)),
            pl.BlockSpec((block, bins), lambda i: (i, 0)),
            pl.BlockSpec(weight.shape, lambda i: (0, 0)),
        ],
        out_specs=[
            pl.BlockSpec(halves, lambda i: (0, 0, 0, 0)),
            pl.BlockSpec(halves, lambda i: (0, 0, 0, 0)),
            pl.BlockSpec((high, block, LANES), lambda i: (0, i, 0)),
            pl.BlockSpec((2 * LANES, width), lambda i: (0, 0)),
        ],
        out_shape=[
            jax.ShapeDtypeStruct(halves, BF),
            jax.ShapeDtypeStruct(halves, BF),
            jax.ShapeDtypeStruct((high, pixels, LANES), BF),
            jax.ShapeDtypeStruct((2 * LANES, width), BF),
        ],
        scratch_shapes=[pltpu.VMEM((block, LANES), F32)] * 3
        + [
            pltpu.VMEM((high * plan["stride"], LANES), F32),
            pltpu.VMEM((high, channels, LANES), F32),
        ],
        compiler_params=pltpu.CompilerParams(vmem_limit_bytes=56 << 20),
        cost_estimate=pl.CostEstimate(
            flops=4 * pixels * high * LANES * LANES,
            bytes_accessed=2 * pixels * high * LANES,
            transcendentals=0,
        ),
        name="pool",
    )(place, features, index, weight)


def unpool_kernel(place_ref, feat_ref, index_ref, both_ref, dense_ref, mine_ref, theirs_ref, grad_ref, high_ref, low_ref, pick_ref, held, sum_ref, grid_ref, *, plan):
    bins = index_ref.shape[1]
    channels = grid_ref.shape[1]
    chips, count = mine_ref.shape[:2]
    block, stride, high = (plan[k] for k in ("block", "stride", "high"))
    step = pl.program_id(0)

    @pl.when(step == 0)
    def _():
        high_ref[...] = jnp.zeros_like(high_ref)
        low_ref[...] = jnp.zeros_like(low_ref)
        held[...] = jnp.zeros_like(held)
        grad_ref[...] = jnp.zeros_like(grad_ref)
        for shift in range(chips):
            chip = lax.rem(place_ref[0] + (chips - shift), chips)
            for ref, core in ((mine_ref, place_ref[1]), (theirs_ref, 1 - place_ref[1])):
                grid_ref[pl.ds((2 * chip + core) * count, count)] = ref[shift]

    feat = feat_ref[...]
    logits = lax.dot_general(feat, both_ref[...], (((1,), (1,)), ((), ())), preferred_element_type=F32)
    depth = softmax_lanes(logits[:, :LANES], bins)
    context = logits[:, LANES : LANES + channels].astype(BF)
    high_id, low_id = split_cells(index_ref[...], plan)
    high_ref[:, :bins] = high_id
    low_ref[:, :bins] = low_id

    def project(k, carry):
        grid = jnp.concatenate([grid_ref[k * 2], grid_ref[k * 2 + 1]], 1)
        out = jnp.dot(context, grid, preferred_element_type=F32)
        for j in range(2):
            held[pl.ds((k * 2 + j) * stride, block), :] = out[:, j * LANES : (j + 1) * LANES]
        return carry

    lax.fori_loop(0, high // 2, project, 0, unroll=36)
    parts = 72

    def mix(k, carry):
        dense = jnp.concatenate([dense_ref[k * parts + j] for j in range(parts)], 1)
        grid = jnp.concatenate([grid_ref[k * parts + j] for j in range(parts)], 1)
        sum_ref[...] += lax.dot_general(
            dense, grid, (((1,), (1,)), ((), ())), preferred_element_type=F32
        )
        return carry

    sum_ref[...] = jnp.zeros_like(sum_ref)
    lax.fori_loop(0, high // parts, mix, 0)
    one = jnp.ones((16, LANES), BF)
    rows = (lax.broadcasted_iota(jnp.int32, (high, LANES), 0) - plan["offset"]).astype(F32)

    def collect(group, carry):
        for k in range(0, plan["group"], 2):
            first = group * plan["group"] + k
            left, right = [], []
            for j in range(2):
                left.append(held[pl.ds(first + j, high, stride=stride), :])
                low = spread(low_ref, first + j).astype(BF)
                right.append(jnp.concatenate(one_hot(low, one, LANES), 0))
            tile = jnp.dot(jnp.concatenate(left, 0).astype(BF), jnp.concatenate(right, 1), preferred_element_type=F32)
            for j in range(2):
                part = tile[j * high : (j + 1) * high, j * LANES : (j + 1) * LANES]
                kept = jnp.where(rows == high_ref[pl.ds(first + j, 1), :], part, 0.0)
                pick_ref[pl.ds(first + j, 1), :] = jnp.sum(kept, axis=0, keepdims=True)
        return carry

    lax.fori_loop(0, block // plan["group"], collect, 0)
    grad_prob = pick_ref[...]
    grad_context = sum_ref[...]
    grad_depth = depth * (grad_prob - jnp.sum(grad_prob * depth, axis=1, keepdims=True))
    grad_low = jnp.concatenate(
        [grad_depth, grad_context, jnp.zeros((block, LANES - channels), F32)], axis=1
    ).astype(BF)
    grad_ref[...] += lax.dot_general(grad_low, feat, (((0,), (0,)), ((), ())), preferred_element_type=F32)


def unpool(place, features, index, both_low, dense, mine, theirs, plan):
    pixels, width = features.shape
    bins = index.shape[1]
    channels = mine.shape[2]
    block, high = plan["block"], plan["high"]
    return pl.pallas_call(
        functools.partial(unpool_kernel, plan=plan),
        grid=(pixels // block,),
        in_specs=[
            pl.BlockSpec(memory_space=pltpu.SMEM),
            pl.BlockSpec((block, width), lambda i: (i, 0)),
            pl.BlockSpec((block, bins), lambda i: (i, 0)),
            pl.BlockSpec(both_low.shape, lambda i: (0, 0)),
            pl.BlockSpec((high, block, LANES), lambda i: (0, i, 0)),
            pl.BlockSpec(mine.shape, lambda i: (0, 0, 0, 0)),
            pl.BlockSpec(theirs.shape, lambda i: (0, 0, 0, 0)),
        ],
        out_specs=pl.BlockSpec((2 * LANES, width), lambda i: (0, 0)),
        out_shape=jax.ShapeDtypeStruct((2 * LANES, width), F32),
        scratch_shapes=[pltpu.VMEM((block, LANES), F32)] * 3
        + [
            pltpu.VMEM((high * plan["stride"], LANES), F32),
            pltpu.VMEM((block, channels), F32),
            pltpu.VMEM((high, channels, LANES), BF),
        ],
        compiler_params=pltpu.CompilerParams(vmem_limit_bytes=56 << 20),
        cost_estimate=pl.CostEstimate(
            flops=6 * pixels * high * LANES * LANES,
            bytes_accessed=2 * pixels * high * LANES,
            transcendentals=0,
        ),
        name="unpool",
    )(place, features, index, both_low, dense, mine, theirs)


def fill_windows(window_ref, part, cols, span):
    before_ref, shard_ref, after_ref = part
    rows = shard_ref.shape[0]
    width = window_ref.shape[2]
    window_ref[...] = jnp.zeros_like(window_ref)
    for row in range(rows + 2):
        if row == 0:
            line = before_ref[0]
        elif row == rows + 1:
            line = after_ref[0]
        else:
            line = shard_ref[row - 1]
        line = line[:, :width]
        start = row * span
        window_ref[0, start + 1 : start + cols] = line[: cols - 1]
        window_ref[1, start : start + cols] = line
        window_ref[2, start : start + cols - 1] = line[1:]


def window_scratch(part, width, span):
    return pltpu.VMEM((3, (part[1].shape[0] + 2) * span, width), BF)


def span_of(cols):
    return -(-cols // 16) * 16


def conv_kernel(kernel_ref, *refs, count, lanes, turned, finish):
    parts = [refs[3 * k : 3 * k + 3] for k in range(count)]
    rows, cols = parts[0][1].shape[:2]
    span = span_of(cols)
    outs = refs[3 * count : -count]
    windows = refs[-count:]
    left, right = [], []
    for part, window_ref, place in zip(parts, windows, lanes):
        fill_windows(window_ref, part, cols, span)
        for tap in range(9):
            upward, across = tap // 3, tap % 3
            left.append(window_ref[across, upward * span : (upward + rows) * span])
            right.append(kernel_ref[8 - tap if turned else tap, :, place[0] : place[1]])
    left = jnp.concatenate(left, 1)
    if turned:
        total = jnp.dot(left, jnp.concatenate(right, 0), preferred_element_type=F32)
    else:
        total = lax.dot_general(
            left, jnp.concatenate(right, 1), (((1,), (1,)), ((), ())), preferred_element_type=F32
        )
    finish(total, rows, cols, span, *outs)


def keep_rows(total, rows, cols, span, out_ref):
    for row in range(rows):
        out_ref[row] = total[row * span : row * span + cols]


def keep_moments(total, rows, cols, span, out_ref, stats_ref):
    keep_rows(total, rows, cols, span, out_ref)
    cells = float(rows * cols)
    center = jnp.sum(total, axis=0, keepdims=True) / cells
    spot = lax.broadcasted_iota(jnp.int32, (span, total.shape[1]), 0)
    spread_sum = jnp.zeros_like(center)
    for row in range(rows):
        apart = total[row * span : (row + 1) * span] - center
        apart = jnp.where(spot < cols, apart, 0.0)
        spread_sum = spread_sum + jnp.sum(apart * apart, axis=0, keepdims=True)
    stats_ref[...] = jnp.concatenate([center, spread_sum], 0)


def keep_cells(total, rows, cols, span, out_ref):
    cells, channels = out_ref.shape[0] * LANES, out_ref.shape[1]
    flat = [total[row * span : row * span + cols] for row in range(rows)]
    flat.append(jnp.zeros((cells - rows * cols, total.shape[1]), F32))
    flat = jnp.concatenate(flat, 0)
    for part in range(out_ref.shape[0]):
        out_ref[part] = flat[part * LANES : (part + 1) * LANES].T[:channels].astype(BF)


def convolve(parts, kernel, lanes, turned, finish, outs):
    rows, cols = parts[0][1].shape[:2]
    span = span_of(cols)
    widths = [kernel.shape[1] if turned else place[1] - place[0] for place in lanes]
    depth = sum(widths)
    flat = [array for part in parts for array in part]
    return pl.pallas_call(
        functools.partial(
            conv_kernel, count=len(parts), lanes=lanes, turned=turned, finish=finish
        ),
        in_specs=[pl.BlockSpec(memory_space=pltpu.VMEM)] * (1 + len(flat)),
        out_specs=[pl.BlockSpec(memory_space=pltpu.VMEM)] * len(outs),
        out_shape=outs,
        scratch_shapes=[
            window_scratch(part, width, span) for part, width in zip(parts, widths)
        ],
        compiler_params=pltpu.CompilerParams(vmem_limit_bytes=48 << 20),
        cost_estimate=pl.CostEstimate(
            flops=18 * rows * span * depth * kernel.shape[1],
            bytes_accessed=2 * kernel.size,
            transcendentals=0,
        ),
        name="convolve",
    )(kernel, *flat)


def taps_kernel(place_ref, grad_ref, *refs, widths):
    count = len(widths)
    parts = [refs[3 * k : 3 * k + 3] for k in range(count)]
    own_ref, other_ref = refs[3 * count : 3 * count + 2]
    windows = refs[3 * count + 2 : 4 * count + 2]
    flipped_grad, total = refs[4 * count + 2 :]
    rows, cols, depth = grad_ref.shape
    owned = own_ref.shape[2]
    chips = own_ref.shape[0]
    span = span_of(cols)
    for part, window_ref in zip(parts, windows):
        fill_windows(window_ref, part, cols, span)
    flat = []
    for row in range(rows):
        flat += [grad_ref[row], jnp.zeros((span - cols, depth), BF)]
    flipped_grad[...] = jnp.concatenate(flat, 0).T
    for tap in range(9):
        upward, across = tap // 3, tap % 3
        first = 0
        for window_ref in windows:
            window = window_ref[across, upward * span : (upward + rows) * span]
            total[:, first : first + window.shape[1]] = jnp.dot(
                flipped_grad[...], window, preferred_element_type=F32
            )
            first += window.shape[1]
        for shift in range(chips):
            chip = lax.rem(place_ref[0] + shift, chips)
            for ref, core in ((own_ref, place_ref[1]), (other_ref, 1 - place_ref[1])):
                start = pl.multiple_of((2 * chip + core) * owned, 8)
                ref[shift, tap] = total[pl.ds(start, owned)].astype(BF)


def taps(place, parts, widths, grad, chips):
    rows, cols, depth = grad.shape
    channels = sum(widths)
    span = span_of(cols)
    flat = [array for part in parts for array in part]
    half = jax.ShapeDtypeStruct((chips, 9, depth // chips // 2, channels), BF)
    return pl.pallas_call(
        functools.partial(taps_kernel, widths=widths),
        in_specs=[pl.BlockSpec(memory_space=pltpu.SMEM)]
        + [pl.BlockSpec(memory_space=pltpu.VMEM)] * (1 + len(flat)),
        out_specs=[pl.BlockSpec(memory_space=pltpu.VMEM)] * 2,
        out_shape=[half, half],
        scratch_shapes=[window_scratch(part, width, span) for part, width in zip(parts, widths)]
        + [pltpu.VMEM((depth, rows * span), BF), pltpu.VMEM((depth, channels), F32)],
        compiler_params=pltpu.CompilerParams(vmem_limit_bytes=40 << 20),
        cost_estimate=pl.CostEstimate(
            flops=18 * rows * span * depth * channels,
            bytes_accessed=18 * depth * channels + 4 * rows * cols * channels,
            transcendentals=0,
        ),
        name="taps",
    )(place, grad, *flat)


def settle_kernel(*refs):
    out_ref = refs[-1]
    rows, cols = out_ref.shape[:2]
    total = refs[0][...].astype(F32)
    for ref in refs[1:-1]:
        total = total + ref[...].astype(F32)
    parts = total.shape[0]
    flat = jnp.concatenate([total[part].T for part in range(parts)], 0)
    spare = jnp.zeros((cols, out_ref.shape[2] - flat.shape[1]), F32)
    for row in range(rows):
        line = flat[row * cols : (row + 1) * cols]
        out_ref[row] = jnp.concatenate([line, spare], 1).astype(BF)


def settle(parts, rows, cols):
    return pl.pallas_call(
        settle_kernel,
        in_specs=[pl.BlockSpec(memory_space=pltpu.VMEM)] * len(parts),
        out_specs=pl.BlockSpec(memory_space=pltpu.VMEM),
        out_shape=jax.ShapeDtypeStruct((rows, cols, LANES), BF),
        compiler_params=pltpu.CompilerParams(vmem_limit_bytes=32 << 20),
        name="settle",
    )(*parts)


def split_bits(value):
    pieces = []
    for _ in range(3):
        piece = lax.reduce_precision(value, 8, 7)
        pieces.append(piece)
        value = value - piece
    return pieces


def update_kernel(mixed_ref, extra_ref, taps_ref, norm_ref, count_ref, *refs, shapes, rates):
    depth_bins, cam_width, classes, hidden_width = shapes
    mixed = mixed_ref[...].astype(F32)
    column = LANES + cam_width
    edge = taps_ref.shape[2] - cam_width
    grads = [
        jnp.concatenate([mixed[:depth_bins], mixed[LANES:column]], 0),
        jnp.concatenate([taps_ref[:, :, edge:], taps_ref[:, :, hidden_width:edge]], 2),
        taps_ref[:, :, :hidden_width],
        mixed[column : column + classes],
        norm_ref[...],
        mixed[column + classes : column + classes + 1, :classes],
    ]
    sums = jnp.sum(extra_ref[...].astype(F32), axis=0, keepdims=True)
    lane = lax.broadcasted_iota(jnp.int32, sums.shape, 1)
    squared = [None if k in (1, 2) else jnp.sum(grad * grad) for k, grad in enumerate(grads)]
    squared[1] = jnp.sum(jnp.where(lane < 3, sums, 0.0))
    squared[2] = jnp.sum(jnp.where((lane >= 3) & (lane < 6), sums, 0.0))
    loss_sum = jnp.sum(jnp.where((lane >= 6) & (lane < 9), sums, 0.0), axis=1, keepdims=True)
    inputs, outputs = refs[:18], refs[18:]
    loss_ref, norms_ref = outputs[:2]
    loss_ref[...] = loss_sum / count_ref[...]
    norms = jnp.zeros((1, LANES), F32)
    spot = lax.broadcasted_iota(jnp.int32, norms.shape, 1)
    for k, grad in enumerate(grads):
        size = jnp.sqrt(jnp.full((1, LANES), squared[k], F32))
        norms = jnp.where(spot == k, jnp.log(size), norms)
        factor = CLIP_NORM / jnp.maximum(size, CLIP_NORM)
        factor = jnp.max(factor)
        weight, first, second = (ref[...] for ref in inputs[3 * k : 3 * k + 3])
        results = adamw(weight, grad * factor, first, second, rates[k], STEP)
        for ref, result in zip(outputs[2 + 3 * k : 5 + 3 * k], results):
            ref[...] = result
    norms_ref[...] = norms


def update(mixed, extra, taps_sum, norm, positives, states, shapes, rates):
    args = [mixed, extra, taps_sum, norm, positives.reshape(1, 1)] + states
    return pl.pallas_call(
        functools.partial(update_kernel, shapes=shapes, rates=rates),
        in_specs=[pl.BlockSpec(memory_space=pltpu.VMEM)] * len(args),
        out_specs=[pl.BlockSpec(memory_space=pltpu.VMEM)] * 20,
        out_shape=[jax.ShapeDtypeStruct((1, 1), F32), jax.ShapeDtypeStruct((1, LANES), F32)]
        + [jax.ShapeDtypeStruct(state.shape, F32) for state in states],
        compiler_params=pltpu.CompilerParams(vmem_limit_bytes=48 << 20),
        name="update",
    )(*args)


def swapped(tensor):
    strips = lax.axis_size("strip")
    return lax.ppermute(tensor, "strip", [(i, i ^ 1) for i in range(strips)])


def halves_summed(own, other):
    return own.astype(F32) + swapped(other).astype(F32)


def moved(tensor, shift):
    strips = lax.axis_size("strip")
    return lax.ppermute(tensor, "strip", [(i, (i + 2 * shift) % strips) for i in range(strips)])


def far_first(chips):
    return sorted(range(1, chips), key=lambda shift: -min(shift, chips - shift))


def along_chips(tensor):
    chips = tensor.shape[0]
    arrived = {shift: moved(tensor[shift], shift) for shift in far_first(chips)}
    return [tensor[0]] + [arrived[shift] for shift in range(1, chips)]


def total_of(parts):
    total = parts[0].astype(F32)
    for part in parts[1:]:
        total = total + part.astype(F32)
    return total


def from_chips(tensor, later=None):
    chips = lax.axis_size("strip") // 2
    arrived = {shift: moved(tensor, shift) for shift in far_first(chips)}
    if later is not None:
        arrived[1], later = lax.optimization_barrier((arrived[1], later))
    return [tensor] + [arrived[shift] for shift in range(1, chips)], later


def arrange_kernel(place_ref, mine_ref, theirs_ref, out_ref):
    chips, taps_total, owned = mine_ref.shape[:3]
    for chip in range(chips):
        shift = lax.rem(place_ref[0] + (chips - chip), chips)
        for core in range(2):
            first = (2 * chip + core) * owned

            @pl.when(place_ref[1] == core)
            def _():
                for tap in range(taps_total):
                    out_ref[tap, first : first + owned] = mine_ref[shift, tap]

            @pl.when(place_ref[1] != core)
            def _():
                for tap in range(taps_total):
                    out_ref[tap, first : first + owned] = theirs_ref[shift, tap]


def arrange(place, mine, theirs):
    chips, taps_total, owned, width = mine.shape
    return pl.pallas_call(
        arrange_kernel,
        in_specs=[pl.BlockSpec(memory_space=pltpu.SMEM)]
        + [pl.BlockSpec(memory_space=pltpu.VMEM)] * 2,
        out_specs=pl.BlockSpec(memory_space=pltpu.VMEM),
        out_shape=jax.ShapeDtypeStruct((taps_total, 2 * chips * owned, width), BF),
        compiler_params=pltpu.CompilerParams(vmem_limit_bytes=32 << 20),
        cost_estimate=pl.CostEstimate(
            flops=0, bytes_accessed=8 * mine.size, transcendentals=0
        ),
        name="arrange",
    )(place, mine, theirs)


def everywhere(tensor):
    axes = ("batch", "strip")
    copies = jnp.broadcast_to(tensor[None], (lax.axis_size(axes),) + tensor.shape)
    return lax.all_to_all(copies, axes, 0, 0)


def summed_everywhere(tensor):
    return jnp.sum(everywhere(tensor), axis=0)


def moments(stats, cells, extra_term):
    extra_row = jnp.full((1, stats.shape[1]), extra_term)
    shared = everywhere(jnp.concatenate([stats, extra_row]))
    centers = shared[:, 0]
    total = jnp.mean(centers, axis=0)
    spread_mean = jnp.mean(shared[:, 1] / cells + (centers - total) ** 2, axis=0)
    return (total, lax.rsqrt(spread_mean + EPS_NORM), jnp.sum(shared[:, 2, 0]))


def norm_backward(grad_norm, normed, gain, scale_inv, cell_total, later):
    sums = jnp.stack(
        [jnp.sum(grad_norm, axis=(0, 1, 2)), jnp.sum(grad_norm * normed, axis=(0, 1, 2))]
    )
    sums, later = lax.optimization_barrier((sums, later))
    grad_shift, grad_gain = summed_everywhere(sums)
    grad_in = (
        gain * scale_inv * (grad_norm - grad_shift / cell_total - normed * grad_gain / cell_total)
    )
    return (grad_in, grad_gain, grad_shift, later)


def over_batch(tensor):
    count = lax.axis_size("batch")
    shifts = [[(i, (i + s) % count) for i in range(count)] for s in range(1, count)]
    return [tensor] + [lax.ppermute(tensor, "batch", pairs) for pairs in shifts]


def in_order(parts):
    count = len(parts)
    place = lax.axis_index("batch")
    parts = [part.astype(F32) for part in parts]
    total = None
    for member in range(count):
        part = parts[-member % count]
        for here in range(1, count):
            part = jnp.where(place == here, parts[(here - member) % count], part)
        total = part if total is None else total + part
    return total


def silu_slope(value):
    sig = jax.nn.sigmoid(value)
    return sig * (1.0 + value * (1.0 - sig))


def adamw(weight, gradient, first, second, rate, step_value):
    first = 0.9 * first + 0.1 * gradient
    second = 0.999 * second + 0.001 * gradient * gradient
    fix_one = 1.0 - 0.9**step_value
    fix_two = 1.0 - 0.999**step_value
    update = first / fix_one / (jnp.sqrt(second / fix_two) + 1e-08) + 0.01 * weight
    return (weight - rate * update, first, second)


def squares(tensor):
    return jnp.sum(tensor * tensor)


def shards(
    camera_features,
    lidar_bev,
    pool_index,
    box_peaks,
    box_count,
    w_depth,
    m_depth,
    v_depth,
    w_join,
    m_join,
    v_join,
    w_res,
    m_res,
    v_res,
    w_head,
    m_head,
    v_head,
    norm_params,
    m_norm,
    v_norm,
    head_bias,
    m_bias,
    v_bias,
):
    samples, row_local, col_total, lidar_width = lidar_bev.shape
    strips = lax.axis_size("strip")
    row_total = row_local * strips
    cell_total = float(samples * lax.axis_size("batch") * row_total * col_total)
    depth_bins = pool_index.shape[2]
    classes = w_head.shape[1]
    owned = w_join.shape[3]
    cam_width = w_depth.shape[1] - depth_bins
    first_row = lax.axis_index("strip") * row_local
    place = lax.axis_index("strip")
    place = jnp.stack([place // 2, place % 2]).astype(jnp.int32)
    hidden_width = w_res.shape[2]
    taps_low = jnp.concatenate(
        [
            jnp.swapaxes(part, 2, 3).reshape(9, owned, -1)
            for part in (w_res, w_join[:, :, cam_width:], w_join[:, :, :cam_width])
        ],
        axis=2,
    ).astype(BF)
    taps_low = jnp.pad(taps_low, ((0, 0), (0, 0), (0, LANES - cam_width)))
    if owned % 16 == 0:
        taps_mine = jnp.stack(from_chips(taps_low)[0])
    head_low = w_head.astype(jnp.bfloat16)
    strip_cells = row_local * col_total
    layout = plan(camera_features.shape[1], strips, strip_cells)
    own, other, dense, both_low = pool(
        place, camera_features[0], pool_index[0], w_depth.T, layout
    )
    if owned % 16 == 0:
        other, taps_mine = lax.optimization_barrier((other, taps_mine))
    pooled_halves = halves_summed(own, other).astype(BF)
    pooled = along_chips(pooled_halves)
    if owned % 16 == 0:
        taps_full = arrange(place, taps_mine, swapped(taps_mine))
    else:
        taps_full = lax.all_gather(taps_low, "strip", axis=1, tiled=True)
    lidar_parts = halo(lidar_bev[0])
    gaps = nearest_gaps(
        box_peaks[0], box_count, first_row, row_local, col_total, classes
    )[:, None]
    pooled, gaps, taps_full, lidar_parts = lax.optimization_barrier(
        (pooled, gaps, taps_full, lidar_parts)
    )
    heatmap = jnp.where(gaps < FAR, jnp.exp(-gaps / SPREAD_TWICE), 0.0)
    struck = (gaps == 0.0).astype(jnp.float32)
    res_lanes = (0, hidden_width)
    lidar_lanes = (hidden_width, hidden_width + lidar_width)
    camera_lanes = (hidden_width + lidar_width, hidden_width + lidar_width + LANES)
    wide_out = jax.ShapeDtypeStruct((row_local, col_total, hidden_width), F32)
    stats_out = jax.ShapeDtypeStruct((2, hidden_width), F32)
    camera_parts = halo(settle(pooled, row_local, col_total))
    join_out, stats = convolve(
        [lidar_parts, camera_parts],
        taps_full,
        [lidar_lanes, camera_lanes],
        False,
        keep_moments,
        [wide_out, stats_out],
    )
    cells = float(strip_cells)
    center_one, scale_one, positives = moments(stats, cells, jnp.sum(struck))
    join_out = join_out[None]
    normed_one = (join_out - center_one) * scale_one
    pre_one = normed_one * norm_params[0] + norm_params[1]
    act_one = jax.nn.silu(pre_one).astype(jnp.bfloat16)
    act_parts = halo(act_one[0])
    res_out, stats = convolve(
        [act_parts], taps_full, [res_lanes], False, keep_moments, [wide_out, stats_out]
    )
    res_out = res_out[None]
    center_two, scale_two, unused_term = moments(stats, cells, jnp.float32(0.0))
    normed_two = (res_out - center_two) * scale_two
    summed = normed_two * norm_params[2] + norm_params[3] + act_one.astype(jnp.float32)
    hidden = jax.nn.silu(summed).astype(jnp.bfloat16)
    logits = (
        jnp.einsum("brwh,hk->kbrw", hidden, head_low, preferred_element_type=jnp.float32)
        + head_bias[:, None, None, None]
    )
    prob = jax.nn.sigmoid(logits)
    soft_neg = jax.nn.softplus(-logits)
    soft_pos = jax.nn.softplus(logits)
    weighting = (1.0 - heatmap) ** 4
    local_loss = jnp.sum(struck * (1.0 - prob) ** 2 * soft_neg + weighting * prob**2 * soft_pos)
    grad_pos = -2.0 * prob * (1.0 - prob) ** 2 * soft_neg - (1.0 - prob) ** 3
    grad_neg = 2.0 * prob**2 * (1.0 - prob) * soft_pos + prob**3
    grad_logits = ((struck * grad_pos + weighting * grad_neg) / positives).astype(jnp.bfloat16)
    grad_hidden = jnp.einsum(
        "kbrw,hk->brwh", grad_logits, head_low, preferred_element_type=jnp.float32
    )
    grad_summed = grad_hidden * silu_slope(summed)
    grad_res_out, gain_two, shift_two, (hidden_late, logits_late) = norm_backward(
        grad_summed, normed_two, norm_params[2], scale_two, cell_total, (hidden, grad_logits)
    )
    grad_head = jnp.einsum(
        "brwh,kbrw->kh", hidden_late, logits_late, preferred_element_type=jnp.float32
    )
    grad_bias = jnp.sum(logits_late.astype(jnp.float32), axis=(1, 2, 3))
    grad_res_low = grad_res_out.astype(jnp.bfloat16)
    grad_act = (
        convolve([halo(grad_res_low[0])], taps_full, [res_lanes], True, keep_rows, [wide_out])[0]
        + grad_summed
    )
    grad_pre = grad_act * silu_slope(pre_one)
    grad_join_out, gain_one, shift_one, (res_late,) = norm_backward(
        grad_pre, normed_one, norm_params[0], scale_one, cell_total, (grad_res_low,)
    )
    own_res, other_res = taps(
        place, [act_parts], [hidden_width], res_late[0], strips // 2
    )
    grad_join_low = grad_join_out.astype(jnp.bfloat16)
    cells_out = jax.ShapeDtypeStruct((layout["per_strip"], cam_width, LANES), BF)
    (grad_cells,) = convolve(
        [halo(grad_join_low[0])], taps_full, [camera_lanes], True, keep_cells, [cells_out]
    )
    grid_parts, join_late = from_chips(grad_cells, grad_join_low)
    grid_mine = jnp.stack(grid_parts)
    own_join, other_join = taps(
        place,
        [lidar_parts, camera_parts],
        [lidar_width, cam_width],
        join_late[0],
        strips // 2,
    )
    grid_theirs = swapped(grid_mine)
    grads = jnp.concatenate(
        [halves_summed(own_res, other_res), halves_summed(own_join, other_join)], axis=-1
    )
    taps_parts = along_chips(grads.astype(BF))
    grad_both = unpool(
        place, camera_features[0], pool_index[0], both_low, dense, grid_mine, grid_theirs, layout
    )
    grad_both, taps_parts = lax.optimization_barrier((grad_both, taps_parts))
    parts = over_batch(total_of(taps_parts).astype(BF))
    axes = ("batch", "strip")
    devices = lax.axis_size(axes)
    column = LANES + cam_width
    width = w_depth.shape[0]
    extra = jnp.concatenate(
        [
            jnp.zeros((column, width), F32),
            grad_head,
            jnp.pad(grad_bias, (0, width - classes))[None],
            jnp.zeros((2 * LANES - column - classes - 1, width), F32),
        ]
    )
    mixed = (grad_both + extra).astype(BF).reshape(devices, -1, width)
    mixed = jnp.sum(lax.all_to_all(mixed, axes, 0, 0).astype(F32), axis=0)
    total_taps = in_order(parts)
    shares = lax.axis_size("batch")
    scalars = [
        squares(total_taps[..., hidden_width:]) / shares,
        squares(total_taps[..., :hidden_width]) / shares,
        local_loss,
    ]
    pieces = jnp.stack([piece for scalar in scalars for piece in split_bits(scalar)])
    pieces = jnp.pad(pieces[None], ((0, mixed.shape[0] - 1), (0, LANES - pieces.shape[0])))
    shared = everywhere(jnp.concatenate([mixed, pieces], axis=1).astype(BF))
    grad_norm = jnp.stack([gain_one, shift_one, gain_two, shift_two])
    rates = [
        0.5 * w_depth.shape[0] ** (-0.5),
        0.5 * (9 * w_join.shape[2]) ** (-0.5),
        0.5 * (9 * w_res.shape[2]) ** (-0.5),
        0.5 * w_head.shape[0] ** (-0.5),
        SMALL_RATE,
        SMALL_RATE,
    ]
    weights = [w_depth, w_join, w_res, w_head, norm_params, head_bias]
    firsts = [m_depth, m_join, m_res, m_head, m_norm, m_bias]
    seconds = [v_depth, v_join, v_res, v_head, v_norm, v_bias]
    views = [
        jnp.transpose,
        lambda state: jnp.swapaxes(state, 2, 3).reshape(9, owned, -1),
        lambda state: jnp.swapaxes(state, 2, 3).reshape(9, owned, -1),
        jnp.transpose,
        lambda state: state,
        lambda state: state[None],
    ]
    backs = [
        jnp.transpose,
        lambda state: jnp.swapaxes(state.reshape(3, 3, owned, -1), 2, 3),
        lambda state: jnp.swapaxes(state.reshape(3, 3, owned, -1), 2, 3),
        jnp.transpose,
        lambda state: state,
        lambda state: state[0],
    ]
    states = [
        view(state)
        for view, group in zip(views, zip(weights, firsts, seconds))
        for state in group
    ]
    loss, norms, *states = update(
        shared[:, :, :width].reshape(2 * LANES, width),
        shared[:, 0, width:],
        total_taps,
        grad_norm,
        positives,
        states,
        (depth_bins, cam_width, classes, hidden_width),
        rates,
    )
    result = [loss[0], norms[0, :6]]
    for k, state in enumerate(states):
        result.append(backs[k // 3](state))
    return tuple(result)


def solution(mesh):
    in_specs = (
        P("batch", "strip", None),
        P("batch", "strip", None, None),
        P("batch", "strip", None),
        P("batch", None, None),
        P("batch"),
        P(),
        P(),
        P(),
        P(None, None, None, "strip"),
        P(None, None, None, "strip"),
        P(None, None, None, "strip"),
        P(None, None, None, "strip"),
        P(None, None, None, "strip"),
        P(None, None, None, "strip"),
        P(),
        P(),
        P(),
        P(),
        P(),
        P(),
        P(),
        P(),
        P(),
    )
    out_specs = (
        P(),
        P(),
        P(),
        P(),
        P(),
        P(None, None, None, "strip"),
        P(None, None, None, "strip"),
        P(None, None, None, "strip"),
        P(None, None, None, "strip"),
        P(None, None, None, "strip"),
        P(None, None, None, "strip"),
        P(),
        P(),
        P(),
        P(),
        P(),
        P(),
        P(),
        P(),
        P(),
    )
    return jax.shard_map(shards, mesh=mesh, in_specs=in_specs, out_specs=out_specs, check_vma=False)
```

```python
import functools

import jax
import jax.numpy as jnp
from jax import lax
from jax.experimental import pallas as pl
from jax.experimental.pallas import tpu as pltpu
from jax.sharding import PartitionSpec as P

STEP = 5


EPS_NORM = 1e-05
SPREAD_TWICE = 8.0
SMALL_RATE = 0.25
CLIP_NORM = 0.01
FAR = 1e9


def edges(first, last):
    peers = lax.axis_size("strip")
    up = [(i, i + 1) for i in range(peers - 1)]
    before = lax.ppermute(last, "strip", up)
    after = lax.ppermute(first, "strip", [(j, i) for i, j in up])
    return before, after


def halo(shard):
    before, after = edges(shard[:1], shard[-1:])
    return [before, shard, after]


def with_edges(function, shards, borders):
    place = lax.axis_index("strip")
    inside = [place > 0, place < lax.axis_size("strip") - 1]
    sides = [
        jnp.where(there, function(*side), 0).astype(BF)
        for there, side in zip(inside, zip(*borders))
    ]
    return [sides[0], function(*shards), sides[1]]


def target_kernel(peaks_ref, count_ref, first_ref, gap_ref):
    gap_ref[...] = jnp.full(gap_ref.shape, FAR, jnp.float32)
    shape = gap_ref.shape[1:]
    row_ids = lax.broadcasted_iota(jnp.int32, shape, 0) + first_ref[0]
    col_ids = lax.broadcasted_iota(jnp.int32, shape, 1)

    def visit(slot, carry):
        row_gap = row_ids - peaks_ref[0, slot]
        col_gap = col_ids - peaks_ref[1, slot]
        distance = (row_gap * row_gap + col_gap * col_gap).astype(jnp.float32)
        kind = peaks_ref[2, slot]
        gap_ref[kind] = jnp.minimum(gap_ref[kind], distance)
        return carry

    lax.fori_loop(0, count_ref[0], visit, 0)


def nearest_gaps(box_peaks, box_count, first_row, row_total, col_total, classes):
    return pl.pallas_call(
        target_kernel,
        in_specs=[pl.BlockSpec(memory_space=pltpu.SMEM)] * 3,
        out_specs=pl.BlockSpec(memory_space=pltpu.VMEM),
        out_shape=jax.ShapeDtypeStruct((classes, row_total, col_total), jnp.float32),
        cost_estimate=pl.CostEstimate(flops=4000000, bytes_accessed=1000000, transcendentals=0),
        name="targets",
    )(box_peaks, box_count, first_row[None])


LANES = 128
SHORT = pl.CostEstimate(flops=1000, bytes_accessed=1000, transcendentals=0)
BF = jnp.bfloat16
F32 = jnp.float32


def plan(pixels, strips, strip_cells):
    per_strip = -(-strip_cells // LANES)
    high = strips * per_strip
    block = 352 if pixels % 352 == 0 and high <= 128 else 48
    return dict(
        per_strip=per_strip,
        high=high,
        offset=high // 2,
        block=block,
        stride=block + 4,
        group=block,
        strip_cells=strip_cells,
    )


def split_cells(index, plan):
    cell = index.astype(F32)
    strip = jnp.floor((cell + 0.5) * (1.0 / plan["strip_cells"]))
    rest = cell - strip * plan["strip_cells"]
    part = jnp.floor((rest + 0.5) * (1.0 / LANES))
    return strip * plan["per_strip"] + part - plan["offset"], rest - part * LANES


def softmax_lanes(logits, bins):
    lane = lax.broadcasted_iota(jnp.int32, logits.shape, 1)
    logits = jnp.where(lane < bins, logits, -jnp.inf)
    powers = jnp.exp(logits - jnp.max(logits, axis=1, keepdims=True))
    return powers / jnp.sum(powers, axis=1, keepdims=True)


def spread(ref, pixel, rows=16):
    return jnp.broadcast_to(ref[pl.ds(pixel, 1), :], (rows, LANES))


def one_hot(row, value, rows, offset=0):
    base = (lax.broadcasted_iota(jnp.int32, (rows, LANES), 0) - offset).astype(F32).astype(BF)
    none = jnp.zeros((16, LANES), BF)
    return [
        jnp.where(base[k : k + 16] == row, value, none) for k in range(0, rows, 16)
    ]


def high_pair(high_ref, depth_ref, first, plan):
    whole = plan["high"] // 16 * 16
    parts = []
    for j in range(2):
        row = spread(high_ref, first + j).astype(BF)
        value = spread(depth_ref, first + j).astype(BF)
        parts += one_hot(row, value, whole, plan["offset"])
    if whole < plan["high"]:
        both = [
            jnp.concatenate([spread(ref, first, 8), spread(ref, first + 1, 8)], 0).astype(BF)
            for ref in (high_ref, depth_ref)
        ]
        base = lax.broadcasted_iota(jnp.int32, (16, LANES), 0)
        base = jnp.where(base < 8, base, base - 8) + (whole - plan["offset"])
        none = jnp.zeros((16, LANES), BF)
        parts.append(jnp.where(base.astype(F32).astype(BF) == both[0], both[1], none))
    return jnp.concatenate(parts, 0)


def pool_kernel(place_ref, feat_ref, index_ref, weight_ref, own_ref, other_ref, dense_ref, both_ref, high_ref, low_ref, depth_ref, held, total, *, plan):
    bins = index_ref.shape[1]
    block, stride, high = (plan[k] for k in ("block", "stride", "high"))
    step = pl.program_id(0)

    @pl.when(step == 0)
    def _():
        high_ref[...] = jnp.zeros_like(high_ref)
        low_ref[...] = jnp.zeros_like(low_ref)
        total[...] = jnp.zeros_like(total)
        channels = total.shape[1]
        both_ref[...] = jnp.zeros_like(both_ref)
        both_ref[:bins] = weight_ref[:bins].astype(BF)
        both_ref[LANES : LANES + channels] = weight_ref[bins : bins + channels].astype(BF)

    feat = feat_ref[...]
    logits = lax.dot_general(feat, both_ref[:LANES], (((1,), (1,)), ((), ())), preferred_element_type=F32)
    depth_ref[...] = softmax_lanes(logits, bins)
    channels = total.shape[1]
    context_low = both_ref[LANES : LANES + channels]
    context = lax.dot_general(context_low, feat, (((1,), (1,)), ((), ())), preferred_element_type=F32).astype(BF)
    high_id, low_id = split_cells(index_ref[...], plan)
    high_ref[:, :bins] = high_id
    low_ref[:, :bins] = low_id
    one = jnp.ones((16, LANES), BF)

    def scatter(group, carry):
        for k in range(0, plan["group"], 2):
            first = group * plan["group"] + k
            left = high_pair(high_ref, depth_ref, first, plan)
            right = []
            for j in range(2):
                low = spread(low_ref, first + j).astype(BF)
                right.append(jnp.concatenate(one_hot(low, one, LANES), 0))
            tile = lax.dot_general(
                left, jnp.concatenate(right, 0), (((1,), (1,)), ((), ())), preferred_element_type=F32
            )
            whole = high // 16 * 16
            for j in range(2):
                part = tile[:, j * LANES : (j + 1) * LANES]
                held[pl.ds(first + j, whole, stride=stride), :] = part[j * whole : (j + 1) * whole]
                if whole < high:
                    held[pl.ds(first + j + whole * stride, 8, stride=stride), :] = part[
                        2 * whole + 8 * j : 2 * whole + 8 * j + 8
                    ]
        return carry

    lax.fori_loop(0, block // plan["group"], scatter, 0)

    def gather(k, carry):
        parts = []
        for j in range(2):
            part = held[pl.ds((k * 2 + j) * stride, block), :].astype(BF)
            dense_ref[k * 2 + j] = part
            parts.append(part)
        out = jnp.dot(context, jnp.concatenate(parts, 1), preferred_element_type=F32)
        for j in range(2):
            total[k * 2 + j] += out[:, j * LANES : (j + 1) * LANES]
        return carry

    lax.fori_loop(0, high // 2, gather, 0, unroll=36)

    @pl.when(step == pl.num_programs(0) - 1)
    def _():
        count = plan["per_strip"]
        chips = own_ref.shape[0]
        for shift in range(chips):
            chip = lax.rem(place_ref[0] + shift, chips)
            for ref, core in ((own_ref, place_ref[1]), (other_ref, 1 - place_ref[1])):
                first = (2 * chip + core) * count
                ref[shift] = total[pl.ds(first, count)].astype(BF)


def pool(place, features, index, weight, plan):
    pixels, width = features.shape
    bins = index.shape[1]
    channels = weight.shape[0] - bins
    block, high = plan["block"], plan["high"]
    halves = (high // plan["per_strip"] // 2, plan["per_strip"], channels, LANES)
    return pl.pallas_call(
        functools.partial(pool_kernel, plan=plan),
        grid=(pixels // block,),
        in_specs=[
            pl.BlockSpec(memory_space=pltpu.SMEM),
            pl.BlockSpec((block, width), lambda i: (i, 0)),
            pl.BlockSpec((block, bins), lambda i: (i, 0)),
            pl.BlockSpec(weight.shape, lambda i: (0, 0)),
        ],
        out_specs=[
            pl.BlockSpec(halves, lambda i: (0, 0, 0, 0)),
            pl.BlockSpec(halves, lambda i: (0, 0, 0, 0)),
            pl.BlockSpec((high, block, LANES), lambda i: (0, i, 0)),
            pl.BlockSpec((2 * LANES, width), lambda i: (0, 0)),
        ],
        out_shape=[
            jax.ShapeDtypeStruct(halves, BF),
            jax.ShapeDtypeStruct(halves, BF),
            jax.ShapeDtypeStruct((high, pixels, LANES), BF),
            jax.ShapeDtypeStruct((2 * LANES, width), BF),
        ],
        scratch_shapes=[pltpu.VMEM((block, LANES), F32)] * 3
        + [
            pltpu.VMEM((high * plan["stride"], LANES), F32),
            pltpu.VMEM((high, channels, LANES), F32),
        ],
        compiler_params=pltpu.CompilerParams(vmem_limit_bytes=40 << 20),
        cost_estimate=pl.CostEstimate(
            flops=4 * pixels * high * LANES * LANES,
            bytes_accessed=2 * pixels * high * LANES,
            transcendentals=0,
        ),
        name="pool",
    )(place, features, index, weight)


def unpool_kernel(place_ref, feat_ref, index_ref, both_ref, dense_ref, mine_ref, theirs_ref, head_ref, out_ref, high_ref, low_ref, pick_ref, held, sum_ref, grid_ref, grad_ref, *, plan):
    bins = index_ref.shape[1]
    channels = grid_ref.shape[1]
    chips, count = mine_ref.shape[:2]
    block, stride, high = (plan[k] for k in ("block", "stride", "high"))
    step = pl.program_id(0)

    @pl.when(step == 0)
    def _():
        high_ref[...] = jnp.zeros_like(high_ref)
        low_ref[...] = jnp.zeros_like(low_ref)
        held[...] = jnp.zeros_like(held)
        grad_ref[...] = jnp.zeros_like(grad_ref)
        for shift in range(chips):
            chip = lax.rem(place_ref[0] + (chips - shift), chips)
            for ref, core in ((mine_ref, place_ref[1]), (theirs_ref, 1 - place_ref[1])):
                grid_ref[pl.ds((2 * chip + core) * count, count)] = ref[shift]

    feat = feat_ref[...]
    logits = lax.dot_general(feat, both_ref[...], (((1,), (1,)), ((), ())), preferred_element_type=F32)
    depth = softmax_lanes(logits[:, :LANES], bins)
    context = logits[:, LANES : LANES + channels].astype(BF)
    high_id, low_id = split_cells(index_ref[...], plan)
    high_ref[:, :bins] = high_id
    low_ref[:, :bins] = low_id

    def project(k, carry):
        grid = jnp.concatenate([grid_ref[k * 2], grid_ref[k * 2 + 1]], 1)
        out = jnp.dot(context, grid, preferred_element_type=F32)
        for j in range(2):
            held[pl.ds((k * 2 + j) * stride, block), :] = out[:, j * LANES : (j + 1) * LANES]
        return carry

    lax.fori_loop(0, high // 2, project, 0, unroll=36)
    parts = 72

    def mix(k, carry):
        dense = jnp.concatenate([dense_ref[k * parts + j] for j in range(parts)], 1)
        grid = jnp.concatenate([grid_ref[k * parts + j] for j in range(parts)], 1)
        sum_ref[...] += lax.dot_general(
            dense, grid, (((1,), (1,)), ((), ())), preferred_element_type=F32
        )
        return carry

    sum_ref[...] = jnp.zeros_like(sum_ref)
    lax.fori_loop(0, high // parts, mix, 0)
    one = jnp.ones((16, LANES), BF)
    rows = (lax.broadcasted_iota(jnp.int32, (high, LANES), 0) - plan["offset"]).astype(F32)

    def collect(group, carry):
        for k in range(0, plan["group"], 2):
            first = group * plan["group"] + k
            left, right = [], []
            for j in range(2):
                left.append(held[pl.ds(first + j, high, stride=stride), :])
                low = spread(low_ref, first + j).astype(BF)
                right.append(jnp.concatenate(one_hot(low, one, LANES), 0))
            tile = jnp.dot(jnp.concatenate(left, 0).astype(BF), jnp.concatenate(right, 1), preferred_element_type=F32)
            for j in range(2):
                part = tile[j * high : (j + 1) * high, j * LANES : (j + 1) * LANES]
                kept = jnp.where(rows == high_ref[pl.ds(first + j, 1), :], part, 0.0)
                pick_ref[pl.ds(first + j, 1), :] = jnp.sum(kept, axis=0, keepdims=True)
        return carry

    lax.fori_loop(0, block // plan["group"], collect, 0)
    grad_prob = pick_ref[...]
    grad_context = sum_ref[...]
    grad_depth = depth * (grad_prob - jnp.sum(grad_prob * depth, axis=1, keepdims=True))
    grad_low = jnp.concatenate(
        [grad_depth, grad_context, jnp.zeros((block, LANES - channels), F32)], axis=1
    ).astype(BF)
    grad_ref[...] += lax.dot_general(grad_low, feat, (((0,), (0,)), ((), ())), preferred_element_type=F32)

    @pl.when(step == pl.num_programs(0) - 1)
    def _():
        first = LANES + channels
        rows = head_ref.shape[0]
        out_ref[:first] = grad_ref[:first].astype(BF)
        spare = jnp.zeros((2 * LANES - first - rows, grad_ref.shape[1]), F32)
        out_ref[first:] = jnp.concatenate([head_ref[...], spare], 0).astype(BF)


def unpool(place, features, index, both_low, dense, mine, theirs, head, plan):
    pixels, width = features.shape
    bins = index.shape[1]
    channels = mine.shape[2]
    block, high = plan["block"], plan["high"]
    return pl.pallas_call(
        functools.partial(unpool_kernel, plan=plan),
        grid=(pixels // block,),
        in_specs=[
            pl.BlockSpec(memory_space=pltpu.SMEM),
            pl.BlockSpec((block, width), lambda i: (i, 0)),
            pl.BlockSpec((block, bins), lambda i: (i, 0)),
            pl.BlockSpec(both_low.shape, lambda i: (0, 0)),
            pl.BlockSpec((high, block, LANES), lambda i: (0, i, 0)),
            pl.BlockSpec(mine.shape, lambda i: (0, 0, 0, 0)),
            pl.BlockSpec(theirs.shape, lambda i: (0, 0, 0, 0)),
            pl.BlockSpec(head.shape, lambda i: (0, 0)),
        ],
        out_specs=pl.BlockSpec((2 * LANES, width), lambda i: (0, 0)),
        out_shape=jax.ShapeDtypeStruct((2 * LANES, width), BF),
        scratch_shapes=[pltpu.VMEM((block, LANES), F32)] * 3
        + [
            pltpu.VMEM((high * plan["stride"], LANES), F32),
            pltpu.VMEM((block, channels), F32),
            pltpu.VMEM((high, channels, LANES), BF),
            pltpu.VMEM((2 * LANES, width), F32),
        ],
        compiler_params=pltpu.CompilerParams(vmem_limit_bytes=40 << 20),
        cost_estimate=pl.CostEstimate(
            flops=6 * pixels * high * LANES * LANES,
            bytes_accessed=2 * pixels * high * LANES,
            transcendentals=0,
        ),
        name="unpool",
    )(place, features, index, both_low, dense, mine, theirs, head)


def fill_windows(window_ref, part, cols, span):
    before_ref, shard_ref, after_ref = part
    rows = shard_ref.shape[0]
    width = window_ref.shape[2]
    window_ref[...] = jnp.zeros_like(window_ref)
    for row in range(rows + 2):
        if row == 0:
            line = before_ref[0]
        elif row == rows + 1:
            line = after_ref[0]
        else:
            line = shard_ref[row - 1]
        line = line[:, :width]
        start = row * span
        window_ref[0, start + 1 : start + cols] = line[: cols - 1]
        window_ref[1, start : start + cols] = line
        window_ref[2, start : start + cols - 1] = line[1:]


def window_scratch(part, width, span):
    return pltpu.VMEM((3, (part[1].shape[0] + 2) * span, width), BF)


def span_of(cols):
    return -(-cols // 16) * 16


def conv_kernel(*refs, count, turned, finish):
    kernels = refs[:count]
    parts = [refs[count + 3 * k : count + 3 * k + 3] for k in range(count)]
    rows, cols = parts[0][1].shape[:2]
    span = span_of(cols)
    windows = refs[-count:]
    left, right = [], []
    for part, window_ref, kernel_ref in zip(parts, windows, kernels):
        fill_windows(window_ref, part, cols, span)
        for tap in range(9):
            upward, across = tap // 3, tap % 3
            left.append(window_ref[across, upward * span : (upward + rows) * span])
            right.append(kernel_ref[8 - tap if turned else tap])
    left = jnp.concatenate(left, 1)
    if turned:
        total = jnp.dot(left, jnp.concatenate(right, 0), preferred_element_type=F32)
    else:
        total = lax.dot_general(
            left, jnp.concatenate(right, 1), (((1,), (1,)), ((), ())), preferred_element_type=F32
        )
    finish(total, rows, cols, span, *refs[4 * count : -count])


def keep_rows(total, rows, cols, span, out_ref):
    for row in range(rows):
        out_ref[row] = total[row * span : row * span + cols]


def keep_moments(total, rows, cols, span, *refs):
    out_ref, stats_ref = refs[-2:]
    keep_rows(total, rows, cols, span, out_ref)
    cells = float(rows * cols)
    center = jnp.sum(total, axis=0, keepdims=True) / cells
    spot = lax.broadcasted_iota(jnp.int32, (span, total.shape[1]), 0)
    spread_sum = jnp.zeros_like(center)
    for row in range(rows):
        apart = total[row * span : (row + 1) * span] - center
        apart = jnp.where(spot < cols, apart, 0.0)
        spread_sum = spread_sum + jnp.sum(apart * apart, axis=0, keepdims=True)
    hits = jnp.zeros_like(center)
    for ref in refs[:-2]:
        hits = jnp.full(center.shape, jnp.sum(jnp.where(ref[...] == 0.0, 1.0, 0.0)))
    stats = jnp.concatenate([center, spread_sum, hits], 0)

    def store(device, carry):
        stats_ref[device] = stats
        return carry

    lax.fori_loop(0, stats_ref.shape[0], store, 0)


def keep_grad(total, rows, cols, span, more_ref, norm_in_ref, vector_ref, out_ref, first_ref, last_ref, sums_ref):
    center, scale, gain, shift = (vector_ref[k : k + 1] for k in range(4))
    shift_sum = jnp.zeros_like(center)
    gain_sum = jnp.zeros_like(center)
    for row in range(rows):
        normed = (norm_in_ref[row] - center) * scale
        value = normed * gain + shift
        sig = jax.nn.sigmoid(value)
        grad = total[row * span : row * span + cols] + more_ref[row]
        grad = grad * (sig * (1.0 + value * (1.0 - sig)))
        out_ref[row] = grad
        if row == 0:
            first_ref[0] = grad
        if row == rows - 1:
            last_ref[0] = grad
        shift_sum = shift_sum + jnp.sum(grad, axis=0, keepdims=True)
        gain_sum = gain_sum + jnp.sum(grad * normed, axis=0, keepdims=True)
    sums = jnp.concatenate([shift_sum, gain_sum], 0)

    def store(device, carry):
        sums_ref[device] = sums
        return carry

    lax.fori_loop(0, sums_ref.shape[0], store, 0)


def head_kernel(vector_ref, res_ref, act_ref, head_ref, bias_ref, gap_ref, count_ref, grad_ref, sums_ref, loss_ref, head_grad_ref):
    rows, cols, width = res_ref.shape
    center, scale, gain, shift = (vector_ref[k : k + 1] for k in range(4))
    head = head_ref[...]
    shift_sum = jnp.zeros_like(center)
    gain_sum = jnp.zeros_like(center)
    head_grad = jnp.zeros(head.shape, F32)
    bias_grad = jnp.zeros((head.shape[0], 1), F32)
    loss = jnp.zeros((head.shape[0], 1), F32)
    for row in range(rows):
        normed = (res_ref[row] - center) * scale
        summed = normed * gain + shift + act_ref[row].astype(F32)
        sig = jax.nn.sigmoid(summed)
        hidden = (summed * sig).astype(BF)
        logits = lax.dot_general(head, hidden, (((1,), (1,)), ((), ())), preferred_element_type=F32)
        logits = logits + bias_ref[...]
        prob = jax.nn.sigmoid(logits)
        tail = jnp.log1p(jnp.exp(-jnp.abs(logits)))
        soft_pos = jnp.maximum(logits, 0.0) + tail
        soft_neg = jnp.maximum(-logits, 0.0) + tail
        gap = gap_ref[:, row, :]
        heatmap = jnp.where(gap < FAR, jnp.exp(-gap / SPREAD_TWICE), 0.0)
        struck = jnp.where(gap == 0.0, 1.0, 0.0)
        weighting = (1.0 - heatmap) * (1.0 - heatmap)
        weighting = weighting * weighting
        miss = 1.0 - prob
        loss_here = struck * miss * miss * soft_neg + weighting * prob * prob * soft_pos
        loss = loss + jnp.sum(loss_here, axis=1, keepdims=True)
        grad_pos = -2.0 * prob * miss * miss * soft_neg - miss * miss * miss
        grad_neg = 2.0 * prob * prob * miss * soft_pos + prob * prob * prob
        grad_logits = (struck * grad_pos + weighting * grad_neg) / count_ref[...]
        grad_logits = grad_logits.astype(BF)
        bias_grad = bias_grad + jnp.sum(grad_logits.astype(F32), axis=1, keepdims=True)
        head_grad = head_grad + jnp.dot(grad_logits, hidden, preferred_element_type=F32)
        grad = lax.dot_general(grad_logits, head, (((0,), (0,)), ((), ())), preferred_element_type=F32)
        grad = grad * (sig * (1.0 + summed * (1.0 - sig)))
        grad_ref[row] = grad
        shift_sum = shift_sum + jnp.sum(grad, axis=0, keepdims=True)
        gain_sum = gain_sum + jnp.sum(grad * normed, axis=0, keepdims=True)
    loss_ref[...] = jnp.sum(loss, axis=0, keepdims=True)
    classes = head.shape[0]
    head_grad_ref[:classes] = head_grad
    down = lax.broadcasted_iota(jnp.int32, head.shape, 0)
    across = lax.broadcasted_iota(jnp.int32, head.shape, 1)
    bias_row = jnp.sum(jnp.where(down == across, bias_grad, 0.0), axis=0, keepdims=True)
    head_grad_ref[classes : classes + 1] = bias_row
    sums = jnp.concatenate([shift_sum, gain_sum], 0)

    def store(device, carry):
        sums_ref[device] = sums
        return carry

    lax.fori_loop(0, sums_ref.shape[0], store, 0)


def run_head(vectors, res_out, act, head_low, bias, gaps, positives, devices):
    rows, cols, width = res_out.shape
    classes = head_low.shape[0]
    shapes = [
        (rows, cols, width),
        (devices, 2, width),
        (1, 1),
        (classes + 1, width),
    ]
    return pl.pallas_call(
        head_kernel,
        in_specs=[pl.BlockSpec(memory_space=pltpu.VMEM)] * 7,
        out_specs=[pl.BlockSpec(memory_space=pltpu.VMEM)] * 4,
        out_shape=[jax.ShapeDtypeStruct(shape, F32) for shape in shapes],
        compiler_params=pltpu.CompilerParams(vmem_limit_bytes=24 << 20),
        name="head",
    )(vectors, res_out, act, head_low, bias, gaps, positives)


def keep_cells(total, rows, cols, span, out_ref):
    cells, channels = out_ref.shape[0] * LANES, out_ref.shape[1]
    flat = [total[row * span : row * span + cols] for row in range(rows)]
    flat.append(jnp.zeros((cells - rows * cols, total.shape[1]), F32))
    flat = jnp.concatenate(flat, 0)
    for part in range(out_ref.shape[0]):
        out_ref[part] = flat[part * LANES : (part + 1) * LANES].T[:channels].astype(BF)


def convolve(parts, kernels, turned, finish, outs, extras=()):
    rows, cols = parts[0][1].shape[:2]
    span = span_of(cols)
    widths = [kernel.shape[1] if turned else kernel.shape[2] for kernel in kernels]
    flat = [array for part in parts for array in part]
    operands = [*kernels, *flat, *extras]
    return pl.pallas_call(
        functools.partial(conv_kernel, count=len(parts), turned=turned, finish=finish),
        in_specs=[pl.BlockSpec(memory_space=pltpu.VMEM)] * len(operands),
        out_specs=[pl.BlockSpec(memory_space=pltpu.VMEM)] * len(outs),
        out_shape=outs,
        scratch_shapes=[
            window_scratch(part, width, span) for part, width in zip(parts, widths)
        ],
        compiler_params=pltpu.CompilerParams(vmem_limit_bytes=32 << 20),
        cost_estimate=pl.CostEstimate(
            flops=18 * rows * span * sum(widths) * kernels[0].shape[1],
            bytes_accessed=2 * sum(kernel.size for kernel in kernels),
            transcendentals=0,
        ),
        name="convolve",
    )(*operands)


def taps_kernel(place_ref, grad_ref, *refs, widths):
    count = len(widths)
    parts = [refs[3 * k : 3 * k + 3] for k in range(count)]
    own_ref, other_ref = refs[3 * count : 3 * count + 2]
    windows = refs[3 * count + 2 : 4 * count + 2]
    flipped_grad, total = refs[4 * count + 2 :]
    rows, cols, depth = grad_ref.shape
    owned = own_ref.shape[2]
    chips = own_ref.shape[0]
    span = span_of(cols)
    for part, window_ref in zip(parts, windows):
        fill_windows(window_ref, part, cols, span)
    flat = []
    for row in range(rows):
        flat += [grad_ref[row], jnp.zeros((span - cols, depth), BF)]
    flipped_grad[...] = jnp.concatenate(flat, 0).T

    def visit(tap, carry):
        start = pl.multiple_of((tap // 3) * span, 16)
        across = lax.rem(tap, 3)
        first = 0
        for window_ref in windows:
            window = window_ref[across, pl.ds(start, rows * span)]
            total[:, first : first + window.shape[1]] = jnp.dot(
                flipped_grad[...], window, preferred_element_type=F32
            )
            first += window.shape[1]
        for shift in range(chips):
            chip = lax.rem(place_ref[0] + shift, chips)
            for ref, core in ((own_ref, place_ref[1]), (other_ref, 1 - place_ref[1])):
                half = pl.multiple_of((2 * chip + core) * owned, 8)
                ref[shift, tap] = total[pl.ds(half, owned)].astype(BF)
        return carry

    lax.fori_loop(0, 9, visit, 0)


def taps(place, parts, widths, grad, chips):
    rows, cols, depth = grad.shape
    channels = sum(widths)
    span = span_of(cols)
    flat = [array for part in parts for array in part]
    half = jax.ShapeDtypeStruct((chips, 9, depth // chips // 2, channels), BF)
    return pl.pallas_call(
        functools.partial(taps_kernel, widths=widths),
        in_specs=[pl.BlockSpec(memory_space=pltpu.SMEM)]
        + [pl.BlockSpec(memory_space=pltpu.VMEM)] * (1 + len(flat)),
        out_specs=[pl.BlockSpec(memory_space=pltpu.VMEM)] * 2,
        out_shape=[half, half],
        scratch_shapes=[window_scratch(part, width, span) for part, width in zip(parts, widths)]
        + [pltpu.VMEM((depth, rows * span), BF), pltpu.VMEM((depth, channels), F32)],
        compiler_params=pltpu.CompilerParams(vmem_limit_bytes=28 << 20),
        cost_estimate=SHORT,
        name="taps",
    )(place, grad, *flat)


def settle_kernel(*refs):
    out_ref = refs[-1]
    rows, cols = out_ref.shape[:2]
    total = refs[0][...].astype(F32)
    for ref in refs[1:-1]:
        total = total + ref[...].astype(F32)
    parts = total.shape[0]
    flat = jnp.concatenate([total[part].T for part in range(parts)], 0)
    spare = jnp.zeros((cols, out_ref.shape[2] - flat.shape[1]), F32)
    for row in range(rows):
        line = flat[row * cols : (row + 1) * cols]
        out_ref[row] = jnp.concatenate([line, spare], 1).astype(BF)


def settle(parts, rows, cols):
    return pl.pallas_call(
        settle_kernel,
        in_specs=[pl.BlockSpec(memory_space=pltpu.VMEM)] * len(parts),
        out_specs=pl.BlockSpec(memory_space=pltpu.VMEM),
        out_shape=jax.ShapeDtypeStruct((rows, cols, LANES), BF),
        compiler_params=pltpu.CompilerParams(vmem_limit_bytes=32 << 20),
        name="settle",
    )(*parts)


def split_bits(value):
    pieces = []
    for _ in range(3):
        piece = value.astype(BF).astype(F32)
        pieces.append(piece)
        value = value - piece
    return pieces


def join_kernel(place_ref, mixed_ref, loss_ref, *refs, hidden_width):
    parts = refs[:-2]
    total_ref, out_ref = refs[-2:]
    count = len(parts)
    place = place_ref[2]
    taps_total, owned, width = total_ref.shape

    def visit(tap, sums):
        values = [part[tap].astype(F32) for part in parts]
        total = None
        for member in range(count):
            part = values[-member % count]
            for here in range(1, count):
                part = jnp.where(place == here, values[(here - member) % count], part)
            total = part if total is None else total + part
        total_ref[tap] = total
        square = total * total
        res, join = sums
        res = res + jnp.sum(square[:, :hidden_width], axis=0, keepdims=True)
        join = join + jnp.sum(square[:, hidden_width:], axis=0, keepdims=True)
        return res, join

    zeros = (
        jnp.zeros((1, hidden_width), F32),
        jnp.zeros((1, width - hidden_width), F32),
    )
    res, join = lax.fori_loop(0, taps_total, visit, zeros)
    shares = float(count)
    scalars = [
        jnp.sum(join, axis=1, keepdims=True) / shares,
        jnp.sum(res, axis=1, keepdims=True) / shares,
        loss_ref[...],
    ]
    mixed = jnp.sum(mixed_ref[...].astype(F32), axis=0)
    shape = (mixed.shape[0], LANES)
    lane = lax.broadcasted_iota(jnp.int32, shape, 1)
    row = jnp.zeros(shape, F32)
    for k, scalar in enumerate(scalars):
        for j, piece in enumerate(split_bits(scalar)):
            row = jnp.where(lane == 3 * k + j, piece, row)
    block = jnp.concatenate([mixed, row], 1).astype(BF)

    def store(device, carry):
        out_ref[device] = block
        return carry

    lax.fori_loop(0, out_ref.shape[0], store, 0)


def join_shares(place, mixed, loss, parts, hidden_width):
    devices, rows, width = mixed.shape
    return pl.pallas_call(
        functools.partial(join_kernel, hidden_width=hidden_width),
        in_specs=[pl.BlockSpec(memory_space=pltpu.SMEM)]
        + [pl.BlockSpec(memory_space=pltpu.VMEM)] * (2 + len(parts)),
        out_specs=[pl.BlockSpec(memory_space=pltpu.VMEM)] * 2,
        out_shape=[
            jax.ShapeDtypeStruct(parts[0].shape, F32),
            jax.ShapeDtypeStruct((devices, rows, width + LANES), BF),
        ],
        compiler_params=pltpu.CompilerParams(vmem_limit_bytes=32 << 20),
        name="join_shares",
    )(place, mixed, loss.reshape(1, 1), *parts)


def update_kernel(shared_ref, taps_ref, norm_ref, count_ref, *refs, shapes, rates):
    states, outputs = refs[:18], refs[18:38]
    mixed_ref, load_sem, store_sem = refs[38:41]
    held = refs[41:]
    loads = [
        pltpu.make_async_copy(state, buffer, load_sem.at[k])
        for k, (state, buffer) in enumerate(zip(states, held))
    ]
    for load in loads:
        load.start()
    share, width = shared_ref.shape[1], mixed_ref.shape[1]
    for device in range(shared_ref.shape[0]):
        mixed_ref[device * share : (device + 1) * share] = shared_ref[device, :, :width].astype(F32)
    depth_bins, cam_width, classes, hidden_width = shapes
    mixed = mixed_ref[...]
    column = LANES + cam_width
    edge = taps_ref.shape[2] - cam_width
    grads = [
        jnp.concatenate([mixed[:depth_bins], mixed[LANES:column]], 0),
        jnp.concatenate([taps_ref[:, :, edge:], taps_ref[:, :, hidden_width:edge]], 2),
        taps_ref[:, :, :hidden_width],
        mixed[column : column + classes],
        norm_ref[...],
        mixed[column + classes : column + classes + 1, :classes],
    ]
    sums = jnp.sum(shared_ref[:, :1, width:].astype(F32), axis=0)
    lane = lax.broadcasted_iota(jnp.int32, sums.shape, 1)
    squared = [None if k in (1, 2) else jnp.sum(grad * grad) for k, grad in enumerate(grads)]
    squared[1] = jnp.sum(jnp.where(lane < 3, sums, 0.0))
    squared[2] = jnp.sum(jnp.where((lane >= 3) & (lane < 6), sums, 0.0))
    loss_sum = jnp.sum(jnp.where((lane >= 6) & (lane < 9), sums, 0.0), axis=1, keepdims=True)
    loss_ref, norms_ref = outputs[:2]
    loss_ref[...] = loss_sum / count_ref[...]
    stores = [
        pltpu.make_async_copy(buffer, output, store_sem.at[k])
        for k, (buffer, output) in enumerate(zip(held, outputs[2:]))
    ]
    norms = jnp.zeros((1, LANES), F32)
    spot = lax.broadcasted_iota(jnp.int32, norms.shape, 1)
    for k, grad in enumerate(grads):
        size = jnp.sqrt(jnp.full((1, LANES), squared[k], F32))
        norms = jnp.where(spot == k, jnp.log(size), norms)
        factor = CLIP_NORM / jnp.maximum(size, CLIP_NORM)
        factor = jnp.max(factor)
        group = range(3 * k, 3 * k + 3)
        for j in group:
            loads[j].wait()
        weight, first, second = (held[j][...] for j in group)
        results = adamw(weight, grad * factor, first, second, rates[k], STEP)
        for j, result in zip(group, results):
            held[j][...] = result
            stores[j].start()
    norms_ref[...] = norms
    for store in stores:
        store.wait()


def update(shared, taps_sum, norm, positives, states, shapes, rates):
    args = [shared, taps_sum, norm, positives.reshape(1, 1)] + states
    width = norm.shape[1]
    return pl.pallas_call(
        functools.partial(update_kernel, shapes=shapes, rates=rates),
        in_specs=[pl.BlockSpec(memory_space=pltpu.VMEM)] * 4
        + [pl.BlockSpec(memory_space=pl.ANY)] * 18,
        out_specs=[pl.BlockSpec(memory_space=pltpu.VMEM)] * 2
        + [pl.BlockSpec(memory_space=pl.ANY)] * 18,
        out_shape=[jax.ShapeDtypeStruct((1, 1), F32), jax.ShapeDtypeStruct((1, LANES), F32)]
        + [jax.ShapeDtypeStruct(state.shape, F32) for state in states],
        scratch_shapes=[
            pltpu.VMEM((2 * LANES, width), F32),
            pltpu.SemaphoreType.DMA((18,)),
            pltpu.SemaphoreType.DMA((18,)),
        ]
        + [pltpu.VMEM(state.shape, F32) for state in states],
        compiler_params=pltpu.CompilerParams(vmem_limit_bytes=60 << 20),
        name="update",
    )(*args)


def swapped(tensor):
    strips = lax.axis_size("strip")
    return lax.ppermute(tensor, "strip", [(i, i ^ 1) for i in range(strips)])


def halves_summed(own, other):
    return own.astype(F32) + swapped(other).astype(F32)


def moved(tensor, shift):
    strips = lax.axis_size("strip")
    return lax.ppermute(tensor, "strip", [(i, (i + 2 * shift) % strips) for i in range(strips)])


def far_first(chips):
    return sorted(range(1, chips), key=lambda shift: -min(shift, chips - shift))


def along_chips(tensor):
    chips = tensor.shape[0]
    arrived = {shift: moved(tensor[shift], shift) for shift in far_first(chips)}
    return [tensor[0]] + [arrived[shift] for shift in range(1, chips)]


def total_of(parts):
    total = parts[0].astype(F32)
    for part in parts[1:]:
        total = total + part.astype(F32)
    return total


def from_chips(tensor):
    chips = lax.axis_size("strip") // 2
    arrived = {shift: moved(tensor, shift) for shift in far_first(chips)}
    return [tensor] + [arrived[shift] for shift in range(1, chips)]


def arrange_kernel(place_ref, mine_ref, theirs_ref, *outs):
    chips, taps_total, owned = mine_ref.shape[:3]
    for chip in range(chips):
        shift = lax.rem(place_ref[0] + (chips - chip), chips)
        for core in range(2):
            start = (2 * chip + core) * owned

            def copy(ref):
                first = 0
                for out_ref in outs:
                    width = out_ref.shape[2]
                    for tap in range(taps_total):
                        out_ref[tap, start : start + owned] = ref[
                            shift, tap, :, first : first + width
                        ]
                    first += width

            pl.when(place_ref[1] == core)(functools.partial(copy, mine_ref))
            pl.when(place_ref[1] != core)(functools.partial(copy, theirs_ref))


def arrange(place, mine, theirs, widths):
    chips, taps_total, owned = mine.shape[:3]
    return pl.pallas_call(
        arrange_kernel,
        in_specs=[pl.BlockSpec(memory_space=pltpu.SMEM)]
        + [pl.BlockSpec(memory_space=pltpu.VMEM)] * 2,
        out_specs=[pl.BlockSpec(memory_space=pltpu.VMEM)] * len(widths),
        out_shape=[
            jax.ShapeDtypeStruct((taps_total, 2 * chips * owned, width), BF) for width in widths
        ],
        compiler_params=pltpu.CompilerParams(vmem_limit_bytes=32 << 20),
        cost_estimate=pl.CostEstimate(
            flops=0, bytes_accessed=8 * mine.size, transcendentals=0
        ),
        name="arrange",
    )(place, mine, theirs)


def moments(stats, cells, border):
    shared = lax.all_to_all(stats, ("batch", "strip"), 0, 0)
    if border:
        shared, border = lax.optimization_barrier((shared, border))
    centers = shared[:, 0]
    total = jnp.mean(centers, axis=0)
    spread_mean = jnp.mean(shared[:, 1] / cells + (centers - total) ** 2, axis=0)
    return (total, lax.rsqrt(spread_mean + EPS_NORM), jnp.sum(shared[:, 2, 0]), border)


def grad_sums(sums, first, last, later, meanwhile):
    border = edges(first, last)
    shared = lax.all_to_all(sums, ("batch", "strip"), 0, 0)
    later = meanwhile(*later)
    shared, border, later = lax.optimization_barrier((shared, border, later))
    grad_shift, grad_gain = jnp.sum(shared, axis=0)
    return (grad_gain, grad_shift, border, later)


def over_batch(tensor):
    count = lax.axis_size("batch")
    shifts = [[(i, (i + s) % count) for i in range(count)] for s in range(1, count)]
    return [tensor] + [lax.ppermute(tensor, "batch", pairs) for pairs in shifts]


def adamw(weight, gradient, first, second, rate, step_value):
    first = 0.9 * first + 0.1 * gradient
    second = 0.999 * second + 0.001 * gradient * gradient
    fix_one = 1.0 - 0.9**step_value
    fix_two = 1.0 - 0.999**step_value
    update = first / fix_one / (jnp.sqrt(second / fix_two) + 1e-08) + 0.01 * weight
    return (weight - rate * update, first, second)


def shards(
    camera_features,
    lidar_bev,
    pool_index,
    box_peaks,
    box_count,
    w_depth,
    m_depth,
    v_depth,
    w_join,
    m_join,
    v_join,
    w_res,
    m_res,
    v_res,
    w_head,
    m_head,
    v_head,
    norm_params,
    m_norm,
    v_norm,
    head_bias,
    m_bias,
    v_bias,
):
    samples, row_local, col_total, lidar_width = lidar_bev.shape
    strips = lax.axis_size("strip")
    row_total = row_local * strips
    cell_total = float(samples * lax.axis_size("batch") * row_total * col_total)
    depth_bins = pool_index.shape[2]
    classes = w_head.shape[1]
    owned = w_join.shape[3]
    cam_width = w_depth.shape[1] - depth_bins
    first_row = lax.axis_index("strip") * row_local
    place = lax.axis_index("strip")
    place = jnp.stack([place // 2, place % 2, lax.axis_index("batch")]).astype(jnp.int32)
    hidden_width = w_res.shape[2]
    taps_low = jnp.concatenate(
        [
            jnp.swapaxes(part, 2, 3).reshape(9, owned, -1)
            for part in (w_res, w_join[:, :, cam_width:], w_join[:, :, :cam_width])
        ],
        axis=2,
    ).astype(BF)
    taps_low = jnp.pad(taps_low, ((0, 0), (0, 0), (0, LANES - cam_width)))
    if owned % 16 == 0:
        taps_mine = jnp.stack(from_chips(taps_low))
    strip_cells = row_local * col_total
    layout = plan(camera_features.shape[1], strips, strip_cells)
    own, other, dense, both_low = pool(
        place, camera_features[0], pool_index[0], w_depth.T, layout
    )
    if owned % 16 == 0:
        other, taps_mine = lax.optimization_barrier((other, taps_mine))
    pooled_halves = halves_summed(own, other).astype(BF)
    pooled = along_chips(pooled_halves)
    widths = [hidden_width, lidar_width, LANES]
    if owned % 16 == 0:
        taps_full = arrange(place, taps_mine, swapped(taps_mine), widths)
    else:
        gathered = lax.all_gather(taps_low, "strip", axis=1, tiled=True)
        taps_full = jnp.split(gathered, [hidden_width, hidden_width + lidar_width], axis=2)
    lidar_parts = halo(lidar_bev[0])
    gaps = nearest_gaps(
        box_peaks[0], box_count, first_row, row_local, col_total, classes
    )
    pooled, gaps, taps_full, lidar_parts = lax.optimization_barrier(
        (pooled, gaps, taps_full, lidar_parts)
    )
    wide_out = jax.ShapeDtypeStruct((row_local, col_total, hidden_width), F32)
    axes = ("batch", "strip")
    devices = lax.axis_size(axes)
    stats_out = jax.ShapeDtypeStruct((devices, 3, hidden_width), F32)
    camera_parts = halo(settle(pooled, row_local, col_total))
    join_out, stats = convolve(
        [lidar_parts, camera_parts],
        taps_full[1:],
        False,
        keep_moments,
        [wide_out, stats_out],
        [gaps],
    )
    cells = float(strip_cells)
    center_one, scale_one, positives, join_border = moments(
        stats, cells, edges(join_out[:1], join_out[-1:])
    )

    def norm_one(values):
        return (values - center_one) * scale_one

    def act_of(values):
        return jax.nn.silu(norm_one(values) * norm_params[0] + norm_params[1]).astype(BF)

    act_parts = with_edges(act_of, [join_out], [join_border])
    act_one = act_parts[1]
    res_out, stats = convolve(
        [act_parts], taps_full[:1], False, keep_moments, [wide_out, stats_out]
    )
    center_two, scale_two, unused_term, unused_border = moments(stats, cells, ())

    def norm_two(values):
        return (values - center_two) * scale_two

    vectors = jnp.stack([center_two, scale_two, norm_params[2], norm_params[3]])
    grad_summed, sums, local_loss, grad_head = run_head(
        vectors,
        res_out,
        act_one,
        w_head.T.astype(BF),
        head_bias[:, None],
        gaps,
        positives.reshape(1, 1),
        devices,
    )
    shared = lax.all_to_all(sums, axes, 0, 0)
    shift_two, gain_two = jnp.sum(shared, axis=0)

    def grad_res_of(grad, values):
        spare = grad - shift_two / cell_total - norm_two(values) * gain_two / cell_total
        return (norm_params[2] * scale_two * spare).astype(BF)

    res_parts = halo(grad_res_of(grad_summed, res_out))
    line_out = jax.ShapeDtypeStruct((1, col_total, hidden_width), F32)
    sums_out = jax.ShapeDtypeStruct((devices, 2, hidden_width), F32)
    vectors = jnp.stack([center_one, scale_one, norm_params[0], norm_params[1]])
    grad_pre, grad_first, grad_last, sums = convolve(
        [res_parts],
        taps_full[:1],
        True,
        keep_grad,
        [wide_out, line_out, line_out, sums_out],
        [grad_summed, join_out, vectors],
    )
    gain_one, shift_one, pre_border, (own_res, other_res) = grad_sums(
        sums,
        grad_first,
        grad_last,
        (res_parts[1],),
        lambda grad: taps(place, [act_parts], [hidden_width], grad, strips // 2),
    )

    def grad_join_of(grad, values):
        spare = grad - shift_one / cell_total - norm_one(values) * gain_one / cell_total
        return (norm_params[0] * scale_one * spare).astype(BF)

    join_parts = with_edges(grad_join_of, [grad_pre, join_out], [pre_border, join_border])
    cells_out = jax.ShapeDtypeStruct((layout["per_strip"], cam_width, LANES), BF)
    (grad_cells,) = convolve(
        [join_parts], taps_full[2:], True, keep_cells, [cells_out]
    )
    grad_cells, join_late = lax.optimization_barrier((grad_cells, join_parts[1]))
    grid_parts = from_chips(grad_cells)
    own_join, other_join = taps(
        place,
        [lidar_parts, camera_parts],
        [lidar_width, cam_width],
        join_late,
        strips // 2,
    )
    grid_parts, own_join, other_join = lax.optimization_barrier((grid_parts, own_join, other_join))
    grid_mine = jnp.stack(grid_parts)
    grid_theirs = swapped(grid_mine)
    grads = jnp.concatenate(
        [halves_summed(own_res, other_res), halves_summed(own_join, other_join)], axis=-1
    )
    taps_parts = along_chips(grads.astype(BF))
    grad_both = unpool(
        place,
        camera_features[0],
        pool_index[0],
        both_low,
        dense,
        grid_mine,
        grid_theirs,
        grad_head,
        layout,
    )
    grad_both, taps_parts = lax.optimization_barrier((grad_both, taps_parts))
    parts = over_batch(total_of(taps_parts).astype(BF))
    width = w_depth.shape[0]
    mixed = grad_both.reshape(devices, -1, width)
    mixed = lax.all_to_all(mixed, axes, 0, 0)
    total_taps, shared = join_shares(place, mixed, local_loss, parts, hidden_width)
    shared = lax.all_to_all(shared, axes, 0, 0)
    grad_norm = jnp.stack([gain_one, shift_one, gain_two, shift_two])
    rates = [
        0.5 * w_depth.shape[0] ** (-0.5),
        0.5 * (9 * w_join.shape[2]) ** (-0.5),
        0.5 * (9 * w_res.shape[2]) ** (-0.5),
        0.5 * w_head.shape[0] ** (-0.5),
        SMALL_RATE,
        SMALL_RATE,
    ]
    weights = [w_depth, w_join, w_res, w_head, norm_params, head_bias]
    firsts = [m_depth, m_join, m_res, m_head, m_norm, m_bias]
    seconds = [v_depth, v_join, v_res, v_head, v_norm, v_bias]
    views = [
        jnp.transpose,
        lambda state: jnp.swapaxes(state, 2, 3).reshape(9, owned, -1),
        lambda state: jnp.swapaxes(state, 2, 3).reshape(9, owned, -1),
        jnp.transpose,
        lambda state: state,
        lambda state: state[None],
    ]
    backs = [
        jnp.transpose,
        lambda state: jnp.swapaxes(state.reshape(3, 3, owned, -1), 2, 3),
        lambda state: jnp.swapaxes(state.reshape(3, 3, owned, -1), 2, 3),
        jnp.transpose,
        lambda state: state,
        lambda state: state[0],
    ]
    states = [
        view(state)
        for view, group in zip(views, zip(weights, firsts, seconds))
        for state in group
    ]
    loss, norms, *states = update(
        shared,
        total_taps,
        grad_norm,
        positives,
        states,
        (depth_bins, cam_width, classes, hidden_width),
        rates,
    )
    result = [loss[0], norms[0, :6]]
    for k, state in enumerate(states):
        result.append(backs[k // 3](state))
    return tuple(result)


def solution(mesh):
    in_specs = (
        P("batch", "strip", None),
        P("batch", "strip", None, None),
        P("batch", "strip", None),
        P("batch", None, None),
        P("batch"),
        P(),
        P(),
        P(),
        P(None, None, None, "strip"),
        P(None, None, None, "strip"),
        P(None, None, None, "strip"),
        P(None, None, None, "strip"),
        P(None, None, None, "strip"),
        P(None, None, None, "strip"),
        P(),
        P(),
        P(),
        P(),
        P(),
        P(),
        P(),
        P(),
        P(),
    )
    out_specs = (
        P(),
        P(),
        P(),
        P(),
        P(),
        P(None, None, None, "strip"),
        P(None, None, None, "strip"),
        P(None, None, None, "strip"),
        P(None, None, None, "strip"),
        P(None, None, None, "strip"),
        P(None, None, None, "strip"),
        P(),
        P(),
        P(),
        P(),
        P(),
        P(),
        P(),
        P(),
        P(),
    )
    return jax.shard_map(shards, mesh=mesh, in_specs=in_specs, out_specs=out_specs, check_vma=False)
```

```python
import functools

import jax
import jax.numpy as jnp
from jax import lax
from jax.experimental import pallas as pl
from jax.experimental.pallas import tpu as pltpu
from jax.sharding import PartitionSpec as P

STEP = 5


EPS_NORM = 1e-05
SPREAD_TWICE = 8.0
SMALL_RATE = 0.25
CLIP_NORM = 0.01
FAR = 1e9


def edges(first, last):
    peers = lax.axis_size("strip")
    up = [(i, i + 1) for i in range(peers - 1)]
    before = lax.ppermute(last, "strip", up)
    after = lax.ppermute(first, "strip", [(j, i) for i, j in up])
    return before, after


def halo(shard):
    before, after = edges(shard[:1], shard[-1:])
    return [before, shard, after]


def with_edges(function, shards, borders):
    place = lax.axis_index("strip")
    inside = [place > 0, place < lax.axis_size("strip") - 1]
    sides = [
        jnp.where(there, function(*side), 0).astype(BF)
        for there, side in zip(inside, zip(*borders))
    ]
    return [sides[0], function(*shards), sides[1]]


def target_kernel(peaks_ref, count_ref, first_ref, gap_ref):
    gap_ref[...] = jnp.full(gap_ref.shape, FAR, jnp.float32)
    shape = gap_ref.shape[1:]
    row_ids = lax.broadcasted_iota(jnp.int32, shape, 0) + first_ref[0]
    col_ids = lax.broadcasted_iota(jnp.int32, shape, 1)

    def visit(slot, carry):
        row_gap = row_ids - peaks_ref[0, slot]
        col_gap = col_ids - peaks_ref[1, slot]
        distance = (row_gap * row_gap + col_gap * col_gap).astype(jnp.float32)
        kind = peaks_ref[2, slot]
        gap_ref[kind] = jnp.minimum(gap_ref[kind], distance)
        return carry

    lax.fori_loop(0, count_ref[0], visit, 0)


def nearest_gaps(box_peaks, box_count, first_row, row_total, col_total, classes):
    return pl.pallas_call(
        target_kernel,
        in_specs=[pl.BlockSpec(memory_space=pltpu.SMEM)] * 3,
        out_specs=pl.BlockSpec(memory_space=pltpu.VMEM),
        out_shape=jax.ShapeDtypeStruct((classes, row_total, col_total), jnp.float32),
        cost_estimate=SHORT,
        name="targets",
    )(box_peaks, box_count, first_row[None])


LANES = 128
SHORT = pl.CostEstimate(flops=1000, bytes_accessed=1000, transcendentals=0)
BF = jnp.bfloat16
F32 = jnp.float32


def plan(pixels, strips, strip_cells):
    per_strip = -(-strip_cells // LANES)
    high = strips * per_strip
    block = 352 if pixels % 352 == 0 and high <= 128 else 48
    return dict(
        per_strip=per_strip,
        high=high,
        offset=high // 2,
        block=block,
        stride=block + 4,
        group=block,
        strip_cells=strip_cells,
    )


def split_cells(index, plan):
    cell = index.astype(F32)
    strip = jnp.floor((cell + 0.5) * (1.0 / plan["strip_cells"]))
    rest = cell - strip * plan["strip_cells"]
    part = jnp.floor((rest + 0.5) * (1.0 / LANES))
    return strip * plan["per_strip"] + part - plan["offset"], rest - part * LANES


def softmax_lanes(logits, bins):
    lane = lax.broadcasted_iota(jnp.int32, logits.shape, 1)
    logits = jnp.where(lane < bins, logits, -jnp.inf)
    powers = jnp.exp(logits - jnp.max(logits, axis=1, keepdims=True))
    return powers / jnp.sum(powers, axis=1, keepdims=True)


def spread(ref, pixel, rows=16):
    return jnp.broadcast_to(ref[pl.ds(pixel, 1), :], (rows, LANES))


def one_hot(row, value, rows, offset=0):
    base = (lax.broadcasted_iota(jnp.int32, (rows, LANES), 0) - offset).astype(F32).astype(BF)
    none = jnp.zeros((16, LANES), BF)
    return [
        jnp.where(base[k : k + 16] == row, value, none) for k in range(0, rows, 16)
    ]


def high_pair(high_ref, depth_ref, first, plan):
    whole = plan["high"] // 16 * 16
    parts = []
    for j in range(2):
        row = spread(high_ref, first + j).astype(BF)
        value = spread(depth_ref, first + j).astype(BF)
        parts += one_hot(row, value, whole, plan["offset"])
    if whole < plan["high"]:
        both = [
            jnp.concatenate([spread(ref, first, 8), spread(ref, first + 1, 8)], 0).astype(BF)
            for ref in (high_ref, depth_ref)
        ]
        base = lax.broadcasted_iota(jnp.int32, (16, LANES), 0)
        base = jnp.where(base < 8, base, base - 8) + (whole - plan["offset"])
        none = jnp.zeros((16, LANES), BF)
        parts.append(jnp.where(base.astype(F32).astype(BF) == both[0], both[1], none))
    return jnp.concatenate(parts, 0)


def pool_kernel(place_ref, feat_ref, index_ref, weight_ref, own_ref, other_ref, dense_ref, both_ref, high_ref, low_ref, depth_ref, held, total, *, plan):
    bins = index_ref.shape[1]
    block, stride, high = (plan[k] for k in ("block", "stride", "high"))
    step = pl.program_id(0)

    @pl.when(step == 0)
    def _():
        high_ref[...] = jnp.zeros_like(high_ref)
        low_ref[...] = jnp.zeros_like(low_ref)
        total[...] = jnp.zeros_like(total)
        channels = total.shape[1]
        both_ref[...] = jnp.zeros_like(both_ref)
        both_ref[:bins] = weight_ref[:bins].astype(BF)
        both_ref[LANES : LANES + channels] = weight_ref[bins : bins + channels].astype(BF)

    feat = feat_ref[...]
    logits = lax.dot_general(feat, both_ref[:LANES], (((1,), (1,)), ((), ())), preferred_element_type=F32)
    depth_ref[...] = softmax_lanes(logits, bins)
    channels = total.shape[1]
    context_low = both_ref[LANES : LANES + channels]
    context = lax.dot_general(context_low, feat, (((1,), (1,)), ((), ())), preferred_element_type=F32).astype(BF)
    high_id, low_id = split_cells(index_ref[...], plan)
    high_ref[:, :bins] = high_id
    low_ref[:, :bins] = low_id
    one = jnp.ones((16, LANES), BF)

    def scatter(group, carry):
        for k in range(0, plan["group"], 2):
            first = group * plan["group"] + k
            left = high_pair(high_ref, depth_ref, first, plan)
            right = []
            for j in range(2):
                low = spread(low_ref, first + j).astype(BF)
                right.append(jnp.concatenate(one_hot(low, one, LANES), 0))
            tile = lax.dot_general(
                left, jnp.concatenate(right, 0), (((1,), (1,)), ((), ())), preferred_element_type=F32
            )
            whole = high // 16 * 16
            for j in range(2):
                part = tile[:, j * LANES : (j + 1) * LANES]
                held[pl.ds(first + j, whole, stride=stride), :] = part[j * whole : (j + 1) * whole]
                if whole < high:
                    held[pl.ds(first + j + whole * stride, 8, stride=stride), :] = part[
                        2 * whole + 8 * j : 2 * whole + 8 * j + 8
                    ]
        return carry

    lax.fori_loop(0, block // plan["group"], scatter, 0)

    def gather(k, carry):
        parts = []
        for j in range(2):
            part = held[pl.ds((k * 2 + j) * stride, block), :].astype(BF)
            dense_ref[k * 2 + j] = part
            parts.append(part)
        out = jnp.dot(context, jnp.concatenate(parts, 1), preferred_element_type=F32)
        for j in range(2):
            total[k * 2 + j] += out[:, j * LANES : (j + 1) * LANES]
        return carry

    lax.fori_loop(0, high // 2, gather, 0, unroll=36)

    @pl.when(step == pl.num_programs(0) - 1)
    def _():
        count = plan["per_strip"]
        chips = own_ref.shape[0]
        for shift in range(chips):
            chip = lax.rem(place_ref[0] + shift, chips)
            for ref, core in ((own_ref, place_ref[1]), (other_ref, 1 - place_ref[1])):
                first = (2 * chip + core) * count
                ref[shift] = total[pl.ds(first, count)].astype(BF)


def pool(place, features, index, weight, plan):
    pixels, width = features.shape
    bins = index.shape[1]
    channels = weight.shape[0] - bins
    block, high = plan["block"], plan["high"]
    halves = (high // plan["per_strip"] // 2, plan["per_strip"], channels, LANES)
    return pl.pallas_call(
        functools.partial(pool_kernel, plan=plan),
        grid=(pixels // block,),
        in_specs=[
            pl.BlockSpec(memory_space=pltpu.SMEM),
            pl.BlockSpec((block, width), lambda i: (i, 0)),
            pl.BlockSpec((block, bins), lambda i: (i, 0)),
            pl.BlockSpec(weight.shape, lambda i: (0, 0)),
        ],
        out_specs=[
            pl.BlockSpec(halves, lambda i: (0, 0, 0, 0)),
            pl.BlockSpec(halves, lambda i: (0, 0, 0, 0)),
            pl.BlockSpec((high, block, LANES), lambda i: (0, i, 0)),
            pl.BlockSpec((2 * LANES, width), lambda i: (0, 0)),
        ],
        out_shape=[
            jax.ShapeDtypeStruct(halves, BF),
            jax.ShapeDtypeStruct(halves, BF),
            jax.ShapeDtypeStruct((high, pixels, LANES), BF),
            jax.ShapeDtypeStruct((2 * LANES, width), BF),
        ],
        scratch_shapes=[pltpu.VMEM((block, LANES), F32)] * 3
        + [
            pltpu.VMEM((high * plan["stride"], LANES), F32),
            pltpu.VMEM((high, channels, LANES), F32),
        ],
        compiler_params=pltpu.CompilerParams(vmem_limit_bytes=40 << 20),
        cost_estimate=pl.CostEstimate(
            flops=4 * pixels * high * LANES * LANES,
            bytes_accessed=2 * pixels * high * LANES,
            transcendentals=0,
        ),
        name="pool",
    )(place, features, index, weight)


def unpool_kernel(place_ref, feat_ref, index_ref, both_ref, dense_ref, mine_ref, theirs_ref, head_ref, out_ref, high_ref, low_ref, pick_ref, held, sum_ref, grid_ref, grad_ref, *, plan):
    bins = index_ref.shape[1]
    channels = grid_ref.shape[1]
    chips, count = mine_ref.shape[:2]
    block, stride, high = (plan[k] for k in ("block", "stride", "high"))
    step = pl.program_id(0)

    @pl.when(step == 0)
    def _():
        high_ref[...] = jnp.zeros_like(high_ref)
        low_ref[...] = jnp.zeros_like(low_ref)
        held[...] = jnp.zeros_like(held)
        grad_ref[...] = jnp.zeros_like(grad_ref)
        for shift in range(chips):
            chip = lax.rem(place_ref[0] + (chips - shift), chips)
            for ref, core in ((mine_ref, place_ref[1]), (theirs_ref, 1 - place_ref[1])):
                grid_ref[pl.ds((2 * chip + core) * count, count)] = ref[shift]

    feat = feat_ref[...]
    logits = lax.dot_general(feat, both_ref[...], (((1,), (1,)), ((), ())), preferred_element_type=F32)
    depth = softmax_lanes(logits[:, :LANES], bins)
    context = logits[:, LANES : LANES + channels].astype(BF)
    high_id, low_id = split_cells(index_ref[...], plan)
    high_ref[:, :bins] = high_id
    low_ref[:, :bins] = low_id

    def project(k, carry):
        grid = jnp.concatenate([grid_ref[k * 2], grid_ref[k * 2 + 1]], 1)
        out = jnp.dot(context, grid, preferred_element_type=F32)
        for j in range(2):
            held[pl.ds((k * 2 + j) * stride, block), :] = out[:, j * LANES : (j + 1) * LANES]
        return carry

    lax.fori_loop(0, high // 2, project, 0, unroll=36)
    parts = 72

    def mix(k, carry):
        dense = jnp.concatenate([dense_ref[k * parts + j] for j in range(parts)], 1)
        grid = jnp.concatenate([grid_ref[k * parts + j] for j in range(parts)], 1)
        sum_ref[...] += lax.dot_general(
            dense, grid, (((1,), (1,)), ((), ())), preferred_element_type=F32
        )
        return carry

    sum_ref[...] = jnp.zeros_like(sum_ref)
    lax.fori_loop(0, high // parts, mix, 0)
    one = jnp.ones((16, LANES), BF)
    rows = (lax.broadcasted_iota(jnp.int32, (high, LANES), 0) - plan["offset"]).astype(F32)

    def collect(group, carry):
        for k in range(0, plan["group"], 2):
            first = group * plan["group"] + k
            left, right = [], []
            for j in range(2):
                left.append(held[pl.ds(first + j, high, stride=stride), :])
                low = spread(low_ref, first + j).astype(BF)
                right.append(jnp.concatenate(one_hot(low, one, LANES), 0))
            tile = jnp.dot(jnp.concatenate(left, 0).astype(BF), jnp.concatenate(right, 1), preferred_element_type=F32)
            for j in range(2):
                part = tile[j * high : (j + 1) * high, j * LANES : (j + 1) * LANES]
                kept = jnp.where(rows == high_ref[pl.ds(first + j, 1), :], part, 0.0)
                pick_ref[pl.ds(first + j, 1), :] = jnp.sum(kept, axis=0, keepdims=True)
        return carry

    lax.fori_loop(0, block // plan["group"], collect, 0)
    grad_prob = pick_ref[...]
    grad_context = sum_ref[...]
    grad_depth = depth * (grad_prob - jnp.sum(grad_prob * depth, axis=1, keepdims=True))
    grad_low = jnp.concatenate(
        [grad_depth, grad_context, jnp.zeros((block, LANES - channels), F32)], axis=1
    ).astype(BF)
    grad_ref[...] += lax.dot_general(grad_low, feat, (((0,), (0,)), ((), ())), preferred_element_type=F32)

    @pl.when(step == pl.num_programs(0) - 1)
    def _():
        first = LANES + channels
        rows = head_ref.shape[0]
        out_ref[:first] = grad_ref[:first].astype(BF)
        spare = jnp.zeros((2 * LANES - first - rows, grad_ref.shape[1]), F32)
        out_ref[first:] = jnp.concatenate([head_ref[...], spare], 0).astype(BF)


def unpool(place, features, index, both_low, dense, mine, theirs, head, plan):
    pixels, width = features.shape
    bins = index.shape[1]
    channels = mine.shape[2]
    block, high = plan["block"], plan["high"]
    return pl.pallas_call(
        functools.partial(unpool_kernel, plan=plan),
        grid=(pixels // block,),
        in_specs=[
            pl.BlockSpec(memory_space=pltpu.SMEM),
            pl.BlockSpec((block, width), lambda i: (i, 0)),
            pl.BlockSpec((block, bins), lambda i: (i, 0)),
            pl.BlockSpec(both_low.shape, lambda i: (0, 0)),
            pl.BlockSpec((high, block, LANES), lambda i: (0, i, 0)),
            pl.BlockSpec(mine.shape, lambda i: (0, 0, 0, 0)),
            pl.BlockSpec(theirs.shape, lambda i: (0, 0, 0, 0)),
            pl.BlockSpec(head.shape, lambda i: (0, 0)),
        ],
        out_specs=pl.BlockSpec((2 * LANES, width), lambda i: (0, 0)),
        out_shape=jax.ShapeDtypeStruct((2 * LANES, width), BF),
        scratch_shapes=[pltpu.VMEM((block, LANES), F32)] * 3
        + [
            pltpu.VMEM((high * plan["stride"], LANES), F32),
            pltpu.VMEM((block, channels), F32),
            pltpu.VMEM((high, channels, LANES), BF),
            pltpu.VMEM((2 * LANES, width), F32),
        ],
        compiler_params=pltpu.CompilerParams(vmem_limit_bytes=40 << 20),
        cost_estimate=pl.CostEstimate(
            flops=6 * pixels * high * LANES * LANES,
            bytes_accessed=2 * pixels * high * LANES,
            transcendentals=0,
        ),
        name="unpool",
    )(place, features, index, both_low, dense, mine, theirs, head)


def fill_windows(window_ref, part, cols, span):
    before_ref, shard_ref, after_ref = part
    rows = shard_ref.shape[0]
    width = window_ref.shape[2]
    window_ref[...] = jnp.zeros_like(window_ref)
    for row in range(rows + 2):
        if row == 0:
            line = before_ref[0]
        elif row == rows + 1:
            line = after_ref[0]
        else:
            line = shard_ref[row - 1]
        line = line[:, :width]
        start = row * span
        window_ref[0, start + 1 : start + cols] = line[: cols - 1]
        window_ref[1, start : start + cols] = line
        window_ref[2, start : start + cols - 1] = line[1:]


def window_scratch(part, width, span):
    return pltpu.VMEM((3, (part[1].shape[0] + 2) * span, width), BF)


def span_of(cols):
    return -(-cols // 16) * 16


def conv_kernel(*refs, count, turned, finish):
    kernels = refs[:count]
    parts = [refs[count + 3 * k : count + 3 * k + 3] for k in range(count)]
    rows, cols = parts[0][1].shape[:2]
    span = span_of(cols)
    windows = refs[-count:]
    left, right = [], []
    for part, window_ref, kernel_ref in zip(parts, windows, kernels):
        fill_windows(window_ref, part, cols, span)
        for tap in range(9):
            upward, across = tap // 3, tap % 3
            left.append(window_ref[across, upward * span : (upward + rows) * span])
            right.append(kernel_ref[8 - tap if turned else tap])
    left = jnp.concatenate(left, 1)
    if turned:
        total = jnp.dot(left, jnp.concatenate(right, 0), preferred_element_type=F32)
    else:
        total = lax.dot_general(
            left, jnp.concatenate(right, 1), (((1,), (1,)), ((), ())), preferred_element_type=F32
        )
    finish(total, rows, cols, span, *refs[4 * count : -count])


def keep_rows(total, rows, cols, span, out_ref):
    for row in range(rows):
        out_ref[row] = total[row * span : row * span + cols]


def keep_moments(total, rows, cols, span, *refs):
    out_ref, stats_ref = refs[-2:]
    keep_rows(total, rows, cols, span, out_ref)
    cells = float(rows * cols)
    center = jnp.sum(total, axis=0, keepdims=True) / cells
    spot = lax.broadcasted_iota(jnp.int32, (span, total.shape[1]), 0)
    spread_sum = jnp.zeros_like(center)
    for row in range(rows):
        apart = total[row * span : (row + 1) * span] - center
        apart = jnp.where(spot < cols, apart, 0.0)
        spread_sum = spread_sum + jnp.sum(apart * apart, axis=0, keepdims=True)
    hits = jnp.zeros_like(center)
    for ref in refs[:-2]:
        hits = jnp.full(center.shape, jnp.sum(jnp.where(ref[...] == 0.0, 1.0, 0.0)))
    stats = jnp.concatenate([center, spread_sum, hits], 0)

    def store(device, carry):
        stats_ref[device] = stats
        return carry

    lax.fori_loop(0, stats_ref.shape[0], store, 0)


def keep_grad(total, rows, cols, span, more_ref, norm_in_ref, vector_ref, out_ref, first_ref, last_ref, sums_ref):
    center, scale, gain, shift = (vector_ref[k : k + 1] for k in range(4))
    shift_sum = jnp.zeros_like(center)
    gain_sum = jnp.zeros_like(center)
    for row in range(rows):
        normed = (norm_in_ref[row] - center) * scale
        value = normed * gain + shift
        sig = jax.nn.sigmoid(value)
        grad = total[row * span : row * span + cols] + more_ref[row]
        grad = grad * (sig * (1.0 + value * (1.0 - sig)))
        out_ref[row] = grad
        if row == 0:
            first_ref[0] = grad
        if row == rows - 1:
            last_ref[0] = grad
        shift_sum = shift_sum + jnp.sum(grad, axis=0, keepdims=True)
        gain_sum = gain_sum + jnp.sum(grad * normed, axis=0, keepdims=True)
    sums = jnp.concatenate([shift_sum, gain_sum], 0)

    def store(device, carry):
        sums_ref[device] = sums
        return carry

    lax.fori_loop(0, sums_ref.shape[0], store, 0)


def head_kernel(vector_ref, res_ref, act_ref, head_ref, bias_ref, gap_ref, count_ref, grad_ref, sums_ref, loss_ref, head_grad_ref):
    rows, cols, width = res_ref.shape
    center, scale, gain, shift = (vector_ref[k : k + 1] for k in range(4))
    head = head_ref[...]
    shift_sum = jnp.zeros_like(center)
    gain_sum = jnp.zeros_like(center)
    head_grad = jnp.zeros(head.shape, F32)
    bias_grad = jnp.zeros((head.shape[0], 1), F32)
    loss = jnp.zeros((head.shape[0], 1), F32)
    for row in range(rows):
        normed = (res_ref[row] - center) * scale
        summed = normed * gain + shift + act_ref[row].astype(F32)
        sig = jax.nn.sigmoid(summed)
        hidden = (summed * sig).astype(BF)
        logits = lax.dot_general(head, hidden, (((1,), (1,)), ((), ())), preferred_element_type=F32)
        logits = logits + bias_ref[...]
        prob = jax.nn.sigmoid(logits)
        tail = jnp.log1p(jnp.exp(-jnp.abs(logits)))
        soft_pos = jnp.maximum(logits, 0.0) + tail
        soft_neg = jnp.maximum(-logits, 0.0) + tail
        gap = gap_ref[:, row, :]
        heatmap = jnp.where(gap < FAR, jnp.exp(-gap / SPREAD_TWICE), 0.0)
        struck = jnp.where(gap == 0.0, 1.0, 0.0)
        weighting = (1.0 - heatmap) * (1.0 - heatmap)
        weighting = weighting * weighting
        miss = 1.0 - prob
        loss_here = struck * miss * miss * soft_neg + weighting * prob * prob * soft_pos
        loss = loss + jnp.sum(loss_here, axis=1, keepdims=True)
        grad_pos = -2.0 * prob * miss * miss * soft_neg - miss * miss * miss
        grad_neg = 2.0 * prob * prob * miss * soft_pos + prob * prob * prob
        grad_logits = (struck * grad_pos + weighting * grad_neg) / count_ref[...]
        grad_logits = grad_logits.astype(BF)
        bias_grad = bias_grad + jnp.sum(grad_logits.astype(F32), axis=1, keepdims=True)
        head_grad = head_grad + jnp.dot(grad_logits, hidden, preferred_element_type=F32)
        grad = lax.dot_general(grad_logits, head, (((0,), (0,)), ((), ())), preferred_element_type=F32)
        grad = grad * (sig * (1.0 + summed * (1.0 - sig)))
        grad_ref[row] = grad
        shift_sum = shift_sum + jnp.sum(grad, axis=0, keepdims=True)
        gain_sum = gain_sum + jnp.sum(grad * normed, axis=0, keepdims=True)
    loss_ref[...] = jnp.sum(loss, axis=0, keepdims=True)
    classes = head.shape[0]
    head_grad_ref[:classes] = head_grad
    down = lax.broadcasted_iota(jnp.int32, head.shape, 0)
    across = lax.broadcasted_iota(jnp.int32, head.shape, 1)
    bias_row = jnp.sum(jnp.where(down == across, bias_grad, 0.0), axis=0, keepdims=True)
    head_grad_ref[classes : classes + 1] = bias_row
    sums = jnp.concatenate([shift_sum, gain_sum], 0)

    def store(device, carry):
        sums_ref[device] = sums
        return carry

    lax.fori_loop(0, sums_ref.shape[0], store, 0)


def run_head(vectors, res_out, act, head_low, bias, gaps, positives, devices):
    rows, cols, width = res_out.shape
    classes = head_low.shape[0]
    shapes = [
        (rows, cols, width),
        (devices, 2, width),
        (1, 1),
        (classes + 1, width),
    ]
    return pl.pallas_call(
        head_kernel,
        in_specs=[pl.BlockSpec(memory_space=pltpu.VMEM)] * 7,
        out_specs=[pl.BlockSpec(memory_space=pltpu.VMEM)] * 4,
        out_shape=[jax.ShapeDtypeStruct(shape, F32) for shape in shapes],
        compiler_params=pltpu.CompilerParams(vmem_limit_bytes=24 << 20),
        name="head",
    )(vectors, res_out, act, head_low, bias, gaps, positives)


def keep_cells(total, rows, cols, span, out_ref):
    cells, channels = out_ref.shape[0] * LANES, out_ref.shape[1]
    flat = [total[row * span : row * span + cols] for row in range(rows)]
    flat.append(jnp.zeros((cells - rows * cols, total.shape[1]), F32))
    flat = jnp.concatenate(flat, 0)
    for part in range(out_ref.shape[0]):
        out_ref[part] = flat[part * LANES : (part + 1) * LANES].T[:channels].astype(BF)


def convolve(parts, kernels, turned, finish, outs, extras=()):
    rows, cols = parts[0][1].shape[:2]
    span = span_of(cols)
    widths = [kernel.shape[1] if turned else kernel.shape[2] for kernel in kernels]
    flat = [array for part in parts for array in part]
    operands = [*kernels, *flat, *extras]
    return pl.pallas_call(
        functools.partial(conv_kernel, count=len(parts), turned=turned, finish=finish),
        in_specs=[pl.BlockSpec(memory_space=pltpu.VMEM)] * len(operands),
        out_specs=[pl.BlockSpec(memory_space=pltpu.VMEM)] * len(outs),
        out_shape=outs,
        scratch_shapes=[
            window_scratch(part, width, span) for part, width in zip(parts, widths)
        ],
        compiler_params=pltpu.CompilerParams(vmem_limit_bytes=32 << 20),
        cost_estimate=pl.CostEstimate(
            flops=18 * rows * span * sum(widths) * kernels[0].shape[1],
            bytes_accessed=2 * sum(kernel.size for kernel in kernels),
            transcendentals=0,
        ),
        name="convolve",
    )(*operands)


def taps_kernel(place_ref, grad_ref, *refs, widths):
    count = len(widths)
    parts = [refs[3 * k : 3 * k + 3] for k in range(count)]
    own_ref, other_ref = refs[3 * count : 3 * count + 2]
    windows = refs[3 * count + 2 : 4 * count + 2]
    flipped_grad, total = refs[4 * count + 2 :]
    rows, cols, depth = grad_ref.shape
    owned = own_ref.shape[2]
    chips = own_ref.shape[0]
    span = span_of(cols)
    for part, window_ref in zip(parts, windows):
        fill_windows(window_ref, part, cols, span)
    flat = []
    for row in range(rows):
        flat += [grad_ref[row], jnp.zeros((span - cols, depth), BF)]
    flipped_grad[...] = jnp.concatenate(flat, 0).T

    def visit(tap, carry):
        start = pl.multiple_of((tap // 3) * span, 16)
        across = lax.rem(tap, 3)
        first = 0
        for window_ref in windows:
            window = window_ref[across, pl.ds(start, rows * span)]
            total[:, first : first + window.shape[1]] = jnp.dot(
                flipped_grad[...], window, preferred_element_type=F32
            )
            first += window.shape[1]
        for shift in range(chips):
            chip = lax.rem(place_ref[0] + shift, chips)
            for ref, core in ((own_ref, place_ref[1]), (other_ref, 1 - place_ref[1])):
                half = pl.multiple_of((2 * chip + core) * owned, 8)
                ref[shift, tap] = total[pl.ds(half, owned)].astype(BF)
        return carry

    lax.fori_loop(0, 9, visit, 0)


def taps(place, parts, widths, grad, chips):
    rows, cols, depth = grad.shape
    channels = sum(widths)
    span = span_of(cols)
    flat = [array for part in parts for array in part]
    half = jax.ShapeDtypeStruct((chips, 9, depth // chips // 2, channels), BF)
    return pl.pallas_call(
        functools.partial(taps_kernel, widths=widths),
        in_specs=[pl.BlockSpec(memory_space=pltpu.SMEM)]
        + [pl.BlockSpec(memory_space=pltpu.VMEM)] * (1 + len(flat)),
        out_specs=[pl.BlockSpec(memory_space=pltpu.VMEM)] * 2,
        out_shape=[half, half],
        scratch_shapes=[window_scratch(part, width, span) for part, width in zip(parts, widths)]
        + [pltpu.VMEM((depth, rows * span), BF), pltpu.VMEM((depth, channels), F32)],
        compiler_params=pltpu.CompilerParams(vmem_limit_bytes=28 << 20),
        cost_estimate=SHORT,
        name="taps",
    )(place, grad, *flat)


def settle_kernel(*refs):
    out_ref = refs[-1]
    rows, cols = out_ref.shape[:2]
    total = refs[0][...].astype(F32)
    for ref in refs[1:-1]:
        total = total + ref[...].astype(F32)
    parts = total.shape[0]
    flat = jnp.concatenate([total[part].T for part in range(parts)], 0)
    spare = jnp.zeros((cols, out_ref.shape[2] - flat.shape[1]), F32)
    for row in range(rows):
        line = flat[row * cols : (row + 1) * cols]
        out_ref[row] = jnp.concatenate([line, spare], 1).astype(BF)


def settle(parts, rows, cols):
    return pl.pallas_call(
        settle_kernel,
        in_specs=[pl.BlockSpec(memory_space=pltpu.VMEM)] * len(parts),
        out_specs=pl.BlockSpec(memory_space=pltpu.VMEM),
        out_shape=jax.ShapeDtypeStruct((rows, cols, LANES), BF),
        compiler_params=pltpu.CompilerParams(vmem_limit_bytes=32 << 20),
        name="settle",
    )(*parts)


def split_bits(value):
    pieces = []
    for _ in range(3):
        piece = value.astype(BF).astype(F32)
        pieces.append(piece)
        value = value - piece
    return pieces


def join_kernel(mixed_ref, loss_ref, *refs, hidden_width):
    parts = refs[:-2]
    share_ref, out_ref = refs[-2:]
    total = parts[0][...].astype(F32)
    for part in parts[1:]:
        total = total + part[...].astype(F32)
    share_ref[...] = total.astype(BF)
    square = jnp.sum(total * total, axis=0, keepdims=True)
    scalars = [
        jnp.sum(square[:, hidden_width:], axis=1, keepdims=True),
        jnp.sum(square[:, :hidden_width], axis=1, keepdims=True),
        loss_ref[...],
    ]
    mixed = jnp.sum(mixed_ref[...].astype(F32), axis=0)
    shape = (mixed.shape[0], LANES)
    lane = lax.broadcasted_iota(jnp.int32, shape, 1)
    row = jnp.zeros(shape, F32)
    for k, scalar in enumerate(scalars):
        for j, piece in enumerate(split_bits(scalar)):
            row = jnp.where(lane == 3 * k + j, piece, row)
    block = jnp.concatenate([mixed, row], 1).astype(BF)

    def store(device, carry):
        out_ref[device] = block
        return carry

    lax.fori_loop(0, out_ref.shape[0], store, 0)


def join_shares(mixed, loss, parts, hidden_width):
    devices, rows, width = mixed.shape
    return pl.pallas_call(
        functools.partial(join_kernel, hidden_width=hidden_width),
        in_specs=[pl.BlockSpec(memory_space=pltpu.VMEM)] * (2 + len(parts)),
        out_specs=[pl.BlockSpec(memory_space=pltpu.VMEM)] * 2,
        out_shape=[
            jax.ShapeDtypeStruct(parts[0].shape, BF),
            jax.ShapeDtypeStruct((devices, rows, width + LANES), BF),
        ],
        compiler_params=pltpu.CompilerParams(vmem_limit_bytes=16 << 20),
        name="join_shares",
    )(mixed, loss.reshape(1, 1), *parts)


def stage_kernel(after_ref, *refs):
    count = (len(refs) - 1) // 2
    sems = refs[-1]
    copies = [
        pltpu.make_async_copy(refs[k], refs[count + k], sems.at[k]) for k in range(count)
    ]
    for copy in copies:
        copy.start()
    for copy in copies:
        copy.wait()


def stage(after, arrays):
    return pl.pallas_call(
        stage_kernel,
        in_specs=[pl.BlockSpec(memory_space=pltpu.VMEM)]
        + [pl.BlockSpec(memory_space=pl.ANY)] * len(arrays),
        out_specs=[pl.BlockSpec(memory_space=pltpu.VMEM)] * len(arrays),
        out_shape=[jax.ShapeDtypeStruct(array.shape, array.dtype) for array in arrays],
        scratch_shapes=[pltpu.SemaphoreType.DMA((len(arrays),))],
        compiler_params=pltpu.CompilerParams(vmem_limit_bytes=16 << 20),
        cost_estimate=SHORT,
        name="stage",
    )(after, *arrays)


def update_kernel(place_ref, shared_ref, norm_ref, count_ref, *refs, shapes, rates, pieces):
    pieces_refs, refs = refs[:pieces], refs[pieces:]
    states, outputs = refs[:18], refs[18:38]
    mixed_ref, taps_scratch, load_sem, store_sem = refs[38:42]
    held = refs[42:]
    loads = [
        pltpu.make_async_copy(state, buffer, load_sem.at[k])
        for k, (state, buffer) in enumerate(zip(states, held))
    ]
    for load in loads:
        load.start()
    share, width = shared_ref.shape[1], mixed_ref.shape[1]
    for device in range(shared_ref.shape[0]):
        mixed_ref[device * share : (device + 1) * share] = shared_ref[device, :, :width].astype(F32)
    depth_bins, cam_width, classes, hidden_width = shapes
    if pieces > 1:
        for shift, ref in enumerate(pieces_refs):
            taps_scratch[lax.rem(place_ref[2] + (pieces - shift), pieces)] = ref[...].astype(F32)
        taps_ref = taps_scratch[...].reshape(9, held[3].shape[1], taps_scratch.shape[2])
    else:
        taps_ref = pieces_refs[0][...]
    mixed = mixed_ref[...]
    column = LANES + cam_width
    edge = taps_ref.shape[2] - cam_width
    grads = [
        jnp.concatenate([mixed[:depth_bins], mixed[LANES:column]], 0),
        jnp.concatenate([taps_ref[:, :, edge:], taps_ref[:, :, hidden_width:edge]], 2),
        taps_ref[:, :, :hidden_width],
        mixed[column : column + classes],
        norm_ref[...],
        mixed[column + classes : column + classes + 1, :classes],
    ]
    sums = jnp.sum(shared_ref[:, :1, width:].astype(F32), axis=0)
    lane = lax.broadcasted_iota(jnp.int32, sums.shape, 1)
    squared = [None if k in (1, 2) else jnp.sum(grad * grad) for k, grad in enumerate(grads)]
    squared[1] = jnp.sum(jnp.where(lane < 3, sums, 0.0))
    squared[2] = jnp.sum(jnp.where((lane >= 3) & (lane < 6), sums, 0.0))
    loss_sum = jnp.sum(jnp.where((lane >= 6) & (lane < 9), sums, 0.0), axis=1, keepdims=True)
    loss_ref, norms_ref = outputs[:2]
    loss_ref[...] = loss_sum / count_ref[...]
    stores = [
        pltpu.make_async_copy(buffer, output, store_sem.at[k])
        for k, (buffer, output) in enumerate(zip(held, outputs[2:]))
    ]
    norms = jnp.zeros((1, LANES), F32)
    spot = lax.broadcasted_iota(jnp.int32, norms.shape, 1)
    for k, grad in enumerate(grads):
        size = jnp.sqrt(jnp.full((1, LANES), squared[k], F32))
        norms = jnp.where(spot == k, jnp.log(size), norms)
        factor = CLIP_NORM / jnp.maximum(size, CLIP_NORM)
        factor = jnp.max(factor)
        group = range(3 * k, 3 * k + 3)
        for j in group:
            loads[j].wait()
        weight, first, second = (held[j][...] for j in group)
        results = adamw(weight, grad * factor, first, second, rates[k], STEP)
        for j, result in zip(group, results):
            held[j][...] = result
            stores[j].start()
    norms_ref[...] = norms
    for store in stores:
        store.wait()


def update(place, shared, pieces, norm, positives, states, shapes, rates):
    args = [place, shared, norm, positives.reshape(1, 1)] + pieces + states
    count = len(pieces)
    width = norm.shape[1]
    return pl.pallas_call(
        functools.partial(update_kernel, shapes=shapes, rates=rates, pieces=count),
        in_specs=[pl.BlockSpec(memory_space=pltpu.SMEM)]
        + [pl.BlockSpec(memory_space=pltpu.VMEM)] * (3 + count)
        + [pl.BlockSpec(memory_space=pl.ANY)] * 18,
        out_specs=[pl.BlockSpec(memory_space=pltpu.VMEM)] * 2
        + [pl.BlockSpec(memory_space=pl.ANY)] * 18,
        out_shape=[jax.ShapeDtypeStruct((1, 1), F32), jax.ShapeDtypeStruct((1, LANES), F32)]
        + [jax.ShapeDtypeStruct(state.shape, F32) for state in states],
        scratch_shapes=[
            pltpu.VMEM((2 * LANES, width), F32),
            pltpu.VMEM((count, *pieces[0].shape[-2:]), F32),
            pltpu.SemaphoreType.DMA((18,)),
            pltpu.SemaphoreType.DMA((18,)),
        ]
        + [pltpu.VMEM(state.shape, F32) for state in states],
        compiler_params=pltpu.CompilerParams(vmem_limit_bytes=60 << 20),
        name="update",
    )(*args)


def swapped(tensor):
    strips = lax.axis_size("strip")
    return lax.ppermute(tensor, "strip", [(i, i ^ 1) for i in range(strips)])


def halves_summed(own, other):
    return own.astype(F32) + swapped(other).astype(F32)


def moved(tensor, shift):
    strips = lax.axis_size("strip")
    return lax.ppermute(tensor, "strip", [(i, (i + 2 * shift) % strips) for i in range(strips)])


def far_first(chips):
    return sorted(range(1, chips), key=lambda shift: -min(shift, chips - shift))


def along_chips(tensor):
    chips = tensor.shape[0]
    arrived = {shift: moved(tensor[shift], shift) for shift in far_first(chips)}
    return [tensor[0]] + [arrived[shift] for shift in range(1, chips)]


def total_of(parts):
    total = parts[0].astype(F32)
    for part in parts[1:]:
        total = total + part.astype(F32)
    return total


def from_chips(tensor):
    chips = lax.axis_size("strip") // 2
    arrived = {shift: moved(tensor, shift) for shift in far_first(chips)}
    return [tensor] + [arrived[shift] for shift in range(1, chips)]


def arrange_kernel(place_ref, mine_ref, theirs_ref, *outs):
    chips, taps_total, owned = mine_ref.shape[:3]
    for chip in range(chips):
        shift = lax.rem(place_ref[0] + (chips - chip), chips)
        for core in range(2):
            start = (2 * chip + core) * owned

            def copy(ref):
                first = 0
                for out_ref in outs:
                    width = out_ref.shape[2]
                    for tap in range(taps_total):
                        out_ref[tap, start : start + owned] = ref[
                            shift, tap, :, first : first + width
                        ]
                    first += width

            pl.when(place_ref[1] == core)(functools.partial(copy, mine_ref))
            pl.when(place_ref[1] != core)(functools.partial(copy, theirs_ref))


def arrange(place, mine, theirs, widths):
    chips, taps_total, owned = mine.shape[:3]
    return pl.pallas_call(
        arrange_kernel,
        in_specs=[pl.BlockSpec(memory_space=pltpu.SMEM)]
        + [pl.BlockSpec(memory_space=pltpu.VMEM)] * 2,
        out_specs=[pl.BlockSpec(memory_space=pltpu.VMEM)] * len(widths),
        out_shape=[
            jax.ShapeDtypeStruct((taps_total, 2 * chips * owned, width), BF) for width in widths
        ],
        compiler_params=pltpu.CompilerParams(vmem_limit_bytes=32 << 20),
        cost_estimate=SHORT,
        name="arrange",
    )(place, mine, theirs)


def moments(stats, cells, border):
    shared = lax.all_to_all(stats, ("batch", "strip"), 0, 0)
    if border:
        shared, border = lax.optimization_barrier((shared, border))
    centers = shared[:, 0]
    total = jnp.mean(centers, axis=0)
    spread_mean = jnp.mean(shared[:, 1] / cells + (centers - total) ** 2, axis=0)
    return (total, lax.rsqrt(spread_mean + EPS_NORM), jnp.sum(shared[:, 2, 0]), border)


def grad_sums(sums, first, last, later, meanwhile):
    border = edges(first, last)
    shared = lax.all_to_all(sums, ("batch", "strip"), 0, 0)
    later = meanwhile(*later)
    shared, border, later = lax.optimization_barrier((shared, border, later))
    grad_shift, grad_gain = jnp.sum(shared, axis=0)
    return (grad_gain, grad_shift, border, later)


def over_batch(tensor, shift):
    count = lax.axis_size("batch")
    if shift == 0:
        return tensor
    return lax.ppermute(tensor, "batch", [(i, (i + shift) % count) for i in range(count)])


def adamw(weight, gradient, first, second, rate, step_value):
    first = 0.9 * first + 0.1 * gradient
    second = 0.999 * second + 0.001 * gradient * gradient
    fix_one = 1.0 / (1.0 - 0.9**step_value)
    fix_two = 1.0 / (1.0 - 0.999**step_value)
    update = first * fix_one / (jnp.sqrt(second * fix_two) + 1e-08) + 0.01 * weight
    return (weight - rate * update, first, second)


def shards(
    camera_features,
    lidar_bev,
    pool_index,
    box_peaks,
    box_count,
    w_depth,
    m_depth,
    v_depth,
    w_join,
    m_join,
    v_join,
    w_res,
    m_res,
    v_res,
    w_head,
    m_head,
    v_head,
    norm_params,
    m_norm,
    v_norm,
    head_bias,
    m_bias,
    v_bias,
):
    samples, row_local, col_total, lidar_width = lidar_bev.shape
    strips = lax.axis_size("strip")
    row_total = row_local * strips
    cell_total = float(samples * lax.axis_size("batch") * row_total * col_total)
    depth_bins = pool_index.shape[2]
    classes = w_head.shape[1]
    owned = w_join.shape[3]
    cam_width = w_depth.shape[1] - depth_bins
    first_row = lax.axis_index("strip") * row_local
    place = lax.axis_index("strip")
    place = jnp.stack([place // 2, place % 2, lax.axis_index("batch")]).astype(jnp.int32)
    hidden_width = w_res.shape[2]
    taps_low = jnp.concatenate(
        [
            jnp.swapaxes(part, 2, 3).reshape(9, owned, -1)
            for part in (w_res, w_join[:, :, cam_width:], w_join[:, :, :cam_width])
        ],
        axis=2,
    ).astype(BF)
    taps_low = jnp.pad(taps_low, ((0, 0), (0, 0), (0, LANES - cam_width)))
    if owned % 16 == 0:
        taps_mine = from_chips(taps_low)
    strip_cells = row_local * col_total
    layout = plan(camera_features.shape[1], strips, strip_cells)
    own, other, dense, both_low = pool(
        place, camera_features[0], pool_index[0], w_depth.T, layout
    )
    if owned % 16 == 0:
        other, taps_mine = lax.optimization_barrier((other, taps_mine))
    pooled_halves = halves_summed(own, other).astype(BF)
    pooled = along_chips(pooled_halves)
    widths = [hidden_width, lidar_width, LANES]
    if owned % 16 == 0:
        taps_mine = jnp.stack(taps_mine)
        taps_full = arrange(place, taps_mine, swapped(taps_mine), widths)
    else:
        gathered = lax.all_gather(taps_low, "strip", axis=1, tiled=True)
        taps_full = jnp.split(gathered, [hidden_width, hidden_width + lidar_width], axis=2)
    lidar_parts = halo(lidar_bev[0])
    gaps = nearest_gaps(
        box_peaks[0], box_count, first_row, row_local, col_total, classes
    )
    pooled, gaps, taps_full, lidar_parts = lax.optimization_barrier(
        (pooled, gaps, taps_full, lidar_parts)
    )
    wide_out = jax.ShapeDtypeStruct((row_local, col_total, hidden_width), F32)
    axes = ("batch", "strip")
    devices = lax.axis_size(axes)
    stats_out = jax.ShapeDtypeStruct((devices, 3, hidden_width), F32)
    camera_parts = halo(settle(pooled, row_local, col_total))
    join_out, stats = convolve(
        [lidar_parts, camera_parts],
        taps_full[1:],
        False,
        keep_moments,
        [wide_out, stats_out],
        [gaps],
    )
    cells = float(strip_cells)
    center_one, scale_one, positives, join_border = moments(
        stats, cells, edges(join_out[:1], join_out[-1:])
    )

    def norm_one(values):
        return (values - center_one) * scale_one

    def act_of(values):
        return jax.nn.silu(norm_one(values) * norm_params[0] + norm_params[1]).astype(BF)

    act_parts = with_edges(act_of, [join_out], [join_border])
    act_one = act_parts[1]
    res_out, stats = convolve(
        [act_parts], taps_full[:1], False, keep_moments, [wide_out, stats_out]
    )
    center_two, scale_two, unused_term, unused_border = moments(stats, cells, ())

    def norm_two(values):
        return (values - center_two) * scale_two

    vectors = jnp.stack([center_two, scale_two, norm_params[2], norm_params[3]])
    grad_summed, sums, local_loss, grad_head = run_head(
        vectors,
        res_out,
        act_one,
        w_head.T.astype(BF),
        head_bias[:, None],
        gaps,
        positives.reshape(1, 1),
        devices,
    )
    shared = lax.all_to_all(sums, axes, 0, 0)
    shift_two, gain_two = jnp.sum(shared, axis=0)

    def grad_res_of(grad, values):
        spare = grad - shift_two / cell_total - norm_two(values) * gain_two / cell_total
        return (norm_params[2] * scale_two * spare).astype(BF)

    res_parts = halo(grad_res_of(grad_summed, res_out))
    line_out = jax.ShapeDtypeStruct((1, col_total, hidden_width), F32)
    sums_out = jax.ShapeDtypeStruct((devices, 2, hidden_width), F32)
    vectors = jnp.stack([center_one, scale_one, norm_params[0], norm_params[1]])
    grad_pre, grad_first, grad_last, sums = convolve(
        [res_parts],
        taps_full[:1],
        True,
        keep_grad,
        [wide_out, line_out, line_out, sums_out],
        [grad_summed, join_out, vectors],
    )
    gain_one, shift_one, pre_border, (own_res, other_res) = grad_sums(
        sums,
        grad_first,
        grad_last,
        (res_parts[1],),
        lambda grad: taps(place, [act_parts], [hidden_width], grad, strips // 2),
    )

    def grad_join_of(grad, values):
        spare = grad - shift_one / cell_total - norm_one(values) * gain_one / cell_total
        return (norm_params[0] * scale_one * spare).astype(BF)

    join_parts = with_edges(grad_join_of, [grad_pre, join_out], [pre_border, join_border])
    cells_out = jax.ShapeDtypeStruct((layout["per_strip"], cam_width, LANES), BF)
    (grad_cells,) = convolve(
        [join_parts], taps_full[2:], True, keep_cells, [cells_out]
    )
    grad_cells, join_late = lax.optimization_barrier((grad_cells, join_parts[1]))
    grid_parts = from_chips(grad_cells)
    own_join, other_join = taps(
        place,
        [lidar_parts, camera_parts],
        [lidar_width, cam_width],
        join_late,
        strips // 2,
    )
    grid_parts, own_join, other_join = lax.optimization_barrier((grid_parts, own_join, other_join))
    grid_mine = jnp.stack(grid_parts)
    grid_theirs = swapped(grid_mine)
    grads = jnp.concatenate(
        [halves_summed(own_res, other_res), halves_summed(own_join, other_join)], axis=-1
    )
    taps_parts = along_chips(grads.astype(BF))
    grad_both = unpool(
        place,
        camera_features[0],
        pool_index[0],
        both_low,
        dense,
        grid_mine,
        grid_theirs,
        grad_head,
        layout,
    )
    grad_both, taps_parts = lax.optimization_barrier((grad_both, taps_parts))
    members = lax.axis_size("batch")
    member = lax.axis_index("batch")
    quarters = total_of(taps_parts).astype(BF).reshape(members, -1, (hidden_width + lidar_width + cam_width))
    parts = [
        over_batch(lax.dynamic_index_in_dim(quarters, (member + s) % members, 0, False), s)
        for s in range(members)
    ]
    width = w_depth.shape[0]
    mixed = grad_both.reshape(devices, -1, width)
    mixed = lax.all_to_all(mixed, axes, 0, 0)
    share, shared = join_shares(mixed, local_loss, parts, hidden_width)
    shared = lax.all_to_all(shared, axes, 0, 0)
    pieces = [over_batch(share, s) for s in range(members)]
    if share.shape[0] % 8:
        order = (member - jnp.arange(members)) % members
        pieces = [jnp.take(jnp.stack(pieces), order, axis=0).reshape(9, owned, -1).astype(F32)]
    grad_norm = jnp.stack([gain_one, shift_one, gain_two, shift_two])
    rates = [
        0.5 * w_depth.shape[0] ** (-0.5),
        0.5 * (9 * w_join.shape[2]) ** (-0.5),
        0.5 * (9 * w_res.shape[2]) ** (-0.5),
        0.5 * w_head.shape[0] ** (-0.5),
        SMALL_RATE,
        SMALL_RATE,
    ]
    weights = [w_depth, w_join, w_res, w_head, norm_params, head_bias]
    firsts = [m_depth, m_join, m_res, m_head, m_norm, m_bias]
    seconds = [v_depth, v_join, v_res, v_head, v_norm, v_bias]
    views = [
        jnp.transpose,
        lambda state: jnp.swapaxes(state, 2, 3).reshape(9, owned, -1),
        lambda state: jnp.swapaxes(state, 2, 3).reshape(9, owned, -1),
        jnp.transpose,
        lambda state: state,
        lambda state: state[None],
    ]
    backs = [
        jnp.transpose,
        lambda state: jnp.swapaxes(state.reshape(3, 3, owned, -1), 2, 3),
        lambda state: jnp.swapaxes(state.reshape(3, 3, owned, -1), 2, 3),
        jnp.transpose,
        lambda state: state,
        lambda state: state[0],
    ]
    states = [
        view(state)
        for view, group in zip(views, zip(weights, firsts, seconds))
        for state in group
    ]
    loss, norms, *states = update(
        place,
        shared,
        pieces,
        grad_norm,
        positives,
        states,
        (depth_bins, cam_width, classes, hidden_width),
        rates,
    )
    result = [loss[0], norms[0, :6]]
    for k, state in enumerate(states):
        result.append(backs[k // 3](state))
    return tuple(result)


def solution(mesh):
    in_specs = (
        P("batch", "strip", None),
        P("batch", "strip", None, None),
        P("batch", "strip", None),
        P("batch", None, None),
        P("batch"),
        P(),
        P(),
        P(),
        P(None, None, None, "strip"),
        P(None, None, None, "strip"),
        P(None, None, None, "strip"),
        P(None, None, None, "strip"),
        P(None, None, None, "strip"),
        P(None, None, None, "strip"),
        P(),
        P(),
        P(),
        P(),
        P(),
        P(),
        P(),
        P(),
        P(),
    )
    out_specs = (
        P(),
        P(),
        P(),
        P(),
        P(),
        P(None, None, None, "strip"),
        P(None, None, None, "strip"),
        P(None, None, None, "strip"),
        P(None, None, None, "strip"),
        P(None, None, None, "strip"),
        P(None, None, None, "strip"),
        P(),
        P(),
        P(),
        P(),
        P(),
        P(),
        P(),
        P(),
        P(),
    )
    return jax.shard_map(shards, mesh=mesh, in_specs=in_specs, out_specs=out_specs, check_vma=False)
```

```python
import functools

import jax
import jax.numpy as jnp
from jax import lax
from jax.experimental import pallas as pl
from jax.experimental.pallas import tpu as pltpu
from jax.sharding import PartitionSpec as P

STEP = 5


EPS_NORM = 1e-05
SPREAD_TWICE = 8.0
SMALL_RATE = 0.25
CLIP_NORM = 0.01
FAR = 1e9


def edges(first, last):
    peers = lax.axis_size("strip")
    up = [(i, i + 1) for i in range(peers - 1)]
    before = lax.ppermute(last, "strip", up)
    after = lax.ppermute(first, "strip", [(j, i) for i, j in up])
    return before, after


def halo(shard):
    before, after = edges(shard[:1], shard[-1:])
    return [before, shard, after]


def with_edges(function, shards, borders):
    place = lax.axis_index("strip")
    inside = [place > 0, place < lax.axis_size("strip") - 1]
    sides = [
        jnp.where(there, function(*side), 0).astype(BF)
        for there, side in zip(inside, zip(*borders))
    ]
    return [sides[0], function(*shards), sides[1]]


def target_kernel(peaks_ref, count_ref, first_ref, gap_ref):
    gap_ref[...] = jnp.full(gap_ref.shape, FAR, jnp.float32)
    shape = gap_ref.shape[1:]
    row_ids = lax.broadcasted_iota(jnp.int32, shape, 0) + first_ref[0]
    col_ids = lax.broadcasted_iota(jnp.int32, shape, 1)

    def visit(slot, carry):
        row_gap = row_ids - peaks_ref[0, slot]
        col_gap = col_ids - peaks_ref[1, slot]
        distance = (row_gap * row_gap + col_gap * col_gap).astype(jnp.float32)
        kind = peaks_ref[2, slot]
        gap_ref[kind] = jnp.minimum(gap_ref[kind], distance)
        return carry

    lax.fori_loop(0, count_ref[0], visit, 0)


def nearest_gaps(box_peaks, box_count, first_row, row_total, col_total, classes):
    return pl.pallas_call(
        target_kernel,
        in_specs=[pl.BlockSpec(memory_space=pltpu.SMEM)] * 3,
        out_specs=pl.BlockSpec(memory_space=pltpu.VMEM),
        out_shape=jax.ShapeDtypeStruct((classes, row_total, col_total), jnp.float32),
        cost_estimate=SHORT,
        name="targets",
    )(box_peaks, box_count, first_row[None])


LANES = 128
SHORT = pl.CostEstimate(flops=1000, bytes_accessed=1000, transcendentals=0)
BF = jnp.bfloat16
F32 = jnp.float32


def plan(pixels, strips, strip_cells):
    per_strip = -(-strip_cells // LANES)
    high = strips * per_strip
    block = 352 if pixels % 352 == 0 and high <= 128 else 48
    return dict(
        per_strip=per_strip,
        high=high,
        offset=high // 2,
        block=block,
        stride=block + 4,
        group=block,
        strip_cells=strip_cells,
    )


def split_cells(index, plan):
    cell = index.astype(F32)
    strip = jnp.floor((cell + 0.5) * (1.0 / plan["strip_cells"]))
    rest = cell - strip * plan["strip_cells"]
    part = jnp.floor((rest + 0.5) * (1.0 / LANES))
    return strip * plan["per_strip"] + part - plan["offset"], rest - part * LANES


def softmax_lanes(logits, bins):
    lane = lax.broadcasted_iota(jnp.int32, logits.shape, 1)
    logits = jnp.where(lane < bins, logits, -jnp.inf)
    powers = jnp.exp(logits - jnp.max(logits, axis=1, keepdims=True))
    return powers / jnp.sum(powers, axis=1, keepdims=True)


def spread(ref, pixel, rows=16):
    return jnp.broadcast_to(ref[pl.ds(pixel, 1), :], (rows, LANES))


def one_hot(row, value, rows, offset=0):
    base = (lax.broadcasted_iota(jnp.int32, (rows, LANES), 0) - offset).astype(F32).astype(BF)
    none = jnp.zeros((16, LANES), BF)
    return [
        jnp.where(base[k : k + 16] == row, value, none) for k in range(0, rows, 16)
    ]


def high_pair(high_ref, depth_ref, first, plan):
    whole = plan["high"] // 16 * 16
    parts = []
    for j in range(2):
        row = spread(high_ref, first + j).astype(BF)
        value = spread(depth_ref, first + j).astype(BF)
        parts += one_hot(row, value, whole, plan["offset"])
    if whole < plan["high"]:
        both = [
            jnp.concatenate([spread(ref, first, 8), spread(ref, first + 1, 8)], 0).astype(BF)
            for ref in (high_ref, depth_ref)
        ]
        base = lax.broadcasted_iota(jnp.int32, (16, LANES), 0)
        base = jnp.where(base < 8, base, base - 8) + (whole - plan["offset"])
        none = jnp.zeros((16, LANES), BF)
        parts.append(jnp.where(base.astype(F32).astype(BF) == both[0], both[1], none))
    return jnp.concatenate(parts, 0)


def pool_kernel(place_ref, feat_ref, index_ref, weight_ref, own_ref, other_ref, dense_ref, both_ref, high_ref, low_ref, depth_ref, held, total, *, plan):
    bins = index_ref.shape[1]
    block, stride, high = (plan[k] for k in ("block", "stride", "high"))
    step = pl.program_id(0)

    @pl.when(step == 0)
    def _():
        high_ref[...] = jnp.zeros_like(high_ref)
        low_ref[...] = jnp.zeros_like(low_ref)
        total[...] = jnp.zeros_like(total)
        channels = total.shape[1]
        both_ref[...] = jnp.zeros_like(both_ref)
        both_ref[:bins] = weight_ref[:bins].astype(BF)
        both_ref[LANES : LANES + channels] = weight_ref[bins : bins + channels].astype(BF)

    feat = feat_ref[...]
    logits = lax.dot_general(feat, both_ref[:LANES], (((1,), (1,)), ((), ())), preferred_element_type=F32)
    depth_ref[...] = softmax_lanes(logits, bins)
    channels = total.shape[1]
    context_low = both_ref[LANES : LANES + channels]
    context = lax.dot_general(context_low, feat, (((1,), (1,)), ((), ())), preferred_element_type=F32).astype(BF)
    high_id, low_id = split_cells(index_ref[...], plan)
    high_ref[:, :bins] = high_id
    low_ref[:, :bins] = low_id
    one = jnp.ones((16, LANES), BF)

    def scatter(group, carry):
        for k in range(0, plan["group"], 2):
            first = group * plan["group"] + k
            left = high_pair(high_ref, depth_ref, first, plan)
            right = []
            for j in range(2):
                low = spread(low_ref, first + j).astype(BF)
                right.append(jnp.concatenate(one_hot(low, one, LANES), 0))
            tile = lax.dot_general(
                left, jnp.concatenate(right, 0), (((1,), (1,)), ((), ())), preferred_element_type=F32
            )
            whole = high // 16 * 16
            for j in range(2):
                part = tile[:, j * LANES : (j + 1) * LANES]
                held[pl.ds(first + j, whole, stride=stride), :] = part[j * whole : (j + 1) * whole]
                if whole < high:
                    held[pl.ds(first + j + whole * stride, 8, stride=stride), :] = part[
                        2 * whole + 8 * j : 2 * whole + 8 * j + 8
                    ]
        return carry

    lax.fori_loop(0, block // plan["group"], scatter, 0)

    def gather(k, carry):
        parts = []
        for j in range(2):
            part = held[pl.ds((k * 2 + j) * stride, block), :].astype(BF)
            dense_ref[k * 2 + j] = part
            parts.append(part)
        out = jnp.dot(context, jnp.concatenate(parts, 1), preferred_element_type=F32)
        for j in range(2):
            total[k * 2 + j] += out[:, j * LANES : (j + 1) * LANES]
        return carry

    lax.fori_loop(0, high // 2, gather, 0, unroll=36)

    @pl.when(step == pl.num_programs(0) - 1)
    def _():
        count = plan["per_strip"]
        chips = own_ref.shape[0]
        for shift in range(chips):
            chip = lax.rem(place_ref[0] + shift, chips)
            for ref, core in ((own_ref, place_ref[1]), (other_ref, 1 - place_ref[1])):
                first = (2 * chip + core) * count
                ref[shift] = total[pl.ds(first, count)].astype(BF)


def pool(place, features, index, weight, plan):
    pixels, width = features.shape
    bins = index.shape[1]
    channels = weight.shape[0] - bins
    block, high = plan["block"], plan["high"]
    halves = (high // plan["per_strip"] // 2, plan["per_strip"], channels, LANES)
    return pl.pallas_call(
        functools.partial(pool_kernel, plan=plan),
        grid=(pixels // block,),
        in_specs=[
            pl.BlockSpec(memory_space=pltpu.SMEM),
            pl.BlockSpec((block, width), lambda i: (i, 0)),
            pl.BlockSpec((block, bins), lambda i: (i, 0)),
            pl.BlockSpec(weight.shape, lambda i: (0, 0)),
        ],
        out_specs=[
            pl.BlockSpec(halves, lambda i: (0, 0, 0, 0)),
            pl.BlockSpec(halves, lambda i: (0, 0, 0, 0)),
            pl.BlockSpec((high, block, LANES), lambda i: (0, i, 0)),
            pl.BlockSpec((2 * LANES, width), lambda i: (0, 0)),
        ],
        out_shape=[
            jax.ShapeDtypeStruct(halves, BF),
            jax.ShapeDtypeStruct(halves, BF),
            jax.ShapeDtypeStruct((high, pixels, LANES), BF),
            jax.ShapeDtypeStruct((2 * LANES, width), BF),
        ],
        scratch_shapes=[pltpu.VMEM((block, LANES), F32)] * 3
        + [
            pltpu.VMEM((high * plan["stride"], LANES), F32),
            pltpu.VMEM((high, channels, LANES), F32),
        ],
        compiler_params=pltpu.CompilerParams(vmem_limit_bytes=40 << 20),
        cost_estimate=pl.CostEstimate(
            flops=4 * pixels * high * LANES * LANES,
            bytes_accessed=2 * pixels * high * LANES,
            transcendentals=0,
        ),
        name="pool",
    )(place, features, index, weight)


def unpool_kernel(place_ref, feat_ref, index_ref, both_ref, dense_ref, mine_ref, theirs_ref, head_ref, out_ref, high_ref, low_ref, pick_ref, held, sum_ref, grid_ref, grad_ref, *, plan):
    bins = index_ref.shape[1]
    channels = grid_ref.shape[1]
    chips, count = mine_ref.shape[:2]
    block, stride, high = (plan[k] for k in ("block", "stride", "high"))
    step = pl.program_id(0)

    @pl.when(step == 0)
    def _():
        high_ref[...] = jnp.zeros_like(high_ref)
        low_ref[...] = jnp.zeros_like(low_ref)
        held[...] = jnp.zeros_like(held)
        grad_ref[...] = jnp.zeros_like(grad_ref)
        for shift in range(chips):
            chip = lax.rem(place_ref[0] + (chips - shift), chips)
            for ref, core in ((mine_ref, place_ref[1]), (theirs_ref, 1 - place_ref[1])):
                grid_ref[pl.ds((2 * chip + core) * count, count)] = ref[shift]

    feat = feat_ref[...]
    logits = lax.dot_general(feat, both_ref[...], (((1,), (1,)), ((), ())), preferred_element_type=F32)
    depth = softmax_lanes(logits[:, :LANES], bins)
    context = logits[:, LANES : LANES + channels].astype(BF)
    high_id, low_id = split_cells(index_ref[...], plan)
    high_ref[:, :bins] = high_id
    low_ref[:, :bins] = low_id

    def project(k, carry):
        grid = jnp.concatenate([grid_ref[k * 2], grid_ref[k * 2 + 1]], 1)
        out = jnp.dot(context, grid, preferred_element_type=F32)
        for j in range(2):
            held[pl.ds((k * 2 + j) * stride, block), :] = out[:, j * LANES : (j + 1) * LANES]
        return carry

    lax.fori_loop(0, high // 2, project, 0, unroll=36)
    parts = 72

    def mix(k, carry):
        dense = jnp.concatenate([dense_ref[k * parts + j] for j in range(parts)], 1)
        grid = jnp.concatenate([grid_ref[k * parts + j] for j in range(parts)], 1)
        sum_ref[...] += lax.dot_general(
            dense, grid, (((1,), (1,)), ((), ())), preferred_element_type=F32
        )
        return carry

    sum_ref[...] = jnp.zeros_like(sum_ref)
    lax.fori_loop(0, high // parts, mix, 0)
    one = jnp.ones((16, LANES), BF)
    rows = (lax.broadcasted_iota(jnp.int32, (high, LANES), 0) - plan["offset"]).astype(F32)

    def collect(group, carry):
        for k in range(0, plan["group"], 2):
            first = group * plan["group"] + k
            left, right = [], []
            for j in range(2):
                left.append(held[pl.ds(first + j, high, stride=stride), :])
                low = spread(low_ref, first + j).astype(BF)
                right.append(jnp.concatenate(one_hot(low, one, LANES), 0))
            tile = jnp.dot(jnp.concatenate(left, 0).astype(BF), jnp.concatenate(right, 1), preferred_element_type=F32)
            for j in range(2):
                part = tile[j * high : (j + 1) * high, j * LANES : (j + 1) * LANES]
                kept = jnp.where(rows == high_ref[pl.ds(first + j, 1), :], part, 0.0)
                pick_ref[pl.ds(first + j, 1), :] = jnp.sum(kept, axis=0, keepdims=True)
        return carry

    lax.fori_loop(0, block // plan["group"], collect, 0)
    grad_prob = pick_ref[...]
    grad_context = sum_ref[...]
    grad_depth = depth * (grad_prob - jnp.sum(grad_prob * depth, axis=1, keepdims=True))
    grad_low = jnp.concatenate(
        [grad_depth, grad_context, jnp.zeros((block, LANES - channels), F32)], axis=1
    ).astype(BF)
    grad_ref[...] += lax.dot_general(grad_low, feat, (((0,), (0,)), ((), ())), preferred_element_type=F32)

    @pl.when(step == pl.num_programs(0) - 1)
    def _():
        first = LANES + channels
        rows = head_ref.shape[0]
        out_ref[:first] = grad_ref[:first].astype(BF)
        spare = jnp.zeros((2 * LANES - first - rows, grad_ref.shape[1]), F32)
        out_ref[first:] = jnp.concatenate([head_ref[...], spare], 0).astype(BF)


def unpool(place, features, index, both_low, dense, mine, theirs, head, plan):
    pixels, width = features.shape
    bins = index.shape[1]
    channels = mine.shape[2]
    block, high = plan["block"], plan["high"]
    return pl.pallas_call(
        functools.partial(unpool_kernel, plan=plan),
        grid=(pixels // block,),
        in_specs=[
            pl.BlockSpec(memory_space=pltpu.SMEM),
            pl.BlockSpec((block, width), lambda i: (i, 0)),
            pl.BlockSpec((block, bins), lambda i: (i, 0)),
            pl.BlockSpec(both_low.shape, lambda i: (0, 0)),
            pl.BlockSpec((high, block, LANES), lambda i: (0, i, 0)),
            pl.BlockSpec(mine.shape, lambda i: (0, 0, 0, 0)),
            pl.BlockSpec(theirs.shape, lambda i: (0, 0, 0, 0)),
            pl.BlockSpec(head.shape, lambda i: (0, 0)),
        ],
        out_specs=pl.BlockSpec((2 * LANES, width), lambda i: (0, 0)),
        out_shape=jax.ShapeDtypeStruct((2 * LANES, width), BF),
        scratch_shapes=[pltpu.VMEM((block, LANES), F32)] * 3
        + [
            pltpu.VMEM((high * plan["stride"], LANES), F32),
            pltpu.VMEM((block, channels), F32),
            pltpu.VMEM((high, channels, LANES), BF),
            pltpu.VMEM((2 * LANES, width), F32),
        ],
        compiler_params=pltpu.CompilerParams(vmem_limit_bytes=40 << 20),
        cost_estimate=pl.CostEstimate(
            flops=6 * pixels * high * LANES * LANES,
            bytes_accessed=2 * pixels * high * LANES,
            transcendentals=0,
        ),
        name="unpool",
    )(place, features, index, both_low, dense, mine, theirs, head)


def fill_windows(window_ref, part, cols, span):
    before_ref, shard_ref, after_ref = part
    rows = shard_ref.shape[0]
    width = window_ref.shape[2]
    window_ref[...] = jnp.zeros_like(window_ref)
    for row in range(rows + 2):
        if row == 0:
            line = before_ref[0]
        elif row == rows + 1:
            line = after_ref[0]
        else:
            line = shard_ref[row - 1]
        line = line[:, :width]
        start = row * span
        window_ref[0, start + 1 : start + cols] = line[: cols - 1]
        window_ref[1, start : start + cols] = line
        window_ref[2, start : start + cols - 1] = line[1:]


def fill_by_loop(window_ref, part, cols, span):
    before_ref, shard_ref, after_ref = part
    rows = shard_ref.shape[0]
    width = window_ref.shape[2]
    window_ref[...] = jnp.zeros_like(window_ref)

    def lay(row, line):
        line = line[:, :width]
        start = pl.multiple_of(row * span, 16)
        window_ref.at[0, pl.ds(start, span)][1:cols] = line[: cols - 1]
        window_ref.at[1, pl.ds(start, span)][:cols] = line
        window_ref.at[2, pl.ds(start, span)][: cols - 1] = line[1:]

    def middle(row, carry):
        lay(row, shard_ref[row - 1])
        return carry

    lay(0, before_ref[0])
    lay(rows + 1, after_ref[0])
    lax.fori_loop(1, rows + 1, middle, 0)


def window_scratch(part, width, span):
    return pltpu.VMEM((3, (part[1].shape[0] + 2) * span, width), BF)


def span_of(cols):
    return -(-cols // 16) * 16


def conv_kernel(*refs, count, turned, finish):
    kernels = refs[:count]
    parts = [refs[count + 3 * k : count + 3 * k + 3] for k in range(count)]
    rows, cols = parts[0][1].shape[:2]
    span = span_of(cols)
    windows = refs[-count:]
    left, right = [], []
    for part, window_ref, kernel_ref in zip(parts, windows, kernels):
        fill_windows(window_ref, part, cols, span)
        for tap in range(9):
            upward, across = tap // 3, tap % 3
            left.append(window_ref[across, upward * span : (upward + rows) * span])
            right.append(kernel_ref[8 - tap if turned else tap])
    left = jnp.concatenate(left, 1)
    if turned:
        total = jnp.dot(left, jnp.concatenate(right, 0), preferred_element_type=F32)
    else:
        total = lax.dot_general(
            left, jnp.concatenate(right, 1), (((1,), (1,)), ((), ())), preferred_element_type=F32
        )
    finish(total, rows, cols, span, *refs[4 * count : -count])


def keep_rows(total, rows, cols, span, out_ref):
    for row in range(rows):
        out_ref[row] = total[row * span : row * span + cols]


def keep_moments(total, rows, cols, span, *refs):
    out_ref, stats_ref = refs[-2:]
    keep_rows(total, rows, cols, span, out_ref)
    cells = float(rows * cols)
    center = jnp.sum(total, axis=0, keepdims=True) / cells
    spot = lax.broadcasted_iota(jnp.int32, (span, total.shape[1]), 0)
    spread_sum = jnp.zeros_like(center)
    for row in range(rows):
        apart = total[row * span : (row + 1) * span] - center
        apart = jnp.where(spot < cols, apart, 0.0)
        spread_sum = spread_sum + jnp.sum(apart * apart, axis=0, keepdims=True)
    hits = jnp.zeros_like(center)
    for ref in refs[:-2]:
        hits = jnp.full(center.shape, jnp.sum(jnp.where(ref[...] == 0.0, 1.0, 0.0)))
    stats = jnp.concatenate([center, spread_sum, hits], 0)

    def store(device, carry):
        stats_ref[device] = stats
        return carry

    lax.fori_loop(0, stats_ref.shape[0], store, 0)


def keep_grad(total, rows, cols, span, more_ref, norm_in_ref, vector_ref, out_ref, first_ref, last_ref, sums_ref):
    center, scale, gain, shift = (vector_ref[k : k + 1] for k in range(4))
    shift_sum = jnp.zeros_like(center)
    gain_sum = jnp.zeros_like(center)
    for row in range(rows):
        normed = (norm_in_ref[row] - center) * scale
        value = normed * gain + shift
        sig = jax.nn.sigmoid(value)
        grad = total[row * span : row * span + cols] + more_ref[row]
        grad = grad * (sig * (1.0 + value * (1.0 - sig)))
        out_ref[row] = grad
        if row == 0:
            first_ref[0] = grad
        if row == rows - 1:
            last_ref[0] = grad
        shift_sum = shift_sum + jnp.sum(grad, axis=0, keepdims=True)
        gain_sum = gain_sum + jnp.sum(grad * normed, axis=0, keepdims=True)
    sums = jnp.concatenate([shift_sum, gain_sum], 0)

    def store(device, carry):
        sums_ref[device] = sums
        return carry

    lax.fori_loop(0, sums_ref.shape[0], store, 0)


def head_kernel(vector_ref, res_ref, act_ref, head_ref, bias_ref, gap_ref, count_ref, grad_ref, sums_ref, loss_ref, head_grad_ref):
    rows, cols, width = res_ref.shape
    center, scale, gain, shift = (vector_ref[k : k + 1] for k in range(4))
    head = head_ref[...]
    shift_sum = jnp.zeros_like(center)
    gain_sum = jnp.zeros_like(center)
    head_grad = jnp.zeros(head.shape, F32)
    bias_grad = jnp.zeros((head.shape[0], 1), F32)
    loss = jnp.zeros((head.shape[0], 1), F32)
    for row in range(rows):
        normed = (res_ref[row] - center) * scale
        summed = normed * gain + shift + act_ref[row].astype(F32)
        sig = jax.nn.sigmoid(summed)
        hidden = (summed * sig).astype(BF)
        logits = lax.dot_general(head, hidden, (((1,), (1,)), ((), ())), preferred_element_type=F32)
        logits = logits + bias_ref[...]
        prob = jax.nn.sigmoid(logits)
        tail = jnp.log1p(jnp.exp(-jnp.abs(logits)))
        soft_pos = jnp.maximum(logits, 0.0) + tail
        soft_neg = jnp.maximum(-logits, 0.0) + tail
        gap = gap_ref[:, row, :]
        heatmap = jnp.where(gap < FAR, jnp.exp(-gap / SPREAD_TWICE), 0.0)
        struck = jnp.where(gap == 0.0, 1.0, 0.0)
        weighting = (1.0 - heatmap) * (1.0 - heatmap)
        weighting = weighting * weighting
        miss = 1.0 - prob
        loss_here = struck * miss * miss * soft_neg + weighting * prob * prob * soft_pos
        loss = loss + jnp.sum(loss_here, axis=1, keepdims=True)
        grad_pos = -2.0 * prob * miss * miss * soft_neg - miss * miss * miss
        grad_neg = 2.0 * prob * prob * miss * soft_pos + prob * prob * prob
        grad_logits = (struck * grad_pos + weighting * grad_neg) / count_ref[...]
        grad_logits = grad_logits.astype(BF)
        bias_grad = bias_grad + jnp.sum(grad_logits.astype(F32), axis=1, keepdims=True)
        head_grad = head_grad + jnp.dot(grad_logits, hidden, preferred_element_type=F32)
        grad = lax.dot_general(grad_logits, head, (((0,), (0,)), ((), ())), preferred_element_type=F32)
        grad = grad * (sig * (1.0 + summed * (1.0 - sig)))
        grad_ref[row] = grad
        shift_sum = shift_sum + jnp.sum(grad, axis=0, keepdims=True)
        gain_sum = gain_sum + jnp.sum(grad * normed, axis=0, keepdims=True)
    loss_ref[...] = jnp.sum(loss, axis=0, keepdims=True)
    classes = head.shape[0]
    head_grad_ref[:classes] = head_grad
    down = lax.broadcasted_iota(jnp.int32, head.shape, 0)
    across = lax.broadcasted_iota(jnp.int32, head.shape, 1)
    bias_row = jnp.sum(jnp.where(down == across, bias_grad, 0.0), axis=0, keepdims=True)
    head_grad_ref[classes : classes + 1] = bias_row
    sums = jnp.concatenate([shift_sum, gain_sum], 0)

    def store(device, carry):
        sums_ref[device] = sums
        return carry

    lax.fori_loop(0, sums_ref.shape[0], store, 0)


def run_head(vectors, res_out, act, head_low, bias, gaps, positives, devices):
    rows, cols, width = res_out.shape
    classes = head_low.shape[0]
    shapes = [
        (rows, cols, width),
        (devices, 2, width),
        (1, 1),
        (classes + 1, width),
    ]
    return pl.pallas_call(
        head_kernel,
        in_specs=[pl.BlockSpec(memory_space=pltpu.VMEM)] * 7,
        out_specs=[pl.BlockSpec(memory_space=pltpu.VMEM)] * 4,
        out_shape=[jax.ShapeDtypeStruct(shape, F32) for shape in shapes],
        compiler_params=pltpu.CompilerParams(vmem_limit_bytes=24 << 20),
        name="head",
    )(vectors, res_out, act, head_low, bias, gaps, positives)


def keep_cells(total, rows, cols, span, out_ref):
    cells, channels = out_ref.shape[0] * LANES, out_ref.shape[1]
    flat = [total[row * span : row * span + cols] for row in range(rows)]
    flat.append(jnp.zeros((cells - rows * cols, total.shape[1]), F32))
    flat = jnp.concatenate(flat, 0)
    for part in range(out_ref.shape[0]):
        out_ref[part] = flat[part * LANES : (part + 1) * LANES].T[:channels].astype(BF)


def convolve(parts, kernels, turned, finish, outs, extras=()):
    rows, cols = parts[0][1].shape[:2]
    span = span_of(cols)
    widths = [kernel.shape[1] if turned else kernel.shape[2] for kernel in kernels]
    flat = [array for part in parts for array in part]
    operands = [*kernels, *flat, *extras]
    return pl.pallas_call(
        functools.partial(conv_kernel, count=len(parts), turned=turned, finish=finish),
        in_specs=[pl.BlockSpec(memory_space=pltpu.VMEM)] * len(operands),
        out_specs=[pl.BlockSpec(memory_space=pltpu.VMEM)] * len(outs),
        out_shape=outs,
        scratch_shapes=[
            window_scratch(part, width, span) for part, width in zip(parts, widths)
        ],
        compiler_params=pltpu.CompilerParams(vmem_limit_bytes=32 << 20),
        cost_estimate=pl.CostEstimate(
            flops=18 * rows * span * sum(widths) * kernels[0].shape[1],
            bytes_accessed=2 * sum(kernel.size for kernel in kernels),
            transcendentals=0,
        ),
        name="convolve",
    )(*operands)


def taps_kernel(place_ref, grad_ref, *refs, widths):
    count = len(widths)
    parts = [refs[3 * k : 3 * k + 3] for k in range(count)]
    own_ref, other_ref = refs[3 * count : 3 * count + 2]
    windows = refs[3 * count + 2 : 4 * count + 2]
    flipped_grad, total = refs[4 * count + 2 :]
    rows, cols, depth = grad_ref.shape
    owned = own_ref.shape[2]
    chips = own_ref.shape[0]
    span = span_of(cols)
    for part, window_ref in zip(parts, windows):
        fill_by_loop(window_ref, part, cols, span)
    flat = []
    for row in range(rows):
        flat += [grad_ref[row], jnp.zeros((span - cols, depth), BF)]
    flipped_grad[...] = jnp.concatenate(flat, 0).T

    def visit(tap, carry):
        start = pl.multiple_of((tap // 3) * span, 16)
        across = lax.rem(tap, 3)
        first = 0
        for window_ref in windows:
            window = window_ref[across, pl.ds(start, rows * span)]
            total[:, first : first + window.shape[1]] = jnp.dot(
                flipped_grad[...], window, preferred_element_type=F32
            )
            first += window.shape[1]
        for shift in range(chips):
            chip = lax.rem(place_ref[0] + shift, chips)
            for ref, core in ((own_ref, place_ref[1]), (other_ref, 1 - place_ref[1])):
                half = pl.multiple_of((2 * chip + core) * owned, 8)
                ref[shift, tap] = total[pl.ds(half, owned)].astype(BF)
        return carry

    lax.fori_loop(0, 9, visit, 0)


def taps(place, parts, widths, grad, chips):
    rows, cols, depth = grad.shape
    channels = sum(widths)
    span = span_of(cols)
    flat = [array for part in parts for array in part]
    half = jax.ShapeDtypeStruct((chips, 9, depth // chips // 2, channels), BF)
    return pl.pallas_call(
        functools.partial(taps_kernel, widths=widths),
        in_specs=[pl.BlockSpec(memory_space=pltpu.SMEM)]
        + [pl.BlockSpec(memory_space=pltpu.VMEM)] * (1 + len(flat)),
        out_specs=[pl.BlockSpec(memory_space=pltpu.VMEM)] * 2,
        out_shape=[half, half],
        scratch_shapes=[window_scratch(part, width, span) for part, width in zip(parts, widths)]
        + [pltpu.VMEM((depth, rows * span), BF), pltpu.VMEM((depth, channels), F32)],
        compiler_params=pltpu.CompilerParams(vmem_limit_bytes=28 << 20),
        cost_estimate=SHORT,
        name="taps",
    )(place, grad, *flat)


def settle_kernel(*refs):
    out_ref = refs[-1]
    rows, cols = out_ref.shape[:2]
    total = refs[0][...].astype(F32)
    for ref in refs[1:-1]:
        total = total + ref[...].astype(F32)
    parts = total.shape[0]
    flat = jnp.concatenate([total[part].T for part in range(parts)], 0)
    spare = jnp.zeros((cols, out_ref.shape[2] - flat.shape[1]), F32)
    for row in range(rows):
        line = flat[row * cols : (row + 1) * cols]
        out_ref[row] = jnp.concatenate([line, spare], 1).astype(BF)


def settle(parts, rows, cols):
    return pl.pallas_call(
        settle_kernel,
        in_specs=[pl.BlockSpec(memory_space=pltpu.VMEM)] * len(parts),
        out_specs=pl.BlockSpec(memory_space=pltpu.VMEM),
        out_shape=jax.ShapeDtypeStruct((rows, cols, LANES), BF),
        compiler_params=pltpu.CompilerParams(vmem_limit_bytes=32 << 20),
        name="settle",
    )(*parts)


def split_bits(value):
    pieces = []
    for _ in range(3):
        piece = value.astype(BF).astype(F32)
        pieces.append(piece)
        value = value - piece
    return pieces


def join_kernel(mixed_ref, loss_ref, *refs, hidden_width):
    parts = refs[:-2]
    share_ref, out_ref = refs[-2:]
    total = parts[0][...].astype(F32)
    for part in parts[1:]:
        total = total + part[...].astype(F32)
    share_ref[...] = total.astype(BF)
    square = jnp.sum(total * total, axis=0, keepdims=True)
    scalars = [
        jnp.sum(square[:, hidden_width:], axis=1, keepdims=True),
        jnp.sum(square[:, :hidden_width], axis=1, keepdims=True),
        loss_ref[...],
    ]
    mixed = jnp.sum(mixed_ref[...].astype(F32), axis=0)
    shape = (mixed.shape[0], LANES)
    lane = lax.broadcasted_iota(jnp.int32, shape, 1)
    row = jnp.zeros(shape, F32)
    for k, scalar in enumerate(scalars):
        for j, piece in enumerate(split_bits(scalar)):
            row = jnp.where(lane == 3 * k + j, piece, row)
    block = jnp.concatenate([mixed, row], 1).astype(BF)

    def store(device, carry):
        out_ref[device] = block
        return carry

    lax.fori_loop(0, out_ref.shape[0], store, 0)


def join_shares(mixed, loss, parts, hidden_width):
    devices, rows, width = mixed.shape
    return pl.pallas_call(
        functools.partial(join_kernel, hidden_width=hidden_width),
        in_specs=[pl.BlockSpec(memory_space=pltpu.VMEM)] * (2 + len(parts)),
        out_specs=[pl.BlockSpec(memory_space=pltpu.VMEM)] * 2,
        out_shape=[
            jax.ShapeDtypeStruct(parts[0].shape, BF),
            jax.ShapeDtypeStruct((devices, rows, width + LANES), BF),
        ],
        compiler_params=pltpu.CompilerParams(vmem_limit_bytes=16 << 20),
        name="join_shares",
    )(mixed, loss.reshape(1, 1), *parts)


def stage_kernel(after_ref, *refs):
    count = (len(refs) - 1) // 2
    sems = refs[-1]
    copies = [
        pltpu.make_async_copy(refs[k], refs[count + k], sems.at[k]) for k in range(count)
    ]
    for copy in copies:
        copy.start()
    for copy in copies:
        copy.wait()


def stage(after, arrays):
    return pl.pallas_call(
        stage_kernel,
        in_specs=[pl.BlockSpec(memory_space=pltpu.VMEM)]
        + [pl.BlockSpec(memory_space=pl.ANY)] * len(arrays),
        out_specs=[pl.BlockSpec(memory_space=pltpu.VMEM)] * len(arrays),
        out_shape=[jax.ShapeDtypeStruct(array.shape, array.dtype) for array in arrays],
        scratch_shapes=[pltpu.SemaphoreType.DMA((len(arrays),))],
        compiler_params=pltpu.CompilerParams(vmem_limit_bytes=16 << 20),
        cost_estimate=SHORT,
        name="stage",
    )(after, *arrays)


def update_kernel(place_ref, shared_ref, norm_ref, count_ref, *refs, shapes, rates, pieces):
    pieces_refs, refs = refs[:pieces], refs[pieces:]
    states, outputs = refs[:18], refs[18:38]
    mixed_ref, taps_scratch, load_sem, store_sem = refs[38:42]
    held = refs[42:]
    loads = [
        pltpu.make_async_copy(state, buffer, load_sem.at[k])
        for k, (state, buffer) in enumerate(zip(states, held))
    ]
    for load in loads:
        load.start()
    share, width = shared_ref.shape[1], mixed_ref.shape[1]
    for device in range(shared_ref.shape[0]):
        mixed_ref[device * share : (device + 1) * share] = shared_ref[device, :, :width].astype(F32)
    depth_bins, cam_width, classes, hidden_width = shapes
    if pieces > 1:
        for shift, ref in enumerate(pieces_refs):
            taps_scratch[lax.rem(place_ref[2] + (pieces - shift), pieces)] = ref[...].astype(F32)
        taps_ref = taps_scratch[...].reshape(9, held[3].shape[1], taps_scratch.shape[2])
    else:
        taps_ref = pieces_refs[0][...]
    mixed = mixed_ref[...]
    column = LANES + cam_width
    edge = taps_ref.shape[2] - cam_width
    grads = [
        jnp.concatenate([mixed[:depth_bins], mixed[LANES:column]], 0),
        jnp.concatenate([taps_ref[:, :, edge:], taps_ref[:, :, hidden_width:edge]], 2),
        taps_ref[:, :, :hidden_width],
        mixed[column : column + classes],
        norm_ref[...],
        mixed[column + classes : column + classes + 1, :classes],
    ]
    sums = jnp.sum(shared_ref[:, :1, width:].astype(F32), axis=0)
    lane = lax.broadcasted_iota(jnp.int32, sums.shape, 1)
    squared = [None if k in (1, 2) else jnp.sum(grad * grad) for k, grad in enumerate(grads)]
    squared[1] = jnp.sum(jnp.where(lane < 3, sums, 0.0))
    squared[2] = jnp.sum(jnp.where((lane >= 3) & (lane < 6), sums, 0.0))
    loss_sum = jnp.sum(jnp.where((lane >= 6) & (lane < 9), sums, 0.0), axis=1, keepdims=True)
    loss_ref, norms_ref = outputs[:2]
    loss_ref[...] = loss_sum / count_ref[...]
    stores = [
        pltpu.make_async_copy(buffer, output, store_sem.at[k])
        for k, (buffer, output) in enumerate(zip(held, outputs[2:]))
    ]
    norms = jnp.zeros((1, LANES), F32)
    spot = lax.broadcasted_iota(jnp.int32, norms.shape, 1)
    for k, grad in enumerate(grads):
        size = jnp.sqrt(jnp.full((1, LANES), squared[k], F32))
        norms = jnp.where(spot == k, jnp.log(size), norms)
        factor = CLIP_NORM / jnp.maximum(size, CLIP_NORM)
        factor = jnp.max(factor)
        group = range(3 * k, 3 * k + 3)
        for j in group:
            loads[j].wait()
        weight, first, second = (held[j][...] for j in group)
        results = adamw(weight, grad * factor, first, second, rates[k], STEP)
        for j, result in zip(group, results):
            held[j][...] = result
            stores[j].start()
    norms_ref[...] = norms
    for store in stores:
        store.wait()


def update(place, shared, pieces, norm, positives, states, shapes, rates):
    args = [place, shared, norm, positives.reshape(1, 1)] + pieces + states
    count = len(pieces)
    width = norm.shape[1]
    return pl.pallas_call(
        functools.partial(update_kernel, shapes=shapes, rates=rates, pieces=count),
        in_specs=[pl.BlockSpec(memory_space=pltpu.SMEM)]
        + [pl.BlockSpec(memory_space=pltpu.VMEM)] * (3 + count)
        + [pl.BlockSpec(memory_space=pl.ANY)] * 18,
        out_specs=[pl.BlockSpec(memory_space=pltpu.VMEM)] * 2
        + [pl.BlockSpec(memory_space=pl.ANY)] * 18,
        out_shape=[jax.ShapeDtypeStruct((1, 1), F32), jax.ShapeDtypeStruct((1, LANES), F32)]
        + [jax.ShapeDtypeStruct(state.shape, F32) for state in states],
        scratch_shapes=[
            pltpu.VMEM((2 * LANES, width), F32),
            pltpu.VMEM((count, *pieces[0].shape[-2:]), F32),
            pltpu.SemaphoreType.DMA((18,)),
            pltpu.SemaphoreType.DMA((18,)),
        ]
        + [pltpu.VMEM(state.shape, F32) for state in states],
        compiler_params=pltpu.CompilerParams(vmem_limit_bytes=60 << 20),
        name="update",
    )(*args)


def swapped(tensor):
    strips = lax.axis_size("strip")
    return lax.ppermute(tensor, "strip", [(i, i ^ 1) for i in range(strips)])


def halves_summed(own, other):
    return own.astype(F32) + swapped(other).astype(F32)


def moved(tensor, shift):
    strips = lax.axis_size("strip")
    return lax.ppermute(tensor, "strip", [(i, (i + 2 * shift) % strips) for i in range(strips)])


def far_first(chips):
    return sorted(range(1, chips), key=lambda shift: -min(shift, chips - shift))


def along_chips(tensor):
    chips = tensor.shape[0]
    arrived = {shift: moved(tensor[shift], shift) for shift in far_first(chips)}
    return [tensor[0]] + [arrived[shift] for shift in range(1, chips)]


def total_of(parts):
    total = parts[0].astype(F32)
    for part in parts[1:]:
        total = total + part.astype(F32)
    return total


def from_chips(tensor):
    chips = lax.axis_size("strip") // 2
    arrived = {shift: moved(tensor, shift) for shift in far_first(chips)}
    return [tensor] + [arrived[shift] for shift in range(1, chips)]


def arrange_kernel(place_ref, mine_ref, theirs_ref, *outs):
    chips, taps_total, owned = mine_ref.shape[:3]
    for chip in range(chips):
        shift = lax.rem(place_ref[0] + (chips - chip), chips)
        for core in range(2):
            start = (2 * chip + core) * owned

            def copy(ref):
                first = 0
                for out_ref in outs:
                    width = out_ref.shape[2]

                    def one(tap, carry, out_ref=out_ref, first=first, width=width):
                        out_ref[tap, start : start + owned] = ref[
                            shift, tap, :, first : first + width
                        ]
                        return carry

                    lax.fori_loop(0, taps_total, one, 0)
                    first += width

            pl.when(place_ref[1] == core)(functools.partial(copy, mine_ref))
            pl.when(place_ref[1] != core)(functools.partial(copy, theirs_ref))


def arrange(place, mine, theirs, widths):
    chips, taps_total, owned = mine.shape[:3]
    return pl.pallas_call(
        arrange_kernel,
        in_specs=[pl.BlockSpec(memory_space=pltpu.SMEM)]
        + [pl.BlockSpec(memory_space=pltpu.VMEM)] * 2,
        out_specs=[pl.BlockSpec(memory_space=pltpu.VMEM)] * len(widths),
        out_shape=[
            jax.ShapeDtypeStruct((taps_total, 2 * chips * owned, width), BF) for width in widths
        ],
        compiler_params=pltpu.CompilerParams(vmem_limit_bytes=32 << 20),
        cost_estimate=SHORT,
        name="arrange",
    )(place, mine, theirs)


def moments(stats, cells, border):
    shared = lax.all_to_all(stats, ("batch", "strip"), 0, 0)
    if border:
        shared, border = lax.optimization_barrier((shared, border))
    centers = shared[:, 0]
    total = jnp.mean(centers, axis=0)
    spread_mean = jnp.mean(shared[:, 1] / cells + (centers - total) ** 2, axis=0)
    return (total, lax.rsqrt(spread_mean + EPS_NORM), jnp.sum(shared[:, 2, 0]), border)


def grad_sums(sums, first, last, later, meanwhile):
    border = edges(first, last)
    shared = lax.all_to_all(sums, ("batch", "strip"), 0, 0)
    later = meanwhile(*later)
    shared, border, later = lax.optimization_barrier((shared, border, later))
    grad_shift, grad_gain = jnp.sum(shared, axis=0)
    return (grad_gain, grad_shift, border, later)


def over_batch(tensor, shift):
    count = lax.axis_size("batch")
    if shift == 0:
        return tensor
    return lax.ppermute(tensor, "batch", [(i, (i + shift) % count) for i in range(count)])


def adamw(weight, gradient, first, second, rate, step_value):
    first = 0.9 * first + 0.1 * gradient
    second = 0.999 * second + 0.001 * gradient * gradient
    fix_one = 1.0 / (1.0 - 0.9**step_value)
    fix_two = 1.0 / (1.0 - 0.999**step_value)
    update = first * fix_one / (jnp.sqrt(second * fix_two) + 1e-08) + 0.01 * weight
    return (weight - rate * update, first, second)


def shards(
    camera_features,
    lidar_bev,
    pool_index,
    box_peaks,
    box_count,
    w_depth,
    m_depth,
    v_depth,
    w_join,
    m_join,
    v_join,
    w_res,
    m_res,
    v_res,
    w_head,
    m_head,
    v_head,
    norm_params,
    m_norm,
    v_norm,
    head_bias,
    m_bias,
    v_bias,
):
    samples, row_local, col_total, lidar_width = lidar_bev.shape
    strips = lax.axis_size("strip")
    row_total = row_local * strips
    cell_total = float(samples * lax.axis_size("batch") * row_total * col_total)
    depth_bins = pool_index.shape[2]
    classes = w_head.shape[1]
    owned = w_join.shape[3]
    cam_width = w_depth.shape[1] - depth_bins
    first_row = lax.axis_index("strip") * row_local
    place = lax.axis_index("strip")
    place = jnp.stack([place // 2, place % 2, lax.axis_index("batch")]).astype(jnp.int32)
    hidden_width = w_res.shape[2]
    taps_low = jnp.concatenate(
        [
            jnp.swapaxes(part, 2, 3).reshape(9, owned, -1)
            for part in (w_res, w_join[:, :, cam_width:], w_join[:, :, :cam_width])
        ],
        axis=2,
    ).astype(BF)
    taps_low = jnp.pad(taps_low, ((0, 0), (0, 0), (0, LANES - cam_width)))
    if owned % 16 == 0:
        taps_mine = from_chips(taps_low)
    strip_cells = row_local * col_total
    layout = plan(camera_features.shape[1], strips, strip_cells)
    own, other, dense, both_low = pool(
        place, camera_features[0], pool_index[0], w_depth.T, layout
    )
    if owned % 16 == 0:
        other, taps_mine = lax.optimization_barrier((other, taps_mine))
    pooled_halves = halves_summed(own, other).astype(BF)
    pooled = along_chips(pooled_halves)
    widths = [hidden_width, lidar_width, LANES]
    if owned % 16 == 0:
        taps_mine = jnp.stack(taps_mine)
        taps_full = arrange(place, taps_mine, swapped(taps_mine), widths)
    else:
        gathered = lax.all_gather(taps_low, "strip", axis=1, tiled=True)
        taps_full = jnp.split(gathered, [hidden_width, hidden_width + lidar_width], axis=2)
    lidar_parts = halo(lidar_bev[0])
    gaps = nearest_gaps(
        box_peaks[0], box_count, first_row, row_local, col_total, classes
    )
    pooled, gaps, taps_full, lidar_parts = lax.optimization_barrier(
        (pooled, gaps, taps_full, lidar_parts)
    )
    wide_out = jax.ShapeDtypeStruct((row_local, col_total, hidden_width), F32)
    axes = ("batch", "strip")
    devices = lax.axis_size(axes)
    stats_out = jax.ShapeDtypeStruct((devices, 3, hidden_width), F32)
    camera_parts = halo(settle(pooled, row_local, col_total))
    join_out, stats = convolve(
        [lidar_parts, camera_parts],
        taps_full[1:],
        False,
        keep_moments,
        [wide_out, stats_out],
        [gaps],
    )
    cells = float(strip_cells)
    center_one, scale_one, positives, join_border = moments(
        stats, cells, edges(join_out[:1], join_out[-1:])
    )

    def norm_one(values):
        return (values - center_one) * scale_one

    def act_of(values):
        return jax.nn.silu(norm_one(values) * norm_params[0] + norm_params[1]).astype(BF)

    act_parts = with_edges(act_of, [join_out], [join_border])
    act_one = act_parts[1]
    res_out, stats = convolve(
        [act_parts], taps_full[:1], False, keep_moments, [wide_out, stats_out]
    )
    center_two, scale_two, unused_term, unused_border = moments(stats, cells, ())

    def norm_two(values):
        return (values - center_two) * scale_two

    vectors = jnp.stack([center_two, scale_two, norm_params[2], norm_params[3]])
    grad_summed, sums, local_loss, grad_head = run_head(
        vectors,
        res_out,
        act_one,
        w_head.T.astype(BF),
        head_bias[:, None],
        gaps,
        positives.reshape(1, 1),
        devices,
    )
    shared = lax.all_to_all(sums, axes, 0, 0)
    shift_two, gain_two = jnp.sum(shared, axis=0)

    def grad_res_of(grad, values):
        spare = grad - shift_two / cell_total - norm_two(values) * gain_two / cell_total
        return (norm_params[2] * scale_two * spare).astype(BF)

    res_parts = halo(grad_res_of(grad_summed, res_out))
    line_out = jax.ShapeDtypeStruct((1, col_total, hidden_width), F32)
    sums_out = jax.ShapeDtypeStruct((devices, 2, hidden_width), F32)
    vectors = jnp.stack([center_one, scale_one, norm_params[0], norm_params[1]])
    grad_pre, grad_first, grad_last, sums = convolve(
        [res_parts],
        taps_full[:1],
        True,
        keep_grad,
        [wide_out, line_out, line_out, sums_out],
        [grad_summed, join_out, vectors],
    )
    gain_one, shift_one, pre_border, (own_res, other_res) = grad_sums(
        sums,
        grad_first,
        grad_last,
        (res_parts[1],),
        lambda grad: taps(place, [act_parts], [hidden_width], grad, strips // 2),
    )

    def grad_join_of(grad, values):
        spare = grad - shift_one / cell_total - norm_one(values) * gain_one / cell_total
        return (norm_params[0] * scale_one * spare).astype(BF)

    join_parts = with_edges(grad_join_of, [grad_pre, join_out], [pre_border, join_border])
    cells_out = jax.ShapeDtypeStruct((layout["per_strip"], cam_width, LANES), BF)
    (grad_cells,) = convolve(
        [join_parts], taps_full[2:], True, keep_cells, [cells_out]
    )
    grad_cells, join_late = lax.optimization_barrier((grad_cells, join_parts[1]))
    grid_parts = from_chips(grad_cells)
    own_join, other_join = taps(
        place,
        [lidar_parts, camera_parts],
        [lidar_width, cam_width],
        join_late,
        strips // 2,
    )
    grid_parts, own_join, other_join = lax.optimization_barrier((grid_parts, own_join, other_join))
    grid_mine = jnp.stack(grid_parts)
    grid_theirs = swapped(grid_mine)
    grads = jnp.concatenate(
        [halves_summed(own_res, other_res), halves_summed(own_join, other_join)], axis=-1
    )
    taps_parts = along_chips(grads.astype(BF))
    grad_both = unpool(
        place,
        camera_features[0],
        pool_index[0],
        both_low,
        dense,
        grid_mine,
        grid_theirs,
        grad_head,
        layout,
    )
    grad_both, taps_parts = lax.optimization_barrier((grad_both, taps_parts))
    members = lax.axis_size("batch")
    member = lax.axis_index("batch")
    quarters = total_of(taps_parts).astype(BF).reshape(members, -1, (hidden_width + lidar_width + cam_width))
    parts = [
        over_batch(lax.dynamic_index_in_dim(quarters, (member + s) % members, 0, False), s)
        for s in range(members)
    ]
    width = w_depth.shape[0]
    mixed = grad_both.reshape(devices, -1, width)
    mixed = lax.all_to_all(mixed, axes, 0, 0)
    share, shared = join_shares(mixed, local_loss, parts, hidden_width)
    shared = lax.all_to_all(shared, axes, 0, 0)
    pieces = [over_batch(share, s) for s in range(members)]
    if share.shape[0] % 8:
        order = (member - jnp.arange(members)) % members
        pieces = [jnp.take(jnp.stack(pieces), order, axis=0).reshape(9, owned, -1).astype(F32)]
    grad_norm = jnp.stack([gain_one, shift_one, gain_two, shift_two])
    rates = [
        0.5 * w_depth.shape[0] ** (-0.5),
        0.5 * (9 * w_join.shape[2]) ** (-0.5),
        0.5 * (9 * w_res.shape[2]) ** (-0.5),
        0.5 * w_head.shape[0] ** (-0.5),
        SMALL_RATE,
        SMALL_RATE,
    ]
    weights = [w_depth, w_join, w_res, w_head, norm_params, head_bias]
    firsts = [m_depth, m_join, m_res, m_head, m_norm, m_bias]
    seconds = [v_depth, v_join, v_res, v_head, v_norm, v_bias]
    views = [
        jnp.transpose,
        lambda state: jnp.swapaxes(state, 2, 3).reshape(9, owned, -1),
        lambda state: jnp.swapaxes(state, 2, 3).reshape(9, owned, -1),
        jnp.transpose,
        lambda state: state,
        lambda state: state[None],
    ]
    backs = [
        jnp.transpose,
        lambda state: jnp.swapaxes(state.reshape(3, 3, owned, -1), 2, 3),
        lambda state: jnp.swapaxes(state.reshape(3, 3, owned, -1), 2, 3),
        jnp.transpose,
        lambda state: state,
        lambda state: state[0],
    ]
    states = [
        view(state)
        for view, group in zip(views, zip(weights, firsts, seconds))
        for state in group
    ]
    loss, norms, *states = update(
        place,
        shared,
        pieces,
        grad_norm,
        positives,
        states,
        (depth_bins, cam_width, classes, hidden_width),
        rates,
    )
    result = [loss[0], norms[0, :6]]
    for k, state in enumerate(states):
        result.append(backs[k // 3](state))
    return tuple(result)


def solution(mesh):
    in_specs = (
        P("batch", "strip", None),
        P("batch", "strip", None, None),
        P("batch", "strip", None),
        P("batch", None, None),
        P("batch"),
        P(),
        P(),
        P(),
        P(None, None, None, "strip"),
        P(None, None, None, "strip"),
        P(None, None, None, "strip"),
        P(None, None, None, "strip"),
        P(None, None, None, "strip"),
        P(None, None, None, "strip"),
        P(),
        P(),
        P(),
        P(),
        P(),
        P(),
        P(),
        P(),
        P(),
    )
    out_specs = (
        P(),
        P(),
        P(),
        P(),
        P(),
        P(None, None, None, "strip"),
        P(None, None, None, "strip"),
        P(None, None, None, "strip"),
        P(None, None, None, "strip"),
        P(None, None, None, "strip"),
        P(None, None, None, "strip"),
        P(),
        P(),
        P(),
        P(),
        P(),
        P(),
        P(),
        P(),
        P(),
    )
    return jax.shard_map(shards, mesh=mesh, in_specs=in_specs, out_specs=out_specs, check_vma=False)
```

```python
import functools

import jax
import jax.numpy as jnp
from jax import lax
from jax.experimental import pallas as pl
from jax.experimental.pallas import tpu as pltpu
from jax.sharding import PartitionSpec as P

STEP = 5


EPS_NORM = 1e-05
SPREAD_TWICE = 8.0
SMALL_RATE = 0.25
CLIP_NORM = 0.01
FAR = 1e9


def edges(first, last):
    peers = lax.axis_size("strip")
    up = [(i, i + 1) for i in range(peers - 1)]
    before = lax.ppermute(last, "strip", up)
    after = lax.ppermute(first, "strip", [(j, i) for i, j in up])
    return before, after


def halo(shard):
    before, after = edges(shard[:1], shard[-1:])
    return [before, shard, after]


def with_edges(function, shards, borders):
    place = lax.axis_index("strip")
    inside = [place > 0, place < lax.axis_size("strip") - 1]
    sides = [
        jnp.where(there, function(*side), 0).astype(BF)
        for there, side in zip(inside, zip(*borders))
    ]
    return [sides[0], function(*shards), sides[1]]


def target_kernel(peaks_ref, count_ref, first_ref, gap_ref):
    gap_ref[...] = jnp.full(gap_ref.shape, FAR, jnp.float32)
    shape = gap_ref.shape[1:]
    row_ids = lax.broadcasted_iota(jnp.int32, shape, 0) + first_ref[0]
    col_ids = lax.broadcasted_iota(jnp.int32, shape, 1)

    def visit(slot, carry):
        row_gap = row_ids - peaks_ref[0, slot]
        col_gap = col_ids - peaks_ref[1, slot]
        distance = (row_gap * row_gap + col_gap * col_gap).astype(jnp.float32)
        kind = peaks_ref[2, slot]
        gap_ref[kind] = jnp.minimum(gap_ref[kind], distance)
        return carry

    lax.fori_loop(0, count_ref[0], visit, 0)


def nearest_gaps(box_peaks, box_count, first_row, row_total, col_total, classes):
    return pl.pallas_call(
        target_kernel,
        in_specs=[pl.BlockSpec(memory_space=pltpu.SMEM)] * 3,
        out_specs=pl.BlockSpec(memory_space=pltpu.VMEM),
        out_shape=jax.ShapeDtypeStruct((classes, row_total, col_total), jnp.float32),
        cost_estimate=SHORT,
        name="targets",
    )(box_peaks, box_count, first_row[None])


LANES = 128
SHORT = pl.CostEstimate(flops=1000, bytes_accessed=1000, transcendentals=0)
BF = jnp.bfloat16
F32 = jnp.float32


def plan(pixels, strips, strip_cells):
    per_strip = -(-strip_cells // LANES)
    high = strips * per_strip
    block = 352 if pixels % 352 == 0 and high <= 128 else 48
    return dict(
        per_strip=per_strip,
        high=high,
        offset=high // 2,
        block=block,
        stride=block + 4,
        group=block,
        strip_cells=strip_cells,
    )


def split_cells(index, plan):
    cell = index.astype(F32)
    strip = jnp.floor((cell + 0.5) * (1.0 / plan["strip_cells"]))
    rest = cell - strip * plan["strip_cells"]
    part = jnp.floor((rest + 0.5) * (1.0 / LANES))
    return strip * plan["per_strip"] + part - plan["offset"], rest - part * LANES


def softmax_lanes(logits, bins):
    lane = lax.broadcasted_iota(jnp.int32, logits.shape, 1)
    logits = jnp.where(lane < bins, logits, -jnp.inf)
    powers = jnp.exp(logits - jnp.max(logits, axis=1, keepdims=True))
    return powers / jnp.sum(powers, axis=1, keepdims=True)


def spread(ref, pixel, rows=16):
    return jnp.broadcast_to(ref[pl.ds(pixel, 1), :], (rows, LANES))


def one_hot(row, value, rows, offset=0):
    base = (lax.broadcasted_iota(jnp.int32, (rows, LANES), 0) - offset).astype(F32).astype(BF)
    none = jnp.zeros((16, LANES), BF)
    return [
        jnp.where(base[k : k + 16] == row, value, none) for k in range(0, rows, 16)
    ]


def high_pair(high_ref, depth_ref, first, plan):
    whole = plan["high"] // 16 * 16
    parts = []
    for j in range(2):
        row = spread(high_ref, first + j).astype(BF)
        value = spread(depth_ref, first + j).astype(BF)
        parts += one_hot(row, value, whole, plan["offset"])
    if whole < plan["high"]:
        both = [
            jnp.concatenate([spread(ref, first, 8), spread(ref, first + 1, 8)], 0).astype(BF)
            for ref in (high_ref, depth_ref)
        ]
        base = lax.broadcasted_iota(jnp.int32, (16, LANES), 0)
        base = jnp.where(base < 8, base, base - 8) + (whole - plan["offset"])
        none = jnp.zeros((16, LANES), BF)
        parts.append(jnp.where(base.astype(F32).astype(BF) == both[0], both[1], none))
    return jnp.concatenate(parts, 0)


def pool_kernel(place_ref, feat_ref, index_ref, weight_ref, own_ref, other_ref, dense_ref, both_ref, high_ref, low_ref, depth_ref, held, total, *, plan):
    bins = index_ref.shape[1]
    block, stride, high = (plan[k] for k in ("block", "stride", "high"))
    step = pl.program_id(0)

    @pl.when(step == 0)
    def _():
        high_ref[...] = jnp.zeros_like(high_ref)
        low_ref[...] = jnp.zeros_like(low_ref)
        total[...] = jnp.zeros_like(total)
        channels = total.shape[1]
        both_ref[...] = jnp.zeros_like(both_ref)
        both_ref[:bins] = weight_ref[:bins].astype(BF)
        both_ref[LANES : LANES + channels] = weight_ref[bins : bins + channels].astype(BF)

    feat = feat_ref[...]
    logits = lax.dot_general(feat, both_ref[:LANES], (((1,), (1,)), ((), ())), preferred_element_type=F32)
    depth_ref[...] = softmax_lanes(logits, bins)
    channels = total.shape[1]
    context_low = both_ref[LANES : LANES + channels]
    context = lax.dot_general(context_low, feat, (((1,), (1,)), ((), ())), preferred_element_type=F32).astype(BF)
    high_id, low_id = split_cells(index_ref[...], plan)
    high_ref[:, :bins] = high_id
    low_ref[:, :bins] = low_id
    one = jnp.ones((16, LANES), BF)

    def scatter(group, carry):
        for k in range(0, plan["group"], 2):
            first = group * plan["group"] + k
            left = high_pair(high_ref, depth_ref, first, plan)
            right = []
            for j in range(2):
                low = spread(low_ref, first + j).astype(BF)
                right.append(jnp.concatenate(one_hot(low, one, LANES), 0))
            tile = lax.dot_general(
                left, jnp.concatenate(right, 0), (((1,), (1,)), ((), ())), preferred_element_type=F32
            )
            whole = high // 16 * 16
            for j in range(2):
                part = tile[:, j * LANES : (j + 1) * LANES]
                held[pl.ds(first + j, whole, stride=stride), :] = part[j * whole : (j + 1) * whole]
                if whole < high:
                    held[pl.ds(first + j + whole * stride, 8, stride=stride), :] = part[
                        2 * whole + 8 * j : 2 * whole + 8 * j + 8
                    ]
        return carry

    lax.fori_loop(0, block // plan["group"], scatter, 0)

    def gather(k, carry):
        parts = []
        for j in range(2):
            part = held[pl.ds((k * 2 + j) * stride, block), :].astype(BF)
            dense_ref[k * 2 + j] = part
            parts.append(part)
        out = jnp.dot(context, jnp.concatenate(parts, 1), preferred_element_type=F32)
        for j in range(2):
            total[k * 2 + j] += out[:, j * LANES : (j + 1) * LANES]
        return carry

    lax.fori_loop(0, high // 2, gather, 0, unroll=36)

    @pl.when(step == pl.num_programs(0) - 1)
    def _():
        count = plan["per_strip"]
        chips = own_ref.shape[0]
        for shift in range(chips):
            chip = lax.rem(place_ref[0] + shift, chips)
            for ref, core in ((own_ref, place_ref[1]), (other_ref, 1 - place_ref[1])):
                first = (2 * chip + core) * count
                ref[shift] = total[pl.ds(first, count)].astype(BF)


def pool(place, features, index, weight, plan):
    pixels, width = features.shape
    bins = index.shape[1]
    channels = weight.shape[0] - bins
    block, high = plan["block"], plan["high"]
    halves = (high // plan["per_strip"] // 2, plan["per_strip"], channels, LANES)
    return pl.pallas_call(
        functools.partial(pool_kernel, plan=plan),
        grid=(pixels // block,),
        in_specs=[
            pl.BlockSpec(memory_space=pltpu.SMEM),
            pl.BlockSpec((block, width), lambda i: (i, 0)),
            pl.BlockSpec((block, bins), lambda i: (i, 0)),
            pl.BlockSpec(weight.shape, lambda i: (0, 0)),
        ],
        out_specs=[
            pl.BlockSpec(halves, lambda i: (0, 0, 0, 0)),
            pl.BlockSpec(halves, lambda i: (0, 0, 0, 0)),
            pl.BlockSpec((high, block, LANES), lambda i: (0, i, 0)),
            pl.BlockSpec((2 * LANES, width), lambda i: (0, 0)),
        ],
        out_shape=[
            jax.ShapeDtypeStruct(halves, BF),
            jax.ShapeDtypeStruct(halves, BF),
            jax.ShapeDtypeStruct((high, pixels, LANES), BF),
            jax.ShapeDtypeStruct((2 * LANES, width), BF),
        ],
        scratch_shapes=[pltpu.VMEM((block, LANES), F32)] * 3
        + [
            pltpu.VMEM((high * plan["stride"], LANES), F32),
            pltpu.VMEM((high, channels, LANES), F32),
        ],
        compiler_params=pltpu.CompilerParams(vmem_limit_bytes=40 << 20),
        cost_estimate=pl.CostEstimate(
            flops=4 * pixels * high * LANES * LANES,
            bytes_accessed=2 * pixels * high * LANES,
            transcendentals=0,
        ),
        name="pool",
    )(place, features, index, weight)


def unpool_kernel(place_ref, feat_ref, index_ref, both_ref, dense_ref, mine_ref, theirs_ref, head_ref, out_ref, high_ref, low_ref, pick_ref, held, sum_ref, grid_ref, grad_ref, *, plan):
    bins = index_ref.shape[1]
    channels = grid_ref.shape[1]
    chips, count = mine_ref.shape[:2]
    block, stride, high = (plan[k] for k in ("block", "stride", "high"))
    step = pl.program_id(0)

    @pl.when(step == 0)
    def _():
        high_ref[...] = jnp.zeros_like(high_ref)
        low_ref[...] = jnp.zeros_like(low_ref)
        held[...] = jnp.zeros_like(held)
        grad_ref[...] = jnp.zeros_like(grad_ref)
        for shift in range(chips):
            chip = lax.rem(place_ref[0] + (chips - shift), chips)
            for ref, core in ((mine_ref, place_ref[1]), (theirs_ref, 1 - place_ref[1])):
                grid_ref[pl.ds((2 * chip + core) * count, count)] = ref[shift]

    feat = feat_ref[...]
    logits = lax.dot_general(feat, both_ref[...], (((1,), (1,)), ((), ())), preferred_element_type=F32)
    depth = softmax_lanes(logits[:, :LANES], bins)
    context = logits[:, LANES : LANES + channels].astype(BF)
    high_id, low_id = split_cells(index_ref[...], plan)
    high_ref[:, :bins] = high_id
    low_ref[:, :bins] = low_id

    def project(k, carry):
        grid = jnp.concatenate([grid_ref[k * 2], grid_ref[k * 2 + 1]], 1)
        out = jnp.dot(context, grid, preferred_element_type=F32)
        for j in range(2):
            held[pl.ds((k * 2 + j) * stride, block), :] = out[:, j * LANES : (j + 1) * LANES]
        return carry

    lax.fori_loop(0, high // 2, project, 0, unroll=36)
    parts = 72

    def mix(k, carry):
        dense = jnp.concatenate([dense_ref[k * parts + j] for j in range(parts)], 1)
        grid = jnp.concatenate([grid_ref[k * parts + j] for j in range(parts)], 1)
        sum_ref[...] += lax.dot_general(
            dense, grid, (((1,), (1,)), ((), ())), preferred_element_type=F32
        )
        return carry

    sum_ref[...] = jnp.zeros_like(sum_ref)
    lax.fori_loop(0, high // parts, mix, 0)
    one = jnp.ones((16, LANES), BF)
    rows = (lax.broadcasted_iota(jnp.int32, (high, LANES), 0) - plan["offset"]).astype(F32)

    def collect(group, carry):
        for k in range(0, plan["group"], 2):
            first = group * plan["group"] + k
            left, right = [], []
            for j in range(2):
                left.append(held[pl.ds(first + j, high, stride=stride), :])
                low = spread(low_ref, first + j).astype(BF)
                right.append(jnp.concatenate(one_hot(low, one, LANES), 0))
            tile = jnp.dot(jnp.concatenate(left, 0).astype(BF), jnp.concatenate(right, 1), preferred_element_type=F32)
            for j in range(2):
                part = tile[j * high : (j + 1) * high, j * LANES : (j + 1) * LANES]
                kept = jnp.where(rows == high_ref[pl.ds(first + j, 1), :], part, 0.0)
                pick_ref[pl.ds(first + j, 1), :] = jnp.sum(kept, axis=0, keepdims=True)
        return carry

    lax.fori_loop(0, block // plan["group"], collect, 0)
    grad_prob = pick_ref[...]
    grad_context = sum_ref[...]
    grad_depth = depth * (grad_prob - jnp.sum(grad_prob * depth, axis=1, keepdims=True))
    grad_low = jnp.concatenate(
        [grad_depth, grad_context, jnp.zeros((block, LANES - channels), F32)], axis=1
    ).astype(BF)
    grad_ref[...] += lax.dot_general(grad_low, feat, (((0,), (0,)), ((), ())), preferred_element_type=F32)

    @pl.when(step == pl.num_programs(0) - 1)
    def _():
        first = LANES + channels
        rows = head_ref.shape[0]
        out_ref[:first] = grad_ref[:first].astype(BF)
        spare = jnp.zeros((2 * LANES - first - rows, grad_ref.shape[1]), F32)
        out_ref[first:] = jnp.concatenate([head_ref[...], spare], 0).astype(BF)


def unpool(place, features, index, both_low, dense, mine, theirs, head, plan):
    pixels, width = features.shape
    bins = index.shape[1]
    channels = mine.shape[2]
    block, high = plan["block"], plan["high"]
    return pl.pallas_call(
        functools.partial(unpool_kernel, plan=plan),
        grid=(pixels // block,),
        in_specs=[
            pl.BlockSpec(memory_space=pltpu.SMEM),
            pl.BlockSpec((block, width), lambda i: (i, 0)),
            pl.BlockSpec((block, bins), lambda i: (i, 0)),
            pl.BlockSpec(both_low.shape, lambda i: (0, 0)),
            pl.BlockSpec((high, block, LANES), lambda i: (0, i, 0)),
            pl.BlockSpec(mine.shape, lambda i: (0, 0, 0, 0)),
            pl.BlockSpec(theirs.shape, lambda i: (0, 0, 0, 0)),
            pl.BlockSpec(head.shape, lambda i: (0, 0)),
        ],
        out_specs=pl.BlockSpec((2 * LANES, width), lambda i: (0, 0)),
        out_shape=jax.ShapeDtypeStruct((2 * LANES, width), BF),
        scratch_shapes=[pltpu.VMEM((block, LANES), F32)] * 3
        + [
            pltpu.VMEM((high * plan["stride"], LANES), F32),
            pltpu.VMEM((block, channels), F32),
            pltpu.VMEM((high, channels, LANES), BF),
            pltpu.VMEM((2 * LANES, width), F32),
        ],
        compiler_params=pltpu.CompilerParams(vmem_limit_bytes=40 << 20),
        cost_estimate=pl.CostEstimate(
            flops=6 * pixels * high * LANES * LANES,
            bytes_accessed=2 * pixels * high * LANES,
            transcendentals=0,
        ),
        name="unpool",
    )(place, features, index, both_low, dense, mine, theirs, head)


def fill_windows(window_ref, part, cols, span):
    before_ref, shard_ref, after_ref = part
    rows = shard_ref.shape[0]
    width = window_ref.shape[2]
    window_ref[...] = jnp.zeros_like(window_ref)
    for row in range(rows + 2):
        if row == 0:
            line = before_ref[0]
        elif row == rows + 1:
            line = after_ref[0]
        else:
            line = shard_ref[row - 1]
        line = line[:, :width]
        start = row * span
        window_ref[0, start + 1 : start + cols] = line[: cols - 1]
        window_ref[1, start : start + cols] = line
        window_ref[2, start : start + cols - 1] = line[1:]


def window_scratch(part, width, span):
    return pltpu.VMEM((3, (part[1].shape[0] + 2) * span, width), BF)


def span_of(cols):
    return -(-cols // 16) * 16


def conv_kernel(*refs, count, turned, finish):
    kernels = refs[:count]
    parts = [refs[count + 3 * k : count + 3 * k + 3] for k in range(count)]
    rows, cols = parts[0][1].shape[:2]
    span = span_of(cols)
    windows = refs[-count:]
    left, right = [], []
    for part, window_ref, kernel_ref in zip(parts, windows, kernels):
        fill_windows(window_ref, part, cols, span)
        for tap in range(9):
            upward, across = tap // 3, tap % 3
            left.append(window_ref[across, upward * span : (upward + rows) * span])
            right.append(kernel_ref[8 - tap if turned else tap])
    left = jnp.concatenate(left, 1)
    if turned:
        total = jnp.dot(left, jnp.concatenate(right, 0), preferred_element_type=F32)
    else:
        total = lax.dot_general(
            left, jnp.concatenate(right, 1), (((1,), (1,)), ((), ())), preferred_element_type=F32
        )
    finish(total, rows, cols, span, *refs[4 * count : -count])


def keep_rows(total, rows, cols, span, out_ref):
    for row in range(rows):
        out_ref[row] = total[row * span : row * span + cols]


def keep_moments(total, rows, cols, span, *refs):
    out_ref, stats_ref = refs[-2:]
    keep_rows(total, rows, cols, span, out_ref)
    cells = float(rows * cols)
    center = jnp.sum(total, axis=0, keepdims=True) / cells
    spot = lax.broadcasted_iota(jnp.int32, (span, total.shape[1]), 0)
    spread_sum = jnp.zeros_like(center)
    for row in range(rows):
        apart = total[row * span : (row + 1) * span] - center
        apart = jnp.where(spot < cols, apart, 0.0)
        spread_sum = spread_sum + jnp.sum(apart * apart, axis=0, keepdims=True)
    hits = jnp.zeros_like(center)
    for ref in refs[:-2]:
        hits = jnp.full(center.shape, jnp.sum(jnp.where(ref[...] == 0.0, 1.0, 0.0)))
    stats = jnp.concatenate([center, spread_sum, hits], 0)

    def store(device, carry):
        stats_ref[device] = stats
        return carry

    lax.fori_loop(0, stats_ref.shape[0], store, 0)


def keep_grad(total, rows, cols, span, more_ref, norm_in_ref, vector_ref, out_ref, sums_ref):
    center, scale, gain, shift = (vector_ref[k : k + 1] for k in range(4))
    shift_sum = jnp.zeros_like(center)
    gain_sum = jnp.zeros_like(center)
    for row in range(rows):
        normed = (norm_in_ref[row] - center) * scale
        value = normed * gain + shift
        sig = jax.nn.sigmoid(value)
        grad = total[row * span : row * span + cols] + more_ref[row]
        grad = grad * (sig * (1.0 + value * (1.0 - sig)))
        out_ref[row] = grad
        shift_sum = shift_sum + jnp.sum(grad, axis=0, keepdims=True)
        gain_sum = gain_sum + jnp.sum(grad * normed, axis=0, keepdims=True)
    sums = jnp.concatenate([shift_sum, gain_sum], 0)

    def store(device, carry):
        sums_ref[device] = sums
        return carry

    lax.fori_loop(0, sums_ref.shape[0], store, 0)


def head_kernel(vector_ref, res_ref, act_ref, head_ref, bias_ref, gap_ref, count_ref, grad_ref, sums_ref, loss_ref, head_grad_ref):
    rows, cols, width = res_ref.shape
    center, scale, gain, shift = (vector_ref[k : k + 1] for k in range(4))
    head = head_ref[...]
    shift_sum = jnp.zeros_like(center)
    gain_sum = jnp.zeros_like(center)
    head_grad = jnp.zeros(head.shape, F32)
    bias_grad = jnp.zeros((head.shape[0], 1), F32)
    loss = jnp.zeros((head.shape[0], 1), F32)
    for row in range(rows):
        normed = (res_ref[row] - center) * scale
        summed = normed * gain + shift + act_ref[row].astype(F32)
        sig = jax.nn.sigmoid(summed)
        hidden = (summed * sig).astype(BF)
        logits = lax.dot_general(head, hidden, (((1,), (1,)), ((), ())), preferred_element_type=F32)
        logits = logits + bias_ref[...]
        prob = jax.nn.sigmoid(logits)
        tail = jnp.log1p(jnp.exp(-jnp.abs(logits)))
        soft_pos = jnp.maximum(logits, 0.0) + tail
        soft_neg = jnp.maximum(-logits, 0.0) + tail
        gap = gap_ref[:, row, :]
        heatmap = jnp.where(gap < FAR, jnp.exp(-gap / SPREAD_TWICE), 0.0)
        struck = jnp.where(gap == 0.0, 1.0, 0.0)
        weighting = (1.0 - heatmap) * (1.0 - heatmap)
        weighting = weighting * weighting
        miss = 1.0 - prob
        loss_here = struck * miss * miss * soft_neg + weighting * prob * prob * soft_pos
        loss = loss + jnp.sum(loss_here, axis=1, keepdims=True)
        grad_pos = -2.0 * prob * miss * miss * soft_neg - miss * miss * miss
        grad_neg = 2.0 * prob * prob * miss * soft_pos + prob * prob * prob
        grad_logits = (struck * grad_pos + weighting * grad_neg) / count_ref[...]
        grad_logits = grad_logits.astype(BF)
        bias_grad = bias_grad + jnp.sum(grad_logits.astype(F32), axis=1, keepdims=True)
        head_grad = head_grad + jnp.dot(grad_logits, hidden, preferred_element_type=F32)
        grad = lax.dot_general(grad_logits, head, (((0,), (0,)), ((), ())), preferred_element_type=F32)
        grad = grad * (sig * (1.0 + summed * (1.0 - sig)))
        grad_ref[row] = grad
        shift_sum = shift_sum + jnp.sum(grad, axis=0, keepdims=True)
        gain_sum = gain_sum + jnp.sum(grad * normed, axis=0, keepdims=True)
    loss_ref[...] = jnp.sum(loss, axis=0, keepdims=True)
    classes = head.shape[0]
    head_grad_ref[:classes] = head_grad
    down = lax.broadcasted_iota(jnp.int32, head.shape, 0)
    across = lax.broadcasted_iota(jnp.int32, head.shape, 1)
    bias_row = jnp.sum(jnp.where(down == across, bias_grad, 0.0), axis=0, keepdims=True)
    head_grad_ref[classes : classes + 1] = bias_row
    sums = jnp.concatenate([shift_sum, gain_sum], 0)

    def store(device, carry):
        sums_ref[device] = sums
        return carry

    lax.fori_loop(0, sums_ref.shape[0], store, 0)


def run_head(vectors, res_out, act, head_low, bias, gaps, positives, devices):
    rows, cols, width = res_out.shape
    classes = head_low.shape[0]
    shapes = [
        (rows, cols, width),
        (devices, 2, width),
        (1, 1),
        (classes + 1, width),
    ]
    return pl.pallas_call(
        head_kernel,
        in_specs=[pl.BlockSpec(memory_space=pltpu.VMEM)] * 7,
        out_specs=[pl.BlockSpec(memory_space=pltpu.VMEM)] * 4,
        out_shape=[jax.ShapeDtypeStruct(shape, F32) for shape in shapes],
        compiler_params=pltpu.CompilerParams(vmem_limit_bytes=24 << 20),
        name="head",
    )(vectors, res_out, act, head_low, bias, gaps, positives)


def keep_cells(total, rows, cols, span, out_ref):
    cells, channels = out_ref.shape[0] * LANES, out_ref.shape[1]
    flat = [total[row * span : row * span + cols] for row in range(rows)]
    flat.append(jnp.zeros((cells - rows * cols, total.shape[1]), F32))
    flat = jnp.concatenate(flat, 0)
    for part in range(out_ref.shape[0]):
        out_ref[part] = flat[part * LANES : (part + 1) * LANES].T[:channels].astype(BF)


def convolve(parts, kernels, turned, finish, outs, extras=()):
    rows, cols = parts[0][1].shape[:2]
    span = span_of(cols)
    widths = [kernel.shape[1] if turned else kernel.shape[2] for kernel in kernels]
    flat = [array for part in parts for array in part]
    operands = [*kernels, *flat, *extras]
    return pl.pallas_call(
        functools.partial(conv_kernel, count=len(parts), turned=turned, finish=finish),
        in_specs=[pl.BlockSpec(memory_space=pltpu.VMEM)] * len(operands),
        out_specs=[pl.BlockSpec(memory_space=pltpu.VMEM)] * len(outs),
        out_shape=outs,
        scratch_shapes=[
            window_scratch(part, width, span) for part, width in zip(parts, widths)
        ],
        compiler_params=pltpu.CompilerParams(vmem_limit_bytes=32 << 20),
        cost_estimate=pl.CostEstimate(
            flops=18 * rows * span * sum(widths) * kernels[0].shape[1],
            bytes_accessed=2 * sum(kernel.size for kernel in kernels),
            transcendentals=0,
        ),
        name="convolve",
    )(*operands)


def taps_kernel(place_ref, grad_ref, *refs, widths):
    count = len(widths)
    parts = [refs[3 * k : 3 * k + 3] for k in range(count)]
    own_ref, other_ref = refs[3 * count : 3 * count + 2]
    windows = refs[3 * count + 2 : 4 * count + 2]
    flipped_grad, total = refs[4 * count + 2 :]
    rows, cols, depth = grad_ref.shape
    owned = own_ref.shape[2]
    chips = own_ref.shape[0]
    span = span_of(cols)
    for part, window_ref in zip(parts, windows):
        fill_windows(window_ref, part, cols, span)
    flat = []
    for row in range(rows):
        flat += [grad_ref[row], jnp.zeros((span - cols, depth), BF)]
    flipped_grad[...] = jnp.concatenate(flat, 0).T

    def visit(tap, carry):
        start = pl.multiple_of((tap // 3) * span, 16)
        across = lax.rem(tap, 3)
        first = 0
        for window_ref in windows:
            window = window_ref[across, pl.ds(start, rows * span)]
            total[:, first : first + window.shape[1]] = jnp.dot(
                flipped_grad[...], window, preferred_element_type=F32
            )
            first += window.shape[1]
        for shift in range(chips):
            chip = lax.rem(place_ref[0] + shift, chips)
            for ref, core in ((own_ref, place_ref[1]), (other_ref, 1 - place_ref[1])):
                half = pl.multiple_of((2 * chip + core) * owned, 8)
                ref[shift, tap] = total[pl.ds(half, owned)].astype(BF)
        return carry

    lax.fori_loop(0, 9, visit, 0)


def taps(place, parts, widths, grad, chips):
    rows, cols, depth = grad.shape
    channels = sum(widths)
    span = span_of(cols)
    flat = [array for part in parts for array in part]
    half = jax.ShapeDtypeStruct((chips, 9, depth // chips // 2, channels), BF)
    return pl.pallas_call(
        functools.partial(taps_kernel, widths=widths),
        in_specs=[pl.BlockSpec(memory_space=pltpu.SMEM)]
        + [pl.BlockSpec(memory_space=pltpu.VMEM)] * (1 + len(flat)),
        out_specs=[pl.BlockSpec(memory_space=pltpu.VMEM)] * 2,
        out_shape=[half, half],
        scratch_shapes=[window_scratch(part, width, span) for part, width in zip(parts, widths)]
        + [pltpu.VMEM((depth, rows * span), BF), pltpu.VMEM((depth, channels), F32)],
        compiler_params=pltpu.CompilerParams(vmem_limit_bytes=28 << 20),
        cost_estimate=SHORT,
        name="taps",
    )(place, grad, *flat)


def settle_kernel(*refs):
    out_ref = refs[-1]
    rows, cols = out_ref.shape[:2]
    total = refs[0][...].astype(F32)
    for ref in refs[1:-1]:
        total = total + ref[...].astype(F32)
    parts = total.shape[0]
    flat = jnp.concatenate([total[part].T for part in range(parts)], 0)
    spare = jnp.zeros((cols, out_ref.shape[2] - flat.shape[1]), F32)
    for row in range(rows):
        line = flat[row * cols : (row + 1) * cols]
        out_ref[row] = jnp.concatenate([line, spare], 1).astype(BF)


def settle(parts, rows, cols):
    return pl.pallas_call(
        settle_kernel,
        in_specs=[pl.BlockSpec(memory_space=pltpu.VMEM)] * len(parts),
        out_specs=pl.BlockSpec(memory_space=pltpu.VMEM),
        out_shape=jax.ShapeDtypeStruct((rows, cols, LANES), BF),
        compiler_params=pltpu.CompilerParams(vmem_limit_bytes=32 << 20),
        name="settle",
    )(*parts)


def split_bits(value):
    pieces = []
    for _ in range(3):
        piece = value.astype(BF).astype(F32)
        pieces.append(piece)
        value = value - piece
    return pieces


def join_kernel(mixed_ref, loss_ref, *refs, hidden_width):
    parts = refs[:-2]
    share_ref, out_ref = refs[-2:]
    total = parts[0][...].astype(F32)
    for part in parts[1:]:
        total = total + part[...].astype(F32)
    share_ref[...] = total.astype(BF)
    square = jnp.sum(total * total, axis=0, keepdims=True)
    scalars = [
        jnp.sum(square[:, hidden_width:], axis=1, keepdims=True),
        jnp.sum(square[:, :hidden_width], axis=1, keepdims=True),
        loss_ref[...],
    ]
    mixed = jnp.sum(mixed_ref[...].astype(F32), axis=0)
    shape = (mixed.shape[0], LANES)
    lane = lax.broadcasted_iota(jnp.int32, shape, 1)
    row = jnp.zeros(shape, F32)
    for k, scalar in enumerate(scalars):
        for j, piece in enumerate(split_bits(scalar)):
            row = jnp.where(lane == 3 * k + j, piece, row)
    block = jnp.concatenate([mixed, row], 1).astype(BF)

    def store(device, carry):
        out_ref[device] = block
        return carry

    lax.fori_loop(0, out_ref.shape[0], store, 0)


def join_shares(mixed, loss, parts, hidden_width):
    devices, rows, width = mixed.shape
    return pl.pallas_call(
        functools.partial(join_kernel, hidden_width=hidden_width),
        in_specs=[pl.BlockSpec(memory_space=pltpu.VMEM)] * (2 + len(parts)),
        out_specs=[pl.BlockSpec(memory_space=pltpu.VMEM)] * 2,
        out_shape=[
            jax.ShapeDtypeStruct(parts[0].shape, BF),
            jax.ShapeDtypeStruct((devices, rows, width + LANES), BF),
        ],
        compiler_params=pltpu.CompilerParams(vmem_limit_bytes=16 << 20),
        name="join_shares",
    )(mixed, loss.reshape(1, 1), *parts)


def stage_kernel(after_ref, *refs):
    count = (len(refs) - 1) // 2
    sems = refs[-1]
    copies = [
        pltpu.make_async_copy(refs[k], refs[count + k], sems.at[k]) for k in range(count)
    ]
    for copy in copies:
        copy.start()
    for copy in copies:
        copy.wait()


def stage(after, arrays):
    return pl.pallas_call(
        stage_kernel,
        in_specs=[pl.BlockSpec(memory_space=pltpu.VMEM)]
        + [pl.BlockSpec(memory_space=pl.ANY)] * len(arrays),
        out_specs=[pl.BlockSpec(memory_space=pltpu.VMEM)] * len(arrays),
        out_shape=[jax.ShapeDtypeStruct(array.shape, array.dtype) for array in arrays],
        scratch_shapes=[pltpu.SemaphoreType.DMA((len(arrays),))],
        compiler_params=pltpu.CompilerParams(vmem_limit_bytes=16 << 20),
        cost_estimate=SHORT,
        name="stage",
    )(after, *arrays)


def squares(tensor):
    rows = (tensor * tensor).reshape(-1, tensor.shape[-1])
    return jnp.sum(jnp.sum(rows, axis=0, keepdims=True), axis=1, keepdims=True)


def update_kernel(place_ref, shared_ref, norm_ref, count_ref, *refs, shapes, rates, pieces):
    pieces_refs, refs = refs[:pieces], refs[pieces:]
    states, outputs = refs[:18], refs[18:38]
    mixed_ref, taps_scratch, load_sem, store_sem = refs[38:42]
    held = refs[42:]
    loads = [
        pltpu.make_async_copy(state, buffer, load_sem.at[k])
        for k, (state, buffer) in enumerate(zip(states, held))
    ]
    for k in (3, 4, 5, 6, 7, 8, 0, 1, 2) + tuple(range(9, 18)):
        loads[k].start()
    share, width = shared_ref.shape[1], mixed_ref.shape[1]
    for device in range(shared_ref.shape[0]):
        mixed_ref[device * share : (device + 1) * share] = shared_ref[device, :, :width].astype(F32)
    depth_bins, cam_width, classes, hidden_width = shapes
    if pieces > 1:
        for shift, ref in enumerate(pieces_refs):
            taps_scratch[lax.rem(place_ref[2] + (pieces - shift), pieces)] = ref[...].astype(F32)
        taps_ref = taps_scratch[...].reshape(9, held[3].shape[1], taps_scratch.shape[2])
    else:
        taps_ref = pieces_refs[0][...]
    mixed = mixed_ref[...]
    column = LANES + cam_width
    edge = taps_ref.shape[2] - cam_width
    grads = [
        jnp.concatenate([mixed[:depth_bins], mixed[LANES:column]], 0),
        jnp.concatenate([taps_ref[:, :, edge:], taps_ref[:, :, hidden_width:edge]], 2),
        taps_ref[:, :, :hidden_width],
        mixed[column : column + classes],
        norm_ref[...],
        mixed[column + classes : column + classes + 1, :classes],
    ]
    sums = jnp.sum(shared_ref[:, :1, width:].astype(F32), axis=0)
    lane = lax.broadcasted_iota(jnp.int32, sums.shape, 1)
    squared = [None if k in (1, 2) else squares(grad) for k, grad in enumerate(grads)]
    squared[1] = jnp.sum(jnp.where(lane < 3, sums, 0.0), axis=1, keepdims=True)
    squared[2] = jnp.sum(jnp.where((lane >= 3) & (lane < 6), sums, 0.0), axis=1, keepdims=True)
    loss_sum = jnp.sum(jnp.where((lane >= 6) & (lane < 9), sums, 0.0), axis=1, keepdims=True)
    loss_ref, norms_ref = outputs[:2]
    loss_ref[...] = loss_sum / count_ref[...]
    stores = [
        pltpu.make_async_copy(buffer, output, store_sem.at[k])
        for k, (buffer, output) in enumerate(zip(held, outputs[2:]))
    ]
    norms = jnp.zeros((1, LANES), F32)
    spot = lax.broadcasted_iota(jnp.int32, norms.shape, 1)
    for k in (1, 2, 0, 3, 4, 5):
        grad = grads[k]
        size = jnp.sqrt(jnp.broadcast_to(squared[k], (1, LANES)))
        norms = jnp.where(spot == k, jnp.log(size), norms)
        factor = CLIP_NORM / jnp.maximum(size, CLIP_NORM)
        factor = factor[:, :1]
        group = range(3 * k, 3 * k + 3)
        for j in group:
            loads[j].wait()
        weight, first, second = (held[j][...] for j in group)
        results = adamw(weight, grad * factor, first, second, rates[k], STEP)
        for j, result in zip(group, results):
            held[j][...] = result
            stores[j].start()
    norms_ref[...] = norms
    for store in stores:
        store.wait()


def update(place, shared, pieces, norm, positives, states, shapes, rates):
    args = [place, shared, norm, positives.reshape(1, 1)] + pieces + states
    count = len(pieces)
    width = norm.shape[1]
    return pl.pallas_call(
        functools.partial(update_kernel, shapes=shapes, rates=rates, pieces=count),
        in_specs=[pl.BlockSpec(memory_space=pltpu.SMEM)]
        + [pl.BlockSpec(memory_space=pltpu.VMEM)] * (3 + count)
        + [pl.BlockSpec(memory_space=pl.ANY)] * 18,
        out_specs=[pl.BlockSpec(memory_space=pltpu.VMEM)] * 2
        + [pl.BlockSpec(memory_space=pl.ANY)] * 18,
        out_shape=[jax.ShapeDtypeStruct((1, 1), F32), jax.ShapeDtypeStruct((1, LANES), F32)]
        + [jax.ShapeDtypeStruct(state.shape, F32) for state in states],
        scratch_shapes=[
            pltpu.VMEM((2 * LANES, width), F32),
            pltpu.VMEM((count, *pieces[0].shape[-2:]), F32),
            pltpu.SemaphoreType.DMA((18,)),
            pltpu.SemaphoreType.DMA((18,)),
        ]
        + [pltpu.VMEM(state.shape, F32) for state in states],
        compiler_params=pltpu.CompilerParams(vmem_limit_bytes=60 << 20),
        name="update",
    )(*args)


def swapped(tensor):
    strips = lax.axis_size("strip")
    return lax.ppermute(tensor, "strip", [(i, i ^ 1) for i in range(strips)])


def halves_summed(own, other):
    return own.astype(F32) + swapped(other).astype(F32)


def moved(tensor, shift):
    strips = lax.axis_size("strip")
    return lax.ppermute(tensor, "strip", [(i, (i + 2 * shift) % strips) for i in range(strips)])


def far_first(chips):
    return sorted(range(1, chips), key=lambda shift: -min(shift, chips - shift))


def along_chips(tensor):
    chips = tensor.shape[0]
    arrived = {shift: moved(tensor[shift], shift) for shift in far_first(chips)}
    return [tensor[0]] + [arrived[shift] for shift in range(1, chips)]


def total_of(parts):
    total = parts[0].astype(F32)
    for part in parts[1:]:
        total = total + part.astype(F32)
    return total


def from_chips(tensor):
    chips = lax.axis_size("strip") // 2
    arrived = {shift: moved(tensor, shift) for shift in far_first(chips)}
    return [tensor] + [arrived[shift] for shift in range(1, chips)]


def arrange_kernel(place_ref, mine_ref, theirs_ref, *outs):
    chips, taps_total, owned = mine_ref.shape[:3]
    for chip in range(chips):
        shift = lax.rem(place_ref[0] + (chips - chip), chips)
        for core in range(2):
            start = (2 * chip + core) * owned

            def copy(ref):
                first = 0
                for out_ref in outs:
                    width = out_ref.shape[2]

                    def one(tap, carry, out_ref=out_ref, first=first, width=width):
                        out_ref[tap, start : start + owned] = ref[
                            shift, tap, :, first : first + width
                        ]
                        return carry

                    lax.fori_loop(0, taps_total, one, 0)
                    first += width

            pl.when(place_ref[1] == core)(functools.partial(copy, mine_ref))
            pl.when(place_ref[1] != core)(functools.partial(copy, theirs_ref))


def arrange(place, mine, theirs, widths):
    chips, taps_total, owned = mine.shape[:3]
    return pl.pallas_call(
        arrange_kernel,
        in_specs=[pl.BlockSpec(memory_space=pltpu.SMEM)]
        + [pl.BlockSpec(memory_space=pltpu.VMEM)] * 2,
        out_specs=[pl.BlockSpec(memory_space=pltpu.VMEM)] * len(widths),
        out_shape=[
            jax.ShapeDtypeStruct((taps_total, 2 * chips * owned, width), BF) for width in widths
        ],
        compiler_params=pltpu.CompilerParams(vmem_limit_bytes=32 << 20),
        cost_estimate=SHORT,
        name="arrange",
    )(place, mine, theirs)


def moments(stats, cells, border):
    shared = lax.all_to_all(stats, ("batch", "strip"), 0, 0)
    if border:
        shared, border = lax.optimization_barrier((shared, border))
    centers = shared[:, 0]
    total = jnp.mean(centers, axis=0)
    spread_mean = jnp.mean(shared[:, 1] / cells + (centers - total) ** 2, axis=0)
    return (total, lax.rsqrt(spread_mean + EPS_NORM), jnp.sum(shared[:, 2, 0]), border)


def over_batch(tensor, shift):
    count = lax.axis_size("batch")
    if shift == 0:
        return tensor
    return lax.ppermute(tensor, "batch", [(i, (i + shift) % count) for i in range(count)])


def adamw(weight, gradient, first, second, rate, step_value):
    first = 0.9 * first + 0.1 * gradient
    second = 0.999 * second + 0.001 * gradient * gradient
    fix_one = 1.0 / (1.0 - 0.9**step_value)
    fix_two = 1.0 / (1.0 - 0.999**step_value)
    update = first * fix_one / (jnp.sqrt(second * fix_two) + 1e-08) + 0.01 * weight
    return (weight - rate * update, first, second)


def shards(
    camera_features,
    lidar_bev,
    pool_index,
    box_peaks,
    box_count,
    w_depth,
    m_depth,
    v_depth,
    w_join,
    m_join,
    v_join,
    w_res,
    m_res,
    v_res,
    w_head,
    m_head,
    v_head,
    norm_params,
    m_norm,
    v_norm,
    head_bias,
    m_bias,
    v_bias,
):
    samples, row_local, col_total, lidar_width = lidar_bev.shape
    strips = lax.axis_size("strip")
    row_total = row_local * strips
    cell_total = float(samples * lax.axis_size("batch") * row_total * col_total)
    depth_bins = pool_index.shape[2]
    classes = w_head.shape[1]
    owned = w_join.shape[3]
    cam_width = w_depth.shape[1] - depth_bins
    first_row = lax.axis_index("strip") * row_local
    place = lax.axis_index("strip")
    place = jnp.stack([place // 2, place % 2, lax.axis_index("batch")]).astype(jnp.int32)
    hidden_width = w_res.shape[2]
    taps_low = jnp.concatenate(
        [
            jnp.swapaxes(part, 2, 3).reshape(9, owned, -1)
            for part in (w_res, w_join[:, :, cam_width:], w_join[:, :, :cam_width])
        ],
        axis=2,
    ).astype(BF)
    taps_low = jnp.pad(taps_low, ((0, 0), (0, 0), (0, LANES - cam_width)))
    if owned % 16 == 0:
        taps_mine = from_chips(taps_low)
    strip_cells = row_local * col_total
    layout = plan(camera_features.shape[1], strips, strip_cells)
    own, other, dense, both_low = pool(
        place, camera_features[0], pool_index[0], w_depth.T, layout
    )
    if owned % 16 == 0:
        other, taps_mine = lax.optimization_barrier((other, taps_mine))
    pooled_halves = halves_summed(own, other).astype(BF)
    pooled = along_chips(pooled_halves)
    widths = [hidden_width, lidar_width, LANES]
    if owned % 16 == 0:
        taps_mine = jnp.stack(taps_mine)
        taps_full = arrange(place, taps_mine, swapped(taps_mine), widths)
    else:
        gathered = lax.all_gather(taps_low, "strip", axis=1, tiled=True)
        taps_full = jnp.split(gathered, [hidden_width, hidden_width + lidar_width], axis=2)
    lidar_parts = halo(lidar_bev[0])
    gaps = nearest_gaps(
        box_peaks[0], box_count, first_row, row_local, col_total, classes
    )
    pooled, gaps, taps_full, lidar_parts = lax.optimization_barrier(
        (pooled, gaps, taps_full, lidar_parts)
    )
    wide_out = jax.ShapeDtypeStruct((row_local, col_total, hidden_width), F32)
    axes = ("batch", "strip")
    devices = lax.axis_size(axes)
    stats_out = jax.ShapeDtypeStruct((devices, 3, hidden_width), F32)
    camera_parts = halo(settle(pooled, row_local, col_total))
    join_out, stats = convolve(
        [lidar_parts, camera_parts],
        taps_full[1:],
        False,
        keep_moments,
        [wide_out, stats_out],
        [gaps],
    )
    cells = float(strip_cells)
    center_one, scale_one, positives, join_border = moments(
        stats, cells, edges(join_out[:1], join_out[-1:])
    )

    def norm_one(values):
        return (values - center_one) * scale_one

    def act_of(values):
        return jax.nn.silu(norm_one(values) * norm_params[0] + norm_params[1]).astype(BF)

    act_parts = with_edges(act_of, [join_out], [join_border])
    act_one = act_parts[1]
    res_out, stats = convolve(
        [act_parts], taps_full[:1], False, keep_moments, [wide_out, stats_out]
    )
    center_two, scale_two, unused_term, unused_border = moments(stats, cells, ())

    def norm_two(values):
        return (values - center_two) * scale_two

    vectors = jnp.stack([center_two, scale_two, norm_params[2], norm_params[3]])
    grad_summed, sums, local_loss, grad_head = run_head(
        vectors,
        res_out,
        act_one,
        w_head.T.astype(BF),
        head_bias[:, None],
        gaps,
        positives.reshape(1, 1),
        devices,
    )
    shared = lax.all_to_all(sums, axes, 0, 0)
    shift_two, gain_two = jnp.sum(shared, axis=0)

    def grad_res_of(grad, values):
        spare = grad - shift_two / cell_total - norm_two(values) * gain_two / cell_total
        return (norm_params[2] * scale_two * spare).astype(BF)

    res_parts = halo(grad_res_of(grad_summed, res_out))
    sums_out = jax.ShapeDtypeStruct((devices, 2, hidden_width), F32)
    vectors = jnp.stack([center_one, scale_one, norm_params[0], norm_params[1]])
    grad_pre, sums = convolve(
        [res_parts],
        taps_full[:1],
        True,
        keep_grad,
        [wide_out, sums_out],
        [grad_summed, join_out, vectors],
    )
    shared = lax.all_to_all(sums, axes, 0, 0)
    shift_one, gain_one = jnp.sum(shared, axis=0)

    def grad_join_of(grad, values):
        spare = grad - shift_one / cell_total - norm_one(values) * gain_one / cell_total
        return (norm_params[0] * scale_one * spare).astype(BF)

    join_parts = halo(grad_join_of(grad_pre, join_out))
    cells_out = jax.ShapeDtypeStruct((layout["per_strip"], cam_width, LANES), BF)
    (grad_cells,) = convolve(
        [join_parts], taps_full[2:], True, keep_cells, [cells_out]
    )
    grad_cells, join_late, res_late = lax.optimization_barrier(
        (grad_cells, join_parts[1], res_parts[1])
    )
    grid_parts = from_chips(grad_cells)
    own_join, other_join = taps(
        place,
        [lidar_parts, camera_parts],
        [lidar_width, cam_width],
        join_late,
        strips // 2,
    )
    own_res, other_res = taps(place, [act_parts], [hidden_width], res_late, strips // 2)
    grid_parts, own_join, other_join, own_res, other_res = lax.optimization_barrier(
        (grid_parts, own_join, other_join, own_res, other_res)
    )
    grid_mine = jnp.stack(grid_parts)
    grid_theirs = swapped(grid_mine)
    grads = jnp.concatenate(
        [halves_summed(own_res, other_res), halves_summed(own_join, other_join)], axis=-1
    )
    taps_parts = along_chips(grads.astype(BF))
    grad_both = unpool(
        place,
        camera_features[0],
        pool_index[0],
        both_low,
        dense,
        grid_mine,
        grid_theirs,
        grad_head,
        layout,
    )
    grad_both, taps_parts = lax.optimization_barrier((grad_both, taps_parts))
    members = lax.axis_size("batch")
    member = lax.axis_index("batch")
    quarters = total_of(taps_parts).astype(BF).reshape(members, -1, (hidden_width + lidar_width + cam_width))
    parts = [
        over_batch(lax.dynamic_index_in_dim(quarters, (member + s) % members, 0, False), s)
        for s in range(members)
    ]
    width = w_depth.shape[0]
    mixed = grad_both.reshape(devices, -1, width)
    mixed = lax.all_to_all(mixed, axes, 0, 0)
    share, shared = join_shares(mixed, local_loss, parts, hidden_width)
    shared = lax.all_to_all(shared, axes, 0, 0)
    pieces = [over_batch(share, s) for s in range(members)]
    if share.shape[0] % 8:
        order = (member - jnp.arange(members)) % members
        pieces = [jnp.take(jnp.stack(pieces), order, axis=0).reshape(9, owned, -1).astype(F32)]
    grad_norm = jnp.stack([gain_one, shift_one, gain_two, shift_two])
    rates = [
        0.5 * w_depth.shape[0] ** (-0.5),
        0.5 * (9 * w_join.shape[2]) ** (-0.5),
        0.5 * (9 * w_res.shape[2]) ** (-0.5),
        0.5 * w_head.shape[0] ** (-0.5),
        SMALL_RATE,
        SMALL_RATE,
    ]
    weights = [w_depth, w_join, w_res, w_head, norm_params, head_bias]
    firsts = [m_depth, m_join, m_res, m_head, m_norm, m_bias]
    seconds = [v_depth, v_join, v_res, v_head, v_norm, v_bias]
    views = [
        jnp.transpose,
        lambda state: jnp.swapaxes(state, 2, 3).reshape(9, owned, -1),
        lambda state: jnp.swapaxes(state, 2, 3).reshape(9, owned, -1),
        jnp.transpose,
        lambda state: state,
        lambda state: state[None],
    ]
    backs = [
        jnp.transpose,
        lambda state: jnp.swapaxes(state.reshape(3, 3, owned, -1), 2, 3),
        lambda state: jnp.swapaxes(state.reshape(3, 3, owned, -1), 2, 3),
        jnp.transpose,
        lambda state: state,
        lambda state: state[0],
    ]
    states = [
        view(state)
        for view, group in zip(views, zip(weights, firsts, seconds))
        for state in group
    ]
    loss, norms, *states = update(
        place,
        shared,
        pieces,
        grad_norm,
        positives,
        states,
        (depth_bins, cam_width, classes, hidden_width),
        rates,
    )
    result = [loss[0], norms[0, :6]]
    for k, state in enumerate(states):
        result.append(backs[k // 3](state))
    return tuple(result)


def solution(mesh):
    in_specs = (
        P("batch", "strip", None),
        P("batch", "strip", None, None),
        P("batch", "strip", None),
        P("batch", None, None),
        P("batch"),
        P(),
        P(),
        P(),
        P(None, None, None, "strip"),
        P(None, None, None, "strip"),
        P(None, None, None, "strip"),
        P(None, None, None, "strip"),
        P(None, None, None, "strip"),
        P(None, None, None, "strip"),
        P(),
        P(),
        P(),
        P(),
        P(),
        P(),
        P(),
        P(),
        P(),
    )
    out_specs = (
        P(),
        P(),
        P(),
        P(),
        P(),
        P(None, None, None, "strip"),
        P(None, None, None, "strip"),
        P(None, None, None, "strip"),
        P(None, None, None, "strip"),
        P(None, None, None, "strip"),
        P(None, None, None, "strip"),
        P(),
        P(),
        P(),
        P(),
        P(),
        P(),
        P(),
        P(),
        P(),
    )
    return jax.shard_map(shards, mesh=mesh, in_specs=in_specs, out_specs=out_specs, check_vma=False)
```

```python
import functools

import jax
import jax.numpy as jnp
from jax import lax
from jax.experimental import pallas as pl
from jax.experimental.pallas import tpu as pltpu
from jax.sharding import PartitionSpec as P

STEP = 5


EPS_NORM = 1e-05
SPREAD_TWICE = 8.0
SMALL_RATE = 0.25
CLIP_NORM = 0.01
FAR = 1e9


def edges(first, last):
    peers = lax.axis_size("strip")
    up = [(i, i + 1) for i in range(peers - 1)]
    before = lax.ppermute(last, "strip", up)
    after = lax.ppermute(first, "strip", [(j, i) for i, j in up])
    return before, after


def halo(shard):
    before, after = edges(shard[:1], shard[-1:])
    return [before, shard, after]


def with_edges(function, shards, borders):
    place = lax.axis_index("strip")
    inside = [place > 0, place < lax.axis_size("strip") - 1]
    sides = [
        jnp.where(there, function(*side), 0).astype(BF)
        for there, side in zip(inside, zip(*borders))
    ]
    return [sides[0], function(*shards), sides[1]]


def target_kernel(peaks_ref, count_ref, first_ref, gap_ref):
    gap_ref[...] = jnp.full(gap_ref.shape, FAR, jnp.float32)
    shape = gap_ref.shape[1:]
    row_ids = lax.broadcasted_iota(jnp.int32, shape, 0) + first_ref[0]
    col_ids = lax.broadcasted_iota(jnp.int32, shape, 1)

    def visit(slot, carry):
        row_gap = row_ids - peaks_ref[0, slot]
        col_gap = col_ids - peaks_ref[1, slot]
        distance = (row_gap * row_gap + col_gap * col_gap).astype(jnp.float32)
        kind = peaks_ref[2, slot]
        gap_ref[kind] = jnp.minimum(gap_ref[kind], distance)
        return carry

    lax.fori_loop(0, count_ref[0], visit, 0)


def nearest_gaps(box_peaks, box_count, first_row, row_total, col_total, classes):
    return pl.pallas_call(
        target_kernel,
        in_specs=[pl.BlockSpec(memory_space=pltpu.SMEM)] * 3,
        out_specs=pl.BlockSpec(memory_space=pltpu.VMEM),
        out_shape=jax.ShapeDtypeStruct((classes, row_total, col_total), jnp.float32),
        cost_estimate=SHORT,
        name="targets",
    )(box_peaks, box_count, first_row[None])


LANES = 128
SHORT = pl.CostEstimate(flops=1000, bytes_accessed=1000, transcendentals=0)
BF = jnp.bfloat16
F32 = jnp.float32


def plan(pixels, strips, strip_cells):
    per_strip = -(-strip_cells // LANES)
    high = strips * per_strip
    block = 352 if pixels % 352 == 0 and high <= 128 else 48
    return dict(
        per_strip=per_strip,
        high=high,
        offset=high // 2,
        block=block,
        stride=block + 4,
        group=block,
        strip_cells=strip_cells,
    )


def split_cells(index, plan):
    cell = index.astype(F32)
    strip = jnp.floor((cell + 0.5) * (1.0 / plan["strip_cells"]))
    rest = cell - strip * plan["strip_cells"]
    part = jnp.floor((rest + 0.5) * (1.0 / LANES))
    return strip * plan["per_strip"] + part - plan["offset"], rest - part * LANES


def softmax_lanes(logits, bins):
    lane = lax.broadcasted_iota(jnp.int32, logits.shape, 1)
    logits = jnp.where(lane < bins, logits, -jnp.inf)
    powers = jnp.exp(logits - jnp.max(logits, axis=1, keepdims=True))
    return powers / jnp.sum(powers, axis=1, keepdims=True)


def spread(ref, pixel, rows=16):
    return jnp.broadcast_to(ref[pl.ds(pixel, 1), :], (rows, LANES))


def one_hot(row, value, rows, offset=0):
    base = (lax.broadcasted_iota(jnp.int32, (rows, LANES), 0) - offset).astype(F32).astype(BF)
    none = jnp.zeros((16, LANES), BF)
    return [
        jnp.where(base[k : k + 16] == row, value, none) for k in range(0, rows, 16)
    ]


def high_pair(high_ref, depth_ref, first, plan):
    whole = plan["high"] // 16 * 16
    parts = []
    for j in range(2):
        row = spread(high_ref, first + j).astype(BF)
        value = spread(depth_ref, first + j).astype(BF)
        parts += one_hot(row, value, whole, plan["offset"])
    if whole < plan["high"]:
        both = [
            jnp.concatenate([spread(ref, first, 8), spread(ref, first + 1, 8)], 0).astype(BF)
            for ref in (high_ref, depth_ref)
        ]
        base = lax.broadcasted_iota(jnp.int32, (16, LANES), 0)
        base = jnp.where(base < 8, base, base - 8) + (whole - plan["offset"])
        none = jnp.zeros((16, LANES), BF)
        parts.append(jnp.where(base.astype(F32).astype(BF) == both[0], both[1], none))
    return jnp.concatenate(parts, 0)


def pool_kernel(place_ref, feat_ref, index_ref, weight_ref, own_ref, other_ref, dense_ref, both_ref, high_ref, low_ref, depth_ref, held, total, *, plan):
    bins = index_ref.shape[1]
    block, stride, high = (plan[k] for k in ("block", "stride", "high"))
    step = pl.program_id(0)

    @pl.when(step == 0)
    def _():
        high_ref[...] = jnp.zeros_like(high_ref)
        low_ref[...] = jnp.zeros_like(low_ref)
        total[...] = jnp.zeros_like(total)
        channels = total.shape[1]
        both_ref[...] = jnp.zeros_like(both_ref)
        both_ref[:bins] = weight_ref[:bins].astype(BF)
        both_ref[LANES : LANES + channels] = weight_ref[bins : bins + channels].astype(BF)

    feat = feat_ref[...]
    logits = lax.dot_general(feat, both_ref[:LANES], (((1,), (1,)), ((), ())), preferred_element_type=F32)
    depth_ref[...] = softmax_lanes(logits, bins)
    channels = total.shape[1]
    context_low = both_ref[LANES : LANES + channels]
    context = lax.dot_general(context_low, feat, (((1,), (1,)), ((), ())), preferred_element_type=F32).astype(BF)
    high_id, low_id = split_cells(index_ref[...], plan)
    high_ref[:, :bins] = high_id
    low_ref[:, :bins] = low_id
    one = jnp.ones((16, LANES), BF)

    def scatter(group, carry):
        for k in range(0, plan["group"], 2):
            first = group * plan["group"] + k
            left = high_pair(high_ref, depth_ref, first, plan)
            right = []
            for j in range(2):
                low = spread(low_ref, first + j).astype(BF)
                right.append(jnp.concatenate(one_hot(low, one, LANES), 0))
            tile = lax.dot_general(
                left, jnp.concatenate(right, 0), (((1,), (1,)), ((), ())), preferred_element_type=F32
            )
            whole = high // 16 * 16
            for j in range(2):
                part = tile[:, j * LANES : (j + 1) * LANES]
                held[pl.ds(first + j, whole, stride=stride), :] = part[j * whole : (j + 1) * whole]
                if whole < high:
                    held[pl.ds(first + j + whole * stride, 8, stride=stride), :] = part[
                        2 * whole + 8 * j : 2 * whole + 8 * j + 8
                    ]
        return carry

    lax.fori_loop(0, block // plan["group"], scatter, 0)

    def gather(k, carry):
        parts = []
        for j in range(2):
            part = held[pl.ds((k * 2 + j) * stride, block), :].astype(BF)
            dense_ref[k * 2 + j] = part
            parts.append(part)
        out = jnp.dot(context, jnp.concatenate(parts, 1), preferred_element_type=F32)
        for j in range(2):
            total[k * 2 + j] += out[:, j * LANES : (j + 1) * LANES]
        return carry

    lax.fori_loop(0, high // 2, gather, 0, unroll=36)

    @pl.when(step == pl.num_programs(0) - 1)
    def _():
        count = plan["per_strip"]
        chips = own_ref.shape[0]
        for shift in range(chips):
            chip = lax.rem(place_ref[0] + shift, chips)
            for ref, core in ((own_ref, place_ref[1]), (other_ref, 1 - place_ref[1])):
                first = (2 * chip + core) * count
                ref[shift] = total[pl.ds(first, count)].astype(BF)


def pool(place, features, index, weight, plan):
    pixels, width = features.shape
    bins = index.shape[1]
    channels = weight.shape[0] - bins
    block, high = plan["block"], plan["high"]
    halves = (high // plan["per_strip"] // 2, plan["per_strip"], channels, LANES)
    return pl.pallas_call(
        functools.partial(pool_kernel, plan=plan),
        grid=(pixels // block,),
        in_specs=[
            pl.BlockSpec(memory_space=pltpu.SMEM),
            pl.BlockSpec((block, width), lambda i: (i, 0)),
            pl.BlockSpec((block, bins), lambda i: (i, 0)),
            pl.BlockSpec(weight.shape, lambda i: (0, 0)),
        ],
        out_specs=[
            pl.BlockSpec(halves, lambda i: (0, 0, 0, 0)),
            pl.BlockSpec(halves, lambda i: (0, 0, 0, 0)),
            pl.BlockSpec((high, block, LANES), lambda i: (0, i, 0)),
            pl.BlockSpec((2 * LANES, width), lambda i: (0, 0)),
        ],
        out_shape=[
            jax.ShapeDtypeStruct(halves, BF),
            jax.ShapeDtypeStruct(halves, BF),
            jax.ShapeDtypeStruct((high, pixels, LANES), BF),
            jax.ShapeDtypeStruct((2 * LANES, width), BF),
        ],
        scratch_shapes=[pltpu.VMEM((block, LANES), F32)] * 3
        + [
            pltpu.VMEM(((high + 1) * plan["stride"], LANES), F32),
            pltpu.VMEM((high, channels, LANES), F32),
        ],
        compiler_params=pltpu.CompilerParams(vmem_limit_bytes=40 << 20),
        cost_estimate=pl.CostEstimate(
            flops=4 * pixels * high * LANES * LANES,
            bytes_accessed=2 * pixels * high * LANES,
            transcendentals=0,
        ),
        name="pool",
    )(place, features, index, weight)


def unpool_kernel(place_ref, feat_ref, index_ref, both_ref, dense_ref, mine_ref, theirs_ref, head_ref, out_ref, high_ref, low_ref, pick_ref, held, sum_ref, grid_ref, grad_ref, *, plan):
    bins = index_ref.shape[1]
    channels = grid_ref.shape[1]
    chips, count = mine_ref.shape[:2]
    block, stride, high = (plan[k] for k in ("block", "stride", "high"))
    step = pl.program_id(0)

    @pl.when(step == 0)
    def _():
        high_ref[...] = jnp.zeros_like(high_ref)
        low_ref[...] = jnp.zeros_like(low_ref)
        held[...] = jnp.zeros_like(held)
        grad_ref[...] = jnp.zeros_like(grad_ref)
        for shift in range(chips):
            chip = lax.rem(place_ref[0] + (chips - shift), chips)
            for ref, core in ((mine_ref, place_ref[1]), (theirs_ref, 1 - place_ref[1])):
                grid_ref[pl.ds((2 * chip + core) * count, count)] = ref[shift]

    feat = feat_ref[...]
    logits = lax.dot_general(feat, both_ref[...], (((1,), (1,)), ((), ())), preferred_element_type=F32)
    depth = softmax_lanes(logits[:, :LANES], bins)
    context = logits[:, LANES : LANES + channels].astype(BF)
    high_id, low_id = split_cells(index_ref[...], plan)
    high_ref[:, :bins] = high_id
    low_ref[:, :bins] = low_id

    def project(k, carry):
        grid = jnp.concatenate([grid_ref[k * 2], grid_ref[k * 2 + 1]], 1)
        out = jnp.dot(context, grid, preferred_element_type=F32)
        for j in range(2):
            held[pl.ds((k * 2 + j) * stride, block), :] = out[:, j * LANES : (j + 1) * LANES]
        return carry

    lax.fori_loop(0, high // 2, project, 0, unroll=36)
    parts = 72

    def mix(k, carry):
        dense = jnp.concatenate([dense_ref[k * parts + j] for j in range(parts)], 1)
        grid = jnp.concatenate([grid_ref[k * parts + j] for j in range(parts)], 1)
        sum_ref[...] += lax.dot_general(
            dense, grid, (((1,), (1,)), ((), ())), preferred_element_type=F32
        )
        return carry

    sum_ref[...] = jnp.zeros_like(sum_ref)
    lax.fori_loop(0, high // parts, mix, 0)
    one = jnp.ones((16, LANES), BF)
    rows = (lax.broadcasted_iota(jnp.int32, (high, LANES), 0) - plan["offset"]).astype(F32)

    def collect(group, carry):
        for k in range(0, plan["group"], 2):
            first = group * plan["group"] + k
            left, right = [], []
            for j in range(2):
                left.append(held[pl.ds(first + j, high, stride=stride), :])
                low = spread(low_ref, first + j).astype(BF)
                right.append(jnp.concatenate(one_hot(low, one, LANES), 0))
            tile = jnp.dot(jnp.concatenate(left, 0).astype(BF), jnp.concatenate(right, 1), preferred_element_type=F32)
            for j in range(2):
                part = tile[j * high : (j + 1) * high, j * LANES : (j + 1) * LANES]
                kept = jnp.where(rows == high_ref[pl.ds(first + j, 1), :], part, 0.0)
                pick_ref[pl.ds(first + j, 1), :] = jnp.sum(kept, axis=0, keepdims=True)
        return carry

    lax.fori_loop(0, block // plan["group"], collect, 0)
    grad_prob = pick_ref[...]
    grad_context = sum_ref[...]
    grad_depth = depth * (grad_prob - jnp.sum(grad_prob * depth, axis=1, keepdims=True))
    grad_low = jnp.concatenate(
        [grad_depth, grad_context, jnp.zeros((block, LANES - channels), F32)], axis=1
    ).astype(BF)
    grad_ref[...] += lax.dot_general(grad_low, feat, (((0,), (0,)), ((), ())), preferred_element_type=F32)

    @pl.when(step == pl.num_programs(0) - 1)
    def _():
        first = LANES + channels
        rows = head_ref.shape[0]
        out_ref[:first] = grad_ref[:first].astype(BF)
        spare = jnp.zeros((2 * LANES - first - rows, grad_ref.shape[1]), F32)
        out_ref[first:] = jnp.concatenate([head_ref[...], spare], 0).astype(BF)


def unpool(place, features, index, both_low, dense, mine, theirs, head, plan):
    pixels, width = features.shape
    bins = index.shape[1]
    channels = mine.shape[2]
    block, high = plan["block"], plan["high"]
    return pl.pallas_call(
        functools.partial(unpool_kernel, plan=plan),
        grid=(pixels // block,),
        in_specs=[
            pl.BlockSpec(memory_space=pltpu.SMEM),
            pl.BlockSpec((block, width), lambda i: (i, 0)),
            pl.BlockSpec((block, bins), lambda i: (i, 0)),
            pl.BlockSpec(both_low.shape, lambda i: (0, 0)),
            pl.BlockSpec((high, block, LANES), lambda i: (0, i, 0)),
            pl.BlockSpec(mine.shape, lambda i: (0, 0, 0, 0)),
            pl.BlockSpec(theirs.shape, lambda i: (0, 0, 0, 0)),
            pl.BlockSpec(head.shape, lambda i: (0, 0)),
        ],
        out_specs=pl.BlockSpec((2 * LANES, width), lambda i: (0, 0)),
        out_shape=jax.ShapeDtypeStruct((2 * LANES, width), BF),
        scratch_shapes=[pltpu.VMEM((block, LANES), F32)] * 3
        + [
            pltpu.VMEM(((high + 1) * plan["stride"], LANES), F32),
            pltpu.VMEM((block, channels), F32),
            pltpu.VMEM((high, channels, LANES), BF),
            pltpu.VMEM((2 * LANES, width), F32),
        ],
        compiler_params=pltpu.CompilerParams(vmem_limit_bytes=40 << 20),
        cost_estimate=pl.CostEstimate(
            flops=6 * pixels * high * LANES * LANES,
            bytes_accessed=2 * pixels * high * LANES,
            transcendentals=0,
        ),
        name="unpool",
    )(place, features, index, both_low, dense, mine, theirs, head)


def fill_windows(window_ref, part, cols, span):
    before_ref, shard_ref, after_ref = part
    rows = shard_ref.shape[0]
    width = window_ref.shape[2]
    window_ref[...] = jnp.zeros_like(window_ref)
    for row in range(rows + 2):
        if row == 0:
            line = before_ref[0]
        elif row == rows + 1:
            line = after_ref[0]
        else:
            line = shard_ref[row - 1]
        line = line[:, :width]
        start = row * span
        window_ref[0, start + 1 : start + cols] = line[: cols - 1]
        window_ref[1, start : start + cols] = line
        window_ref[2, start : start + cols - 1] = line[1:]


def window_scratch(part, width, span):
    return pltpu.VMEM((3, (part[1].shape[0] + 2) * span, width), BF)


def span_of(cols):
    return -(-cols // 16) * 16


def conv_kernel(*refs, count, turned, finish):
    kernels = refs[:count]
    parts = [refs[count + 3 * k : count + 3 * k + 3] for k in range(count)]
    rows, cols = parts[0][1].shape[:2]
    span = span_of(cols)
    windows = refs[-count:]
    left, right = [], []
    for part, window_ref, kernel_ref in zip(parts, windows, kernels):
        fill_windows(window_ref, part, cols, span)
        for tap in range(9):
            upward, across = tap // 3, tap % 3
            left.append(window_ref[across, upward * span : (upward + rows) * span])
            right.append(kernel_ref[8 - tap if turned else tap])
    left = jnp.concatenate(left, 1)
    if turned:
        total = jnp.dot(left, jnp.concatenate(right, 0), preferred_element_type=F32)
    else:
        total = lax.dot_general(
            left, jnp.concatenate(right, 1), (((1,), (1,)), ((), ())), preferred_element_type=F32
        )
    finish(total, rows, cols, span, *refs[4 * count : -count])


def keep_rows(total, rows, cols, span, out_ref):
    for row in range(rows):
        out_ref[row] = total[row * span : row * span + cols]


def keep_moments(total, rows, cols, span, *refs):
    out_ref, stats_ref = refs[-2:]
    keep_rows(total, rows, cols, span, out_ref)
    cells = float(rows * cols)
    center = jnp.sum(total, axis=0, keepdims=True) / cells
    spot = lax.broadcasted_iota(jnp.int32, (span, total.shape[1]), 0)
    spread_sum = jnp.zeros_like(center)
    for row in range(rows):
        apart = total[row * span : (row + 1) * span] - center
        apart = jnp.where(spot < cols, apart, 0.0)
        spread_sum = spread_sum + jnp.sum(apart * apart, axis=0, keepdims=True)
    hits = jnp.zeros_like(center)
    for ref in refs[:-2]:
        hits = jnp.full(center.shape, jnp.sum(jnp.where(ref[...] == 0.0, 1.0, 0.0)))
    stats = jnp.concatenate([center, spread_sum, hits], 0)

    def store(device, carry):
        stats_ref[device] = stats
        return carry

    lax.fori_loop(0, stats_ref.shape[0], store, 0)


def keep_grad(total, rows, cols, span, more_ref, norm_in_ref, vector_ref, out_ref, sums_ref):
    center, scale, gain, shift = (vector_ref[k : k + 1] for k in range(4))
    shift_sum = jnp.zeros_like(center)
    gain_sum = jnp.zeros_like(center)
    for row in range(rows):
        normed = (norm_in_ref[row] - center) * scale
        value = normed * gain + shift
        sig = jax.nn.sigmoid(value)
        grad = total[row * span : row * span + cols] + more_ref[row]
        grad = grad * (sig * (1.0 + value * (1.0 - sig)))
        out_ref[row] = grad
        shift_sum = shift_sum + jnp.sum(grad, axis=0, keepdims=True)
        gain_sum = gain_sum + jnp.sum(grad * normed, axis=0, keepdims=True)
    sums = jnp.concatenate([shift_sum, gain_sum], 0)

    def store(device, carry):
        sums_ref[device] = sums
        return carry

    lax.fori_loop(0, sums_ref.shape[0], store, 0)


def head_kernel(vector_ref, res_ref, act_ref, head_ref, bias_ref, gap_ref, count_ref, grad_ref, sums_ref, loss_ref, head_grad_ref):
    rows, cols, width = res_ref.shape
    center, scale, gain, shift = (vector_ref[k : k + 1] for k in range(4))
    head = head_ref[...]
    shift_sum = jnp.zeros_like(center)
    gain_sum = jnp.zeros_like(center)
    head_grad = jnp.zeros(head.shape, F32)
    bias_grad = jnp.zeros((head.shape[0], 1), F32)
    loss = jnp.zeros((head.shape[0], 1), F32)
    for row in range(rows):
        normed = (res_ref[row] - center) * scale
        summed = normed * gain + shift + act_ref[row].astype(F32)
        sig = jax.nn.sigmoid(summed)
        hidden = (summed * sig).astype(BF)
        logits = lax.dot_general(head, hidden, (((1,), (1,)), ((), ())), preferred_element_type=F32)
        logits = logits + bias_ref[...]
        prob = jax.nn.sigmoid(logits)
        tail = jnp.log1p(jnp.exp(-jnp.abs(logits)))
        soft_pos = jnp.maximum(logits, 0.0) + tail
        soft_neg = jnp.maximum(-logits, 0.0) + tail
        gap = gap_ref[:, row, :]
        heatmap = jnp.where(gap < FAR, jnp.exp(-gap / SPREAD_TWICE), 0.0)
        struck = jnp.where(gap == 0.0, 1.0, 0.0)
        weighting = (1.0 - heatmap) * (1.0 - heatmap)
        weighting = weighting * weighting
        miss = 1.0 - prob
        loss_here = struck * miss * miss * soft_neg + weighting * prob * prob * soft_pos
        loss = loss + jnp.sum(loss_here, axis=1, keepdims=True)
        grad_pos = -2.0 * prob * miss * miss * soft_neg - miss * miss * miss
        grad_neg = 2.0 * prob * prob * miss * soft_pos + prob * prob * prob
        grad_logits = (struck * grad_pos + weighting * grad_neg) / count_ref[...]
        grad_logits = grad_logits.astype(BF)
        bias_grad = bias_grad + jnp.sum(grad_logits.astype(F32), axis=1, keepdims=True)
        head_grad = head_grad + jnp.dot(grad_logits, hidden, preferred_element_type=F32)
        grad = lax.dot_general(grad_logits, head, (((0,), (0,)), ((), ())), preferred_element_type=F32)
        grad = grad * (sig * (1.0 + summed * (1.0 - sig)))
        grad_ref[row] = grad
        shift_sum = shift_sum + jnp.sum(grad, axis=0, keepdims=True)
        gain_sum = gain_sum + jnp.sum(grad * normed, axis=0, keepdims=True)
    loss_ref[...] = jnp.sum(loss, axis=0, keepdims=True)
    classes = head.shape[0]
    head_grad_ref[:classes] = head_grad
    down = lax.broadcasted_iota(jnp.int32, head.shape, 0)
    across = lax.broadcasted_iota(jnp.int32, head.shape, 1)
    bias_row = jnp.sum(jnp.where(down == across, bias_grad, 0.0), axis=0, keepdims=True)
    head_grad_ref[classes : classes + 1] = bias_row
    sums = jnp.concatenate([shift_sum, gain_sum], 0)

    def store(device, carry):
        sums_ref[device] = sums
        return carry

    lax.fori_loop(0, sums_ref.shape[0], store, 0)


def run_head(vectors, res_out, act, head_low, bias, gaps, positives, devices):
    rows, cols, width = res_out.shape
    classes = head_low.shape[0]
    shapes = [
        (rows, cols, width),
        (devices, 2, width),
        (1, 1),
        (classes + 1, width),
    ]
    return pl.pallas_call(
        head_kernel,
        in_specs=[pl.BlockSpec(memory_space=pltpu.VMEM)] * 7,
        out_specs=[pl.BlockSpec(memory_space=pltpu.VMEM)] * 4,
        out_shape=[jax.ShapeDtypeStruct(shape, F32) for shape in shapes],
        compiler_params=pltpu.CompilerParams(vmem_limit_bytes=24 << 20),
        name="head",
    )(vectors, res_out, act, head_low, bias, gaps, positives)


def keep_cells(total, rows, cols, span, out_ref):
    cells, channels = out_ref.shape[0] * LANES, out_ref.shape[1]
    flat = [total[row * span : row * span + cols] for row in range(rows)]
    flat.append(jnp.zeros((cells - rows * cols, total.shape[1]), F32))
    flat = jnp.concatenate(flat, 0)
    for part in range(out_ref.shape[0]):
        out_ref[part] = flat[part * LANES : (part + 1) * LANES].T[:channels].astype(BF)


def convolve(parts, kernels, turned, finish, outs, extras=()):
    rows, cols = parts[0][1].shape[:2]
    span = span_of(cols)
    widths = [kernel.shape[1] if turned else kernel.shape[2] for kernel in kernels]
    flat = [array for part in parts for array in part]
    operands = [*kernels, *flat, *extras]
    return pl.pallas_call(
        functools.partial(conv_kernel, count=len(parts), turned=turned, finish=finish),
        in_specs=[pl.BlockSpec(memory_space=pltpu.VMEM)] * len(operands),
        out_specs=[pl.BlockSpec(memory_space=pltpu.VMEM)] * len(outs),
        out_shape=outs,
        scratch_shapes=[
            window_scratch(part, width, span) for part, width in zip(parts, widths)
        ],
        compiler_params=pltpu.CompilerParams(vmem_limit_bytes=32 << 20),
        cost_estimate=pl.CostEstimate(
            flops=18 * rows * span * sum(widths) * kernels[0].shape[1],
            bytes_accessed=2 * sum(kernel.size for kernel in kernels),
            transcendentals=0,
        ),
        name="convolve",
    )(*operands)


def taps_kernel(place_ref, grad_ref, *refs, widths):
    count = len(widths)
    parts = [refs[3 * k : 3 * k + 3] for k in range(count)]
    own_ref, other_ref = refs[3 * count : 3 * count + 2]
    windows = refs[3 * count + 2 : 4 * count + 2]
    flipped_grad, total = refs[4 * count + 2 :]
    rows, cols, depth = grad_ref.shape
    owned = own_ref.shape[2]
    chips = own_ref.shape[0]
    span = span_of(cols)
    for part, window_ref in zip(parts, windows):
        fill_windows(window_ref, part, cols, span)
    flat = []
    for row in range(rows):
        flat += [grad_ref[row], jnp.zeros((span - cols, depth), BF)]
    flipped_grad[...] = jnp.concatenate(flat, 0).T

    def visit(tap, carry):
        start = pl.multiple_of((tap // 3) * span, 16)
        across = lax.rem(tap, 3)
        first = 0
        for window_ref in windows:
            window = window_ref[across, pl.ds(start, rows * span)]
            total[:, first : first + window.shape[1]] = jnp.dot(
                flipped_grad[...], window, preferred_element_type=F32
            )
            first += window.shape[1]
        for shift in range(chips):
            chip = lax.rem(place_ref[0] + shift, chips)
            for ref, core in ((own_ref, place_ref[1]), (other_ref, 1 - place_ref[1])):
                half = pl.multiple_of((2 * chip + core) * owned, 8)
                ref[shift, tap] = total[pl.ds(half, owned)].astype(BF)
        return carry

    lax.fori_loop(0, 9, visit, 0)


def taps(place, parts, widths, grad, chips):
    rows, cols, depth = grad.shape
    channels = sum(widths)
    span = span_of(cols)
    flat = [array for part in parts for array in part]
    half = jax.ShapeDtypeStruct((chips, 9, depth // chips // 2, channels), BF)
    return pl.pallas_call(
        functools.partial(taps_kernel, widths=widths),
        in_specs=[pl.BlockSpec(memory_space=pltpu.SMEM)]
        + [pl.BlockSpec(memory_space=pltpu.VMEM)] * (1 + len(flat)),
        out_specs=[pl.BlockSpec(memory_space=pltpu.VMEM)] * 2,
        out_shape=[half, half],
        scratch_shapes=[window_scratch(part, width, span) for part, width in zip(parts, widths)]
        + [pltpu.VMEM((depth, rows * span), BF), pltpu.VMEM((depth, channels), F32)],
        compiler_params=pltpu.CompilerParams(vmem_limit_bytes=28 << 20),
        cost_estimate=SHORT,
        name="taps",
    )(place, grad, *flat)


def settle_kernel(*refs):
    out_ref = refs[-1]
    rows, cols = out_ref.shape[:2]
    total = refs[0][...].astype(F32)
    for ref in refs[1:-1]:
        total = total + ref[...].astype(F32)
    parts = total.shape[0]
    flat = jnp.concatenate([total[part].T for part in range(parts)], 0)
    spare = jnp.zeros((cols, out_ref.shape[2] - flat.shape[1]), F32)
    for row in range(rows):
        line = flat[row * cols : (row + 1) * cols]
        out_ref[row] = jnp.concatenate([line, spare], 1).astype(BF)


def settle(parts, rows, cols):
    return pl.pallas_call(
        settle_kernel,
        in_specs=[pl.BlockSpec(memory_space=pltpu.VMEM)] * len(parts),
        out_specs=pl.BlockSpec(memory_space=pltpu.VMEM),
        out_shape=jax.ShapeDtypeStruct((rows, cols, LANES), BF),
        compiler_params=pltpu.CompilerParams(vmem_limit_bytes=32 << 20),
        name="settle",
    )(*parts)


def split_bits(value):
    pieces = []
    for _ in range(3):
        piece = value.astype(BF).astype(F32)
        pieces.append(piece)
        value = value - piece
    return pieces


def join_kernel(mixed_ref, loss_ref, *refs, hidden_width):
    parts = refs[:-2]
    share_ref, out_ref = refs[-2:]
    total = parts[0][...].astype(F32)
    for part in parts[1:]:
        total = total + part[...].astype(F32)
    share_ref[...] = total.astype(BF)
    square = jnp.sum(total * total, axis=0, keepdims=True)
    scalars = [
        jnp.sum(square[:, hidden_width:], axis=1, keepdims=True),
        jnp.sum(square[:, :hidden_width], axis=1, keepdims=True),
        loss_ref[...],
    ]
    mixed = jnp.sum(mixed_ref[...].astype(F32), axis=0)
    shape = (mixed.shape[0], LANES)
    lane = lax.broadcasted_iota(jnp.int32, shape, 1)
    row = jnp.zeros(shape, F32)
    for k, scalar in enumerate(scalars):
        for j, piece in enumerate(split_bits(scalar)):
            row = jnp.where(lane == 3 * k + j, piece, row)
    block = jnp.concatenate([mixed, row], 1).astype(BF)

    def store(device, carry):
        out_ref[device] = block
        return carry

    lax.fori_loop(0, out_ref.shape[0], store, 0)


def join_shares(mixed, loss, parts, hidden_width):
    devices, rows, width = mixed.shape
    return pl.pallas_call(
        functools.partial(join_kernel, hidden_width=hidden_width),
        in_specs=[pl.BlockSpec(memory_space=pltpu.VMEM)] * (2 + len(parts)),
        out_specs=[pl.BlockSpec(memory_space=pltpu.VMEM)] * 2,
        out_shape=[
            jax.ShapeDtypeStruct(parts[0].shape, BF),
            jax.ShapeDtypeStruct((devices, rows, width + LANES), BF),
        ],
        compiler_params=pltpu.CompilerParams(vmem_limit_bytes=16 << 20),
        name="join_shares",
    )(mixed, loss.reshape(1, 1), *parts)


def stage_kernel(after_ref, *refs):
    count = (len(refs) - 1) // 2
    sems = refs[-1]
    copies = [
        pltpu.make_async_copy(refs[k], refs[count + k], sems.at[k]) for k in range(count)
    ]
    for copy in copies:
        copy.start()
    for copy in copies:
        copy.wait()


def stage(after, arrays):
    return pl.pallas_call(
        stage_kernel,
        in_specs=[pl.BlockSpec(memory_space=pltpu.VMEM)]
        + [pl.BlockSpec(memory_space=pl.ANY)] * len(arrays),
        out_specs=[pl.BlockSpec(memory_space=pltpu.VMEM)] * len(arrays),
        out_shape=[jax.ShapeDtypeStruct(array.shape, array.dtype) for array in arrays],
        scratch_shapes=[pltpu.SemaphoreType.DMA((len(arrays),))],
        compiler_params=pltpu.CompilerParams(vmem_limit_bytes=16 << 20),
        cost_estimate=SHORT,
        name="stage",
    )(after, *arrays)


def squares(tensor):
    rows = (tensor * tensor).reshape(-1, tensor.shape[-1])
    return jnp.sum(jnp.sum(rows, axis=0, keepdims=True), axis=1, keepdims=True)


def update_kernel(place_ref, shared_ref, norm_ref, count_ref, *refs, shapes, rates, pieces):
    pieces_refs, refs = refs[:pieces], refs[pieces:]
    states, outputs = refs[:18], refs[18:38]
    mixed_ref, taps_scratch, load_sem, store_sem = refs[38:42]
    held = refs[42:]
    loads = [
        pltpu.make_async_copy(state, buffer, load_sem.at[k])
        for k, (state, buffer) in enumerate(zip(states, held))
    ]
    for k in (3, 4, 5, 6, 7, 8, 0, 1, 2) + tuple(range(9, 18)):
        loads[k].start()
    share, width = shared_ref.shape[1], mixed_ref.shape[1]
    for device in range(shared_ref.shape[0]):
        mixed_ref[device * share : (device + 1) * share] = shared_ref[device, :, :width].astype(F32)
    depth_bins, cam_width, classes, hidden_width = shapes
    if pieces > 1:
        for shift, ref in enumerate(pieces_refs):
            taps_scratch[lax.rem(place_ref[2] + (pieces - shift), pieces)] = ref[...].astype(F32)
        taps_ref = taps_scratch[...].reshape(9, held[3].shape[1], taps_scratch.shape[2])
    else:
        taps_ref = pieces_refs[0][...]
    mixed = mixed_ref[...]
    column = LANES + cam_width
    edge = taps_ref.shape[2] - cam_width
    grads = [
        jnp.concatenate([mixed[:depth_bins], mixed[LANES:column]], 0),
        jnp.concatenate([taps_ref[:, :, edge:], taps_ref[:, :, hidden_width:edge]], 2),
        taps_ref[:, :, :hidden_width],
        mixed[column : column + classes],
        norm_ref[...],
        mixed[column + classes : column + classes + 1, :classes],
    ]
    sums = jnp.sum(shared_ref[:, :1, width:].astype(F32), axis=0)
    lane = lax.broadcasted_iota(jnp.int32, sums.shape, 1)
    squared = [None if k in (1, 2) else squares(grad) for k, grad in enumerate(grads)]
    squared[1] = jnp.sum(jnp.where(lane < 3, sums, 0.0), axis=1, keepdims=True)
    squared[2] = jnp.sum(jnp.where((lane >= 3) & (lane < 6), sums, 0.0), axis=1, keepdims=True)
    loss_sum = jnp.sum(jnp.where((lane >= 6) & (lane < 9), sums, 0.0), axis=1, keepdims=True)
    loss_ref, norms_ref = outputs[:2]
    loss_ref[...] = loss_sum / count_ref[...]
    stores = [
        pltpu.make_async_copy(buffer, output, store_sem.at[k])
        for k, (buffer, output) in enumerate(zip(held, outputs[2:]))
    ]
    norms = jnp.zeros((1, LANES), F32)
    spot = lax.broadcasted_iota(jnp.int32, norms.shape, 1)
    for k in (1, 2, 0, 3, 4, 5):
        grad = grads[k]
        size = jnp.sqrt(jnp.broadcast_to(squared[k], (1, LANES)))
        norms = jnp.where(spot == k, jnp.log(size), norms)
        factor = CLIP_NORM / jnp.maximum(size, CLIP_NORM)
        factor = factor[:, :1]
        group = range(3 * k, 3 * k + 3)
        for j in group:
            loads[j].wait()
        weight, first, second = (held[j][...] for j in group)
        results = adamw(weight, grad * factor, first, second, rates[k], STEP)
        for j, result in zip(group, results):
            held[j][...] = result
            stores[j].start()
    norms_ref[...] = norms
    for store in stores:
        store.wait()


def update(place, shared, pieces, norm, positives, states, shapes, rates):
    args = [place, shared, norm, positives.reshape(1, 1)] + pieces + states
    count = len(pieces)
    width = norm.shape[1]
    return pl.pallas_call(
        functools.partial(update_kernel, shapes=shapes, rates=rates, pieces=count),
        in_specs=[pl.BlockSpec(memory_space=pltpu.SMEM)]
        + [pl.BlockSpec(memory_space=pltpu.VMEM)] * (3 + count)
        + [pl.BlockSpec(memory_space=pl.ANY)] * 18,
        out_specs=[pl.BlockSpec(memory_space=pltpu.VMEM)] * 2
        + [pl.BlockSpec(memory_space=pl.ANY)] * 18,
        out_shape=[jax.ShapeDtypeStruct((1, 1), F32), jax.ShapeDtypeStruct((1, LANES), F32)]
        + [jax.ShapeDtypeStruct(state.shape, F32) for state in states],
        scratch_shapes=[
            pltpu.VMEM((2 * LANES, width), F32),
            pltpu.VMEM((count, *pieces[0].shape[-2:]), F32),
            pltpu.SemaphoreType.DMA((18,)),
            pltpu.SemaphoreType.DMA((18,)),
        ]
        + [pltpu.VMEM(state.shape, F32) for state in states],
        compiler_params=pltpu.CompilerParams(vmem_limit_bytes=60 << 20),
        name="update",
    )(*args)


def swapped(tensor):
    strips = lax.axis_size("strip")
    return lax.ppermute(tensor, "strip", [(i, i ^ 1) for i in range(strips)])


def halves_summed(own, other):
    return own.astype(F32) + swapped(other).astype(F32)


def moved(tensor, shift):
    strips = lax.axis_size("strip")
    return lax.ppermute(tensor, "strip", [(i, (i + 2 * shift) % strips) for i in range(strips)])


def far_first(chips):
    return sorted(range(1, chips), key=lambda shift: -min(shift, chips - shift))


def along_chips(tensor):
    chips = tensor.shape[0]
    arrived = {shift: moved(tensor[shift], shift) for shift in far_first(chips)}
    return [tensor[0]] + [arrived[shift] for shift in range(1, chips)]


def total_of(parts):
    total = parts[0].astype(F32)
    for part in parts[1:]:
        total = total + part.astype(F32)
    return total


def from_chips(tensor):
    chips = lax.axis_size("strip") // 2
    arrived = {shift: moved(tensor, shift) for shift in far_first(chips)}
    return [tensor] + [arrived[shift] for shift in range(1, chips)]


def arrange_kernel(place_ref, mine_ref, theirs_ref, *outs):
    chips, taps_total, owned = mine_ref.shape[:3]
    for chip in range(chips):
        shift = lax.rem(place_ref[0] + (chips - chip), chips)
        for core in range(2):
            start = (2 * chip + core) * owned

            def copy(ref):
                first = 0
                for out_ref in outs:
                    width = out_ref.shape[2]

                    def one(tap, carry, out_ref=out_ref, first=first, width=width):
                        out_ref[tap, start : start + owned] = ref[
                            shift, tap, :, first : first + width
                        ]
                        return carry

                    lax.fori_loop(0, taps_total, one, 0)
                    first += width

            pl.when(place_ref[1] == core)(functools.partial(copy, mine_ref))
            pl.when(place_ref[1] != core)(functools.partial(copy, theirs_ref))


def arrange(place, mine, theirs, widths):
    chips, taps_total, owned = mine.shape[:3]
    return pl.pallas_call(
        arrange_kernel,
        in_specs=[pl.BlockSpec(memory_space=pltpu.SMEM)]
        + [pl.BlockSpec(memory_space=pltpu.VMEM)] * 2,
        out_specs=[pl.BlockSpec(memory_space=pltpu.VMEM)] * len(widths),
        out_shape=[
            jax.ShapeDtypeStruct((taps_total, 2 * chips * owned, width), BF) for width in widths
        ],
        compiler_params=pltpu.CompilerParams(vmem_limit_bytes=32 << 20),
        cost_estimate=SHORT,
        name="arrange",
    )(place, mine, theirs)


def moments(stats, cells, border):
    shared = lax.all_to_all(stats, ("batch", "strip"), 0, 0)
    if border:
        shared, border = lax.optimization_barrier((shared, border))
    centers = shared[:, 0]
    total = jnp.mean(centers, axis=0)
    spread_mean = jnp.mean(shared[:, 1] / cells + (centers - total) ** 2, axis=0)
    return (total, lax.rsqrt(spread_mean + EPS_NORM), jnp.sum(shared[:, 2, 0]), border)


def over_batch(tensor, shift):
    count = lax.axis_size("batch")
    if shift == 0:
        return tensor
    return lax.ppermute(tensor, "batch", [(i, (i + shift) % count) for i in range(count)])


def adamw(weight, gradient, first, second, rate, step_value):
    first = 0.9 * first + 0.1 * gradient
    second = 0.999 * second + 0.001 * gradient * gradient
    fix_one = 1.0 / (1.0 - 0.9**step_value)
    fix_two = 1.0 / (1.0 - 0.999**step_value)
    update = first * fix_one / (jnp.sqrt(second * fix_two) + 1e-08) + 0.01 * weight
    return (weight - rate * update, first, second)


def shards(
    camera_features,
    lidar_bev,
    pool_index,
    box_peaks,
    box_count,
    w_depth,
    m_depth,
    v_depth,
    w_join,
    m_join,
    v_join,
    w_res,
    m_res,
    v_res,
    w_head,
    m_head,
    v_head,
    norm_params,
    m_norm,
    v_norm,
    head_bias,
    m_bias,
    v_bias,
):
    samples, row_local, col_total, lidar_width = lidar_bev.shape
    strips = lax.axis_size("strip")
    row_total = row_local * strips
    cell_total = float(samples * lax.axis_size("batch") * row_total * col_total)
    depth_bins = pool_index.shape[2]
    classes = w_head.shape[1]
    owned = w_join.shape[3]
    cam_width = w_depth.shape[1] - depth_bins
    first_row = lax.axis_index("strip") * row_local
    place = lax.axis_index("strip")
    place = jnp.stack([place // 2, place % 2, lax.axis_index("batch")]).astype(jnp.int32)
    hidden_width = w_res.shape[2]
    taps_low = jnp.concatenate(
        [
            jnp.swapaxes(part, 2, 3).reshape(9, owned, -1)
            for part in (w_res, w_join[:, :, cam_width:], w_join[:, :, :cam_width])
        ],
        axis=2,
    ).astype(BF)
    taps_low = jnp.pad(taps_low, ((0, 0), (0, 0), (0, LANES - cam_width)))
    if owned % 16 == 0:
        taps_mine = from_chips(taps_low)
    strip_cells = row_local * col_total
    layout = plan(camera_features.shape[1], strips, strip_cells)
    own, other, dense, both_low = pool(
        place, camera_features[0], pool_index[0], w_depth.T, layout
    )
    if owned % 16 == 0:
        other, taps_mine = lax.optimization_barrier((other, taps_mine))
    pooled_halves = halves_summed(own, other).astype(BF)
    pooled = along_chips(pooled_halves)
    widths = [hidden_width, lidar_width, LANES]
    if owned % 16 == 0:
        taps_mine = jnp.stack(taps_mine)
        taps_full = arrange(place, taps_mine, swapped(taps_mine), widths)
    else:
        gathered = lax.all_gather(taps_low, "strip", axis=1, tiled=True)
        taps_full = jnp.split(gathered, [hidden_width, hidden_width + lidar_width], axis=2)
    lidar_parts = halo(lidar_bev[0])
    gaps = nearest_gaps(
        box_peaks[0], box_count, first_row, row_local, col_total, classes
    )
    pooled, gaps, taps_full, lidar_parts = lax.optimization_barrier(
        (pooled, gaps, taps_full, lidar_parts)
    )
    wide_out = jax.ShapeDtypeStruct((row_local, col_total, hidden_width), F32)
    axes = ("batch", "strip")
    devices = lax.axis_size(axes)
    stats_out = jax.ShapeDtypeStruct((devices, 3, hidden_width), F32)
    camera_parts = halo(settle(pooled, row_local, col_total))
    join_out, stats = convolve(
        [lidar_parts, camera_parts],
        taps_full[1:],
        False,
        keep_moments,
        [wide_out, stats_out],
        [gaps],
    )
    cells = float(strip_cells)
    center_one, scale_one, positives, join_border = moments(
        stats, cells, edges(join_out[:1], join_out[-1:])
    )

    def norm_one(values):
        return (values - center_one) * scale_one

    def act_of(values):
        return jax.nn.silu(norm_one(values) * norm_params[0] + norm_params[1]).astype(BF)

    act_parts = with_edges(act_of, [join_out], [join_border])
    act_one = act_parts[1]
    res_out, stats = convolve(
        [act_parts], taps_full[:1], False, keep_moments, [wide_out, stats_out]
    )
    center_two, scale_two, unused_term, unused_border = moments(stats, cells, ())

    def norm_two(values):
        return (values - center_two) * scale_two

    vectors = jnp.stack([center_two, scale_two, norm_params[2], norm_params[3]])
    grad_summed, sums, local_loss, grad_head = run_head(
        vectors,
        res_out,
        act_one,
        w_head.T.astype(BF),
        head_bias[:, None],
        gaps,
        positives.reshape(1, 1),
        devices,
    )
    shared = lax.all_to_all(sums, axes, 0, 0)
    shift_two, gain_two = jnp.sum(shared, axis=0)

    def grad_res_of(grad, values):
        spare = grad - shift_two / cell_total - norm_two(values) * gain_two / cell_total
        return (norm_params[2] * scale_two * spare).astype(BF)

    res_parts = halo(grad_res_of(grad_summed, res_out))
    sums_out = jax.ShapeDtypeStruct((devices, 2, hidden_width), F32)
    vectors = jnp.stack([center_one, scale_one, norm_params[0], norm_params[1]])
    grad_pre, sums = convolve(
        [res_parts],
        taps_full[:1],
        True,
        keep_grad,
        [wide_out, sums_out],
        [grad_summed, join_out, vectors],
    )
    shared = lax.all_to_all(sums, axes, 0, 0)
    shift_one, gain_one = jnp.sum(shared, axis=0)

    def grad_join_of(grad, values):
        spare = grad - shift_one / cell_total - norm_one(values) * gain_one / cell_total
        return (norm_params[0] * scale_one * spare).astype(BF)

    join_parts = halo(grad_join_of(grad_pre, join_out))
    cells_out = jax.ShapeDtypeStruct((layout["per_strip"], cam_width, LANES), BF)
    (grad_cells,) = convolve(
        [join_parts], taps_full[2:], True, keep_cells, [cells_out]
    )
    grad_cells, join_late, res_late = lax.optimization_barrier(
        (grad_cells, join_parts[1], res_parts[1])
    )
    grid_parts = from_chips(grad_cells)
    own_join, other_join = taps(
        place,
        [lidar_parts, camera_parts],
        [lidar_width, cam_width],
        join_late,
        strips // 2,
    )
    own_res, other_res = taps(place, [act_parts], [hidden_width], res_late, strips // 2)
    grid_parts, own_join, other_join, own_res, other_res = lax.optimization_barrier(
        (grid_parts, own_join, other_join, own_res, other_res)
    )
    grid_mine = jnp.stack(grid_parts)
    grid_theirs = swapped(grid_mine)
    grads = jnp.concatenate(
        [halves_summed(own_res, other_res), halves_summed(own_join, other_join)], axis=-1
    )
    taps_parts = along_chips(grads.astype(BF))
    grad_both = unpool(
        place,
        camera_features[0],
        pool_index[0],
        both_low,
        dense,
        grid_mine,
        grid_theirs,
        grad_head,
        layout,
    )
    grad_both, taps_parts = lax.optimization_barrier((grad_both, taps_parts))
    members = lax.axis_size("batch")
    member = lax.axis_index("batch")
    quarters = total_of(taps_parts).astype(BF).reshape(members, -1, (hidden_width + lidar_width + cam_width))
    parts = [
        over_batch(lax.dynamic_index_in_dim(quarters, (member + s) % members, 0, False), s)
        for s in range(members)
    ]
    width = w_depth.shape[0]
    mixed = grad_both.reshape(devices, -1, width)
    mixed = lax.all_to_all(mixed, axes, 0, 0)
    share, shared = join_shares(mixed, local_loss, parts, hidden_width)
    shared = lax.all_to_all(shared, axes, 0, 0)
    pieces = [over_batch(share, s) for s in range(members)]
    if share.shape[0] % 8:
        order = (member - jnp.arange(members)) % members
        pieces = [jnp.take(jnp.stack(pieces), order, axis=0).reshape(9, owned, -1).astype(F32)]
    grad_norm = jnp.stack([gain_one, shift_one, gain_two, shift_two])
    rates = [
        0.5 * w_depth.shape[0] ** (-0.5),
        0.5 * (9 * w_join.shape[2]) ** (-0.5),
        0.5 * (9 * w_res.shape[2]) ** (-0.5),
        0.5 * w_head.shape[0] ** (-0.5),
        SMALL_RATE,
        SMALL_RATE,
    ]
    weights = [w_depth, w_join, w_res, w_head, norm_params, head_bias]
    firsts = [m_depth, m_join, m_res, m_head, m_norm, m_bias]
    seconds = [v_depth, v_join, v_res, v_head, v_norm, v_bias]
    views = [
        jnp.transpose,
        lambda state: jnp.swapaxes(state, 2, 3).reshape(9, owned, -1),
        lambda state: jnp.swapaxes(state, 2, 3).reshape(9, owned, -1),
        jnp.transpose,
        lambda state: state,
        lambda state: state[None],
    ]
    backs = [
        jnp.transpose,
        lambda state: jnp.swapaxes(state.reshape(3, 3, owned, -1), 2, 3),
        lambda state: jnp.swapaxes(state.reshape(3, 3, owned, -1), 2, 3),
        jnp.transpose,
        lambda state: state,
        lambda state: state[0],
    ]
    states = [
        view(state)
        for view, group in zip(views, zip(weights, firsts, seconds))
        for state in group
    ]
    loss, norms, *states = update(
        place,
        shared,
        pieces,
        grad_norm,
        positives,
        states,
        (depth_bins, cam_width, classes, hidden_width),
        rates,
    )
    result = [loss[0], norms[0, :6]]
    for k, state in enumerate(states):
        result.append(backs[k // 3](state))
    return tuple(result)


def solution(mesh):
    in_specs = (
        P("batch", "strip", None),
        P("batch", "strip", None, None),
        P("batch", "strip", None),
        P("batch", None, None),
        P("batch"),
        P(),
        P(),
        P(),
        P(None, None, None, "strip"),
        P(None, None, None, "strip"),
        P(None, None, None, "strip"),
        P(None, None, None, "strip"),
        P(None, None, None, "strip"),
        P(None, None, None, "strip"),
        P(),
        P(),
        P(),
        P(),
        P(),
        P(),
        P(),
        P(),
        P(),
    )
    out_specs = (
        P(),
        P(),
        P(),
        P(),
        P(),
        P(None, None, None, "strip"),
        P(None, None, None, "strip"),
        P(None, None, None, "strip"),
        P(None, None, None, "strip"),
        P(None, None, None, "strip"),
        P(None, None, None, "strip"),
        P(),
        P(),
        P(),
        P(),
        P(),
        P(),
        P(),
        P(),
        P(),
    )
    return jax.shard_map(shards, mesh=mesh, in_specs=in_specs, out_specs=out_specs, check_vma=False)
```
